32 devices in a mesh: members: 2 (over y), lat: 4 (over z), lev: 2 (over x), sub: 2 (over core).
Axes of the slice: x: 2, y: 2, z: 4, core: 2. Of those that a mesh axis runs over, the one named last changes fastest.
Arguments:
- thermal_state_grid: bfloat16 [272, 512, 1024], P(('members', 'lev', 'sub'), 'lat'), parts along dimension 0, may hold values from -6 to 6
- thermal_forcing: bfloat16 [272, 512, 1024], P(('members', 'lev', 'sub'), 'lat'), parts along dimension 0, may hold values from -6 to 6
- spherical_basis_table: bfloat16 [512, 512, 512], P(('lat', 'lev', 'sub')), may hold values from -0.25 to 0.25
- implicit_solver_matrix: bfloat16 [512, 136, 136], P(('lat', 'lev', 'sub')), may hold values from -0.5 to 0.5
- fourier_order_holder: int32 [512], replicated, may hold values from 0 to 511, as said below
Outputs:
- new_temperature: bfloat16 [272, 512, 1024], P(('members', 'lev', 'sub'), 'lat'), parts along dimension 0
The draws below stay inside these ranges and needn't reach their ends.
There are 2 independent parts, one for each index of `members`. The reference program is written for one: setup_inputs(seed, part) draws one part's arguments, and reference() takes and returns one part's arrays. A program takes and returns all parts, laid end to end along the dimension named above; an argument that names none is the same for every part. Nothing has to cross between parts.
Inputs may be any that keep to these rules, and one draw needn't show every extreme that they name: fourier_order_holder is a permutation of the waves; slots 2k and 2k+1 hold waves m and 511-m for some m.
All inputs are finite; a program needn't handle non-finite values.
Results may differ from the reference program's by a relative error of at most 0.0079.
Values may be sent and summed in bfloat16 or wider, within the bound.
No kernel may reach another device: no remote copies, remote signals or barrier semaphores. Data moves between devices by JAX's collectives and lax.ppermute only.
A program may use at most 192 MiB of HBM per device.

```python
import math
import jax
import jax.numpy as jnp
from jax import lax

MERIDIAN_TOTAL = 1024
PARALLEL_TOTAL = 512
SIGMA_LAYERS = 136
M = 512


def draw_fourier_order_holder(key, part):
    half_count = M // 2
    pair_order = jax.random.permutation(key, half_count).astype(jnp.int32)
    flipped = jax.random.randint(jax.random.fold_in(key, 7), (half_count,), 0, 2).astype(jnp.int32)
    slot_ids = jnp.arange(M, dtype=jnp.int32)
    base_wave = pair_order[slot_ids // 2]
    leading = jnp.where(flipped[slot_ids // 2] == 1, M - 1 - base_wave, base_wave)
    is_second = slot_ids % 2
    return jnp.where(is_second == 1, M - 1 - leading, leading).astype(jnp.int32)


def shard_levels(rng, dims, split, smallest, largest):
    factor_of = 1.0
    for position, blocks in split:
        heights = jax.random.uniform(jax.random.fold_in(jax.random.fold_in(rng, 6), position), (blocks,), jnp.float32, smallest / len(split), largest / len(split))
        factor_of = factor_of * jnp.repeat(jnp.exp(heights), dims[position] // blocks).reshape((-1,) + (1,) * (len(dims) - 1 - position))
    return factor_of


def bell_draw(key, dims, deviation, bound, pieces=(), kind=jnp.bfloat16):
    loudness = shard_levels(key, dims, pieces, -0.22, 0.18) if pieces else 1.0
    array = jax.random.normal(key, dims, jnp.float32) * deviation * loudness
    return jnp.minimum(jnp.maximum(array, -bound), bound).astype(kind)


def setup_inputs(seed: int = 0, part: int = 0) -> dict:
    splits = jax.random.split(jax.random.key(seed), 6)
    part_splits = jax.random.split(jax.random.fold_in(splits[5], part), 6)
    thermal_state_grid = bell_draw(part_splits[0], (SIGMA_LAYERS, PARALLEL_TOTAL, MERIDIAN_TOTAL), 1.0, 6.0, ((0, 4), (1, 4)))
    thermal_forcing = bell_draw(part_splits[1], (SIGMA_LAYERS, PARALLEL_TOTAL, MERIDIAN_TOTAL), 1.0, 6.0, ((0, 4), (1, 4)))
    spherical_basis_table = bell_draw(splits[2], (M, PARALLEL_TOTAL, M), PARALLEL_TOTAL ** -0.5, 0.25, ((0, 16),))
    implicit_solver_matrix = bell_draw(splits[3], (M, SIGMA_LAYERS, SIGMA_LAYERS), SIGMA_LAYERS ** -0.5, 0.5, ((0, 16),))
    fourier_order_holder = draw_fourier_order_holder(jax.random.fold_in(splits[5], 71), part)
    return {"thermal_state_grid": thermal_state_grid, "thermal_forcing": thermal_forcing, "spherical_basis_table": spherical_basis_table, "implicit_solver_matrix": implicit_solver_matrix, "fourier_order_holder": fourier_order_holder}


block_slots = 16

def raw_table(fourier_order_holder, lon_count):
    meridian_position = jnp.arange(lon_count, dtype=jnp.int32)
    phases = meridian_position[:, None] * fourier_order_holder[None, :].astype(jnp.int32) % lon_count
    angles = phases.astype(jnp.float32) * (2.0 * math.pi / lon_count)
    factor = 1.0 / math.sqrt(lon_count)
    stacked = jnp.stack([jnp.cos(angles), -jnp.sin(angles)], axis=2)
    return stacked.reshape(lon_count, 2 * fourier_order_holder.shape[0]) * factor

def reference(thermal_state_grid, thermal_forcing, spherical_basis_table, implicit_solver_matrix, fourier_order_holder):
    present_state = thermal_state_grid.astype(jnp.float32)
    explicit = (present_state + 0.5 * thermal_forcing.astype(jnp.float32) - 0.3 * present_state * present_state * present_state / (1.0 + present_state * present_state)).astype(jnp.bfloat16)
    raw = raw_table(fourier_order_holder, MERIDIAN_TOTAL)
    analysis = raw.astype(jnp.bfloat16)
    weights = jnp.where(fourier_order_holder == 0, 1.0, 2.0).astype(jnp.float32)
    synthesis = (raw.T * jnp.repeat(weights, 2)[:, None]).astype(jnp.bfloat16)
    spectral = jnp.dot(explicit.reshape(SIGMA_LAYERS * PARALLEL_TOTAL, MERIDIAN_TOTAL), analysis, preferred_element_type=jnp.float32).astype(jnp.bfloat16)
    groups = M // block_slots
    spec_blocks = spectral.reshape(SIGMA_LAYERS, PARALLEL_TOTAL, groups, block_slots, 2).transpose(2, 0, 1, 3, 4)
    leg_blocks = spherical_basis_table.reshape(groups, block_slots, PARALLEL_TOTAL, M)

    def forward_group(operands):
        return jnp.einsum('lxsc,sxn->lscn', operands[0].astype(jnp.float32), operands[1].astype(jnp.float32)).astype(jnp.bfloat16)
    coeffs = lax.map(forward_group, (spec_blocks, leg_blocks))
    coeffs = coeffs.transpose(1, 0, 2, 3, 4).reshape(SIGMA_LAYERS, M, 2, M)
    solved = jnp.einsum('skl,lscn->kscn', implicit_solver_matrix.astype(jnp.float32), coeffs.astype(jnp.float32))
    degrees = jnp.arange(M, dtype=jnp.int32)
    live_mask = degrees[None, :] >= fourier_order_holder[:, None]
    solved = jnp.where(live_mask[None, :, None, :], solved, 0.0).astype(jnp.bfloat16)
    solved_blocks = solved.reshape(SIGMA_LAYERS, groups, block_slots, 2, M).transpose(1, 0, 2, 3, 4)

    def inverse_group(operands):
        return jnp.einsum('sxn,lscn->lxsc', operands[1].astype(jnp.float32), operands[0].astype(jnp.float32)).astype(jnp.bfloat16)
    synthesized = lax.map(inverse_group, (solved_blocks, leg_blocks))
    synthesized = synthesized.transpose(1, 2, 0, 3, 4).reshape(SIGMA_LAYERS * PARALLEL_TOTAL, 2 * M)
    result = jnp.dot(synthesized, synthesis, preferred_element_type=jnp.float32).astype(jnp.bfloat16)
    return result.reshape(SIGMA_LAYERS, PARALLEL_TOTAL, MERIDIAN_TOTAL)
```

```python
import math

import jax
import jax.numpy as jnp
from jax import lax
from jax.sharding import PartitionSpec as P

OWNERS = ("lat", "lev", "sub")


def raw_table(fourier_order_holder, lon_count):
    meridian_position = jnp.arange(lon_count, dtype=jnp.int32)
    phases = fourier_order_holder[:, None] * meridian_position[None, :] % lon_count
    angles = phases.astype(jnp.float32) * (2.0 * math.pi / lon_count)
    factor = 1.0 / math.sqrt(lon_count)
    stacked = jnp.stack([jnp.cos(angles), -jnp.sin(angles)], axis=1)
    return stacked.reshape(2 * fourier_order_holder.shape[0], lon_count) * factor


def general_shards(lat_bands, level_groups):
    def shards(
        thermal_state_grid,
        thermal_forcing,
        spherical_basis_table,
        implicit_solver_matrix,
        fourier_order_holder,
    ):
        levels, lats, lon_count = thermal_state_grid.shape
        slots, lat_total, wave_total = spherical_basis_table.shape
        owners = lat_bands * level_groups
        state = thermal_state_grid.astype(jnp.float32)
        explicit = (
            state
            + 0.5 * thermal_forcing.astype(jnp.float32)
            - 0.3 * state * state * state / (1.0 + state * state)
        ).astype(jnp.bfloat16)
        raw = raw_table(fourier_order_holder, lon_count)
        analysis = raw.astype(jnp.bfloat16)
        weights = jnp.where(fourier_order_holder == 0, 1.0, 2.0).astype(jnp.float32)
        synthesis = (raw * jnp.repeat(weights, 2)[:, None]).astype(jnp.bfloat16)
        spectral = jnp.einsum(
            "sj,lxj->slx", analysis, explicit, preferred_element_type=jnp.float32
        ).astype(jnp.bfloat16)
        spectral = spectral.reshape(owners, 2 * slots * levels, lats)
        spectral = lax.all_to_all(spectral, OWNERS, 0, 0, tiled=True)
        spectral = spectral.reshape(lat_bands, level_groups, slots, 2, levels, lats)
        spectral = spectral.transpose(2, 3, 1, 4, 0, 5)
        spectral = spectral.reshape(slots, 2 * level_groups * levels, lat_total)
        coeffs = jnp.einsum(
            "srx,sxn->srn", spectral, spherical_basis_table, preferred_element_type=jnp.float32
        ).astype(jnp.bfloat16)
        coeffs = coeffs.reshape(slots, 2, level_groups * levels, wave_total)
        solved = jnp.einsum(
            "skl,scln->sckn", implicit_solver_matrix, coeffs, preferred_element_type=jnp.float32
        )
        owner = lax.axis_index(OWNERS)
        waves = lax.dynamic_slice_in_dim(fourier_order_holder, owner * slots, slots)
        live = jnp.arange(wave_total, dtype=jnp.int32)[None, :] >= waves[:, None]
        solved = jnp.where(live[:, None, None, :], solved, 0.0).astype(jnp.bfloat16)
        solved = solved.reshape(slots, 2 * level_groups * levels, wave_total)
        back = jnp.einsum(
            "srn,sxn->srx", solved, spherical_basis_table, preferred_element_type=jnp.float32
        ).astype(jnp.bfloat16)
        back = back.reshape(slots, 2, level_groups, levels, lat_bands, lats)
        back = back.transpose(4, 2, 0, 1, 3, 5).reshape(owners, 2 * slots * levels, lats)
        back = lax.all_to_all(back, OWNERS, 0, 0, tiled=True)
        back = back.reshape(2 * slots * owners, levels, lats)
        return jnp.einsum(
            "slx,sj->lxj", back, synthesis, preferred_element_type=jnp.float32
        ).astype(jnp.bfloat16)

    return shards


def solution(mesh):
    shape = mesh.shape
    shards = general_shards(shape["lat"], shape["lev"] * shape["sub"])
    return jax.shard_map(
        shards,
        mesh=mesh,
        in_specs=(
            P(("members", "lev", "sub"), "lat", None),
            P(("members", "lev", "sub"), "lat", None),
            P(OWNERS, None, None),
            P(OWNERS, None, None),
            P(),
        ),
        out_specs=P(("members", "lev", "sub"), "lat", None),
        check_vma=False,
    )
```

```python
import functools
import math

import jax
import jax.numpy as jnp
import numpy as np
from jax import lax
from jax.experimental import pallas as pl
from jax.experimental.pallas import tpu as pltpu
from jax.sharding import PartitionSpec as P

OWNERS = ("lat", "lev", "sub")
CHUNKS = 2


def raw_table(fourier_order_holder, lon_count):
    meridian_position = jnp.arange(lon_count, dtype=jnp.int32)
    phases = fourier_order_holder[:, None] * meridian_position[None, :] % lon_count
    angles = phases.astype(jnp.float32) * (2.0 * math.pi / lon_count)
    factor = 1.0 / math.sqrt(lon_count)
    stacked = jnp.stack([jnp.cos(angles), -jnp.sin(angles)], axis=1)
    return stacked.reshape(2 * fourier_order_holder.shape[0], lon_count) * factor


def general_shards(lat_bands, level_groups):
    def shards(
        thermal_state_grid,
        thermal_forcing,
        spherical_basis_table,
        implicit_solver_matrix,
        fourier_order_holder,
    ):
        levels, lats, lon_count = thermal_state_grid.shape
        slots, lat_total, wave_total = spherical_basis_table.shape
        owners = lat_bands * level_groups
        state = thermal_state_grid.astype(jnp.float32)
        explicit = (
            state
            + 0.5 * thermal_forcing.astype(jnp.float32)
            - 0.3 * state * state * state / (1.0 + state * state)
        ).astype(jnp.bfloat16)
        raw = raw_table(fourier_order_holder, lon_count)
        analysis = raw.astype(jnp.bfloat16)
        weights = jnp.where(fourier_order_holder == 0, 1.0, 2.0).astype(jnp.float32)
        synthesis = (raw * jnp.repeat(weights, 2)[:, None]).astype(jnp.bfloat16)
        spectral = jnp.einsum(
            "sj,lxj->slx", analysis, explicit, preferred_element_type=jnp.float32
        ).astype(jnp.bfloat16)
        spectral = spectral.reshape(owners, 2 * slots * levels, lats)
        spectral = lax.all_to_all(spectral, OWNERS, 0, 0, tiled=True)
        spectral = spectral.reshape(lat_bands, level_groups, slots, 2, levels, lats)
        spectral = spectral.transpose(2, 3, 1, 4, 0, 5)
        spectral = spectral.reshape(slots, 2 * level_groups * levels, lat_total)
        coeffs = jnp.einsum(
            "srx,sxn->srn", spectral, spherical_basis_table, preferred_element_type=jnp.float32
        ).astype(jnp.bfloat16)
        coeffs = coeffs.reshape(slots, 2, level_groups * levels, wave_total)
        solved = jnp.einsum(
            "skl,scln->sckn", implicit_solver_matrix, coeffs, preferred_element_type=jnp.float32
        )
        owner = lax.axis_index(OWNERS)
        waves = lax.dynamic_slice_in_dim(fourier_order_holder, owner * slots, slots)
        live = jnp.arange(wave_total, dtype=jnp.int32)[None, :] >= waves[:, None]
        solved = jnp.where(live[:, None, None, :], solved, 0.0).astype(jnp.bfloat16)
        solved = solved.reshape(slots, 2 * level_groups * levels, wave_total)
        back = jnp.einsum(
            "srn,sxn->srx", solved, spherical_basis_table, preferred_element_type=jnp.float32
        ).astype(jnp.bfloat16)
        back = back.reshape(slots, 2, level_groups, levels, lat_bands, lats)
        back = back.transpose(4, 2, 0, 1, 3, 5).reshape(owners, 2 * slots * levels, lats)
        back = lax.all_to_all(back, OWNERS, 0, 0, tiled=True)
        back = back.reshape(2 * slots * owners, levels, lats)
        return jnp.einsum(
            "slx,sj->lxj", back, synthesis, preferred_element_type=jnp.float32
        ).astype(jnp.bfloat16)

    return shards


TILE = 8
VMEM_BYTES = 60 * 1024 * 1024
NT = (((1,), (1,)), ((), ()))
TN = (((0,), (0,)), ((), ()))


def dot(a, b, dims=(((1,), (0,)), ((), ()))):
    return lax.dot_general(a, b, dims, preferred_element_type=jnp.float32)


def longitude_waves(lon_count):
    half = lon_count // 2
    waves = np.arange(half).reshape(half // 2, 2).T
    phases = waves[:, :, None] * np.arange(half)[None, None, :] % lon_count
    angles = phases.astype(np.float32) * np.float32(2.0 * math.pi / lon_count)
    table = np.stack([np.cos(angles), -np.sin(angles)], axis=1) / math.sqrt(lon_count)
    return table.astype(jnp.bfloat16)


def analysis_kernel(
    owners, chunks, holder_ref, waves_ref, state_ref, forcing_ref, *refs
):
    sends, synth_ref, table = refs[:chunks], refs[chunks], refs[chunks + 1]
    pairs = holder_ref.shape[0]
    per_chunk = pairs // owners // chunks
    levels, lats, lon_count = state_ref.shape
    half = lon_count // 2

    @pl.when(pl.program_id(0) == 0)
    def _():
        first, second = holder_ref[:, 0:1], holder_ref[:, 1:2]
        column = lax.broadcasted_iota(jnp.int32, (pairs, waves_ref.shape[2]), 1)
        for parity in range(2):
            wave = 2 * column + parity
            pick = ((first == wave) | (second == wave)).astype(jnp.float32).astype(jnp.bfloat16)
            weight = 2.0
            if parity == 0:
                weight = jnp.where((first == 0) | (second == 0), 1.0, 2.0)
            parts, heavy = [], []
            for c in range(2):
                rows = dot(pick, waves_ref[parity, c])
                parts.append(rows.reshape(owners, chunks, per_chunk, half))
                heavy.append((rows * weight).reshape(owners, chunks, per_chunk, half))
            for k in range(chunks):
                rows = jnp.concatenate([part[:, k] for part in parts], axis=1)
                table[parity, k] = rows.reshape(2 * per_chunk * owners, half).astype(jnp.bfloat16)
                rows = jnp.concatenate([part[:, k] for part in heavy], axis=1)
                synth_ref[parity, k] = rows.reshape(2 * per_chunk * owners, half).astype(
                    jnp.bfloat16
                )

    state = state_ref[...].reshape(levels * lats, lon_count).astype(jnp.float32)
    forcing = forcing_ref[...].reshape(levels * lats, lon_count).astype(jnp.float32)
    explicit = 0.7 * state + 0.5 * forcing + 0.3 * state / (1.0 + state * state)
    low, high = explicit[:, :half], explicit[:, half:]
    for parity in range(2):
        folded = (low + high if parity == 0 else low - high).astype(jnp.bfloat16)
        for k in range(chunks):
            found = dot(table[parity, k], folded, NT).astype(jnp.bfloat16)
            found = found.reshape(owners, 2 * per_chunk, levels * lats)
            rows = slice(parity * 2 * per_chunk, (parity + 1) * 2 * per_chunk)
            for level in range(levels):
                sends[k][:, level, rows, :] = found[:, :, level * lats : (level + 1) * lats]


def run_analysis(owners, chunks, state, forcing, holder):
    levels, lats, lon_count = state.shape
    pairs = holder.shape[0] // 2
    rows = 4 * pairs // owners // chunks
    table = jnp.asarray(longitude_waves(lon_count))
    step = 2 if levels % 2 == 0 else 1
    block = pl.BlockSpec((step, lats, lon_count), lambda i: (i, 0, 0))
    whole = lambda shape: pl.BlockSpec(shape, lambda i: (0,) * len(shape))
    synth = (2, chunks, 2 * pairs // chunks, lon_count // 2)
    outs = pl.pallas_call(
        functools.partial(analysis_kernel, owners, chunks),
        grid=(levels // step,),
        in_specs=[whole((pairs, 2)), whole(table.shape), block, block],
        out_specs=[pl.BlockSpec((owners, step, rows, lats), lambda i: (0, i, 0, 0))] * chunks
        + [whole(synth)],
        out_shape=[jax.ShapeDtypeStruct((owners, levels, rows, lats), jnp.bfloat16)] * chunks
        + [jax.ShapeDtypeStruct(synth, jnp.bfloat16)],
        scratch_shapes=[pltpu.VMEM(synth, jnp.bfloat16)],
        compiler_params=pltpu.CompilerParams(vmem_limit_bytes=VMEM_BYTES),
        cost_estimate=pl.CostEstimate(
            flops=2 * levels * lats * lon_count * pairs * 2,
            bytes_accessed=6 * levels * lats * lon_count,
            transcendentals=0,
        ),
        name="longitude_analysis",
    )(holder.reshape(pairs, 2), table, state, forcing)
    return outs[:chunks], outs[chunks]


def slot_of(k, per_chunk, i, waves):
    first = 2 * (k * per_chunk + lax.rem(i, per_chunk))
    odd = lax.rem(waves[first], 2)
    return first + lax.rem(odd + i // per_chunk, 2)


def column_kernel(
    k, per_chunk, waves_ref, recv_ref, basis_ref, solver_ref, send_ref, spread, back
):
    owners, levels, rows, lats = recv_ref.shape
    bands = spread.shape[0]
    groups = owners // bands
    depth = groups * levels
    total = basis_ref.shape[1]
    i = pl.program_id(0)

    @pl.when(i == 0)
    def _():
        for a in range(bands):
            for g in range(groups):
                part = recv_ref[a * groups + g].astype(jnp.float32)
                spread[a, g * levels * rows : (g + 1) * levels * rows, :] = part.reshape(
                    levels * rows, lats
                )

    wave = waves_ref[slot_of(k, per_chunk, i, waves_ref)]
    base = (i // per_chunk) * (2 * per_chunk) + lax.rem(i, per_chunk)
    starts = [base, base + per_chunk]

    def column(low):
        count = total - low
        taken = [
            jnp.concatenate(
                [spread[a, pl.ds(start, depth, stride=rows), :] for a in range(bands)], axis=1
            )
            for start in starts
        ]
        taken = jnp.concatenate(taken, axis=0).astype(jnp.bfloat16)
        basis = basis_ref[0, :, low:]
        coeffs = dot(taken, basis)
        coeffs = jnp.concatenate([coeffs[:depth], coeffs[depth:]], axis=1).astype(jnp.bfloat16)
        solved = dot(solver_ref[0], coeffs)
        degree = low + lax.broadcasted_iota(jnp.int32, (depth, count), 1)
        parts = [
            jnp.where(degree >= wave, solved[:, c * count : (c + 1) * count], 0.0)
            for c in range(2)
        ]
        solved = jnp.concatenate(parts, axis=0).astype(jnp.bfloat16)
        grid = dot(solved, basis, NT)
        for c in range(2):
            for a in range(bands):
                back[a, pl.ds(starts[c], depth, stride=rows), :] = grid[
                    c * depth : (c + 1) * depth, a * lats : (a + 1) * lats
                ]

    middle = total // 2

    @pl.when(wave < middle)
    def _():
        column(0)

    @pl.when(wave >= middle)
    def _():
        column(middle)

    @pl.when(i == pl.num_programs(0) - 1)
    def _():
        for a in range(bands):
            for g in range(groups):
                part = back[a, g * levels * rows : (g + 1) * levels * rows, :]
                send_ref[a * groups + g] = part.reshape(levels, rows, lats).astype(jnp.bfloat16)


def run_columns(k, per_chunk, bands, waves, received, basis, solver):
    owners, levels, rows, lats = received.shape
    depth = owners // bands * levels
    total = basis.shape[1]
    steps = 2 * per_chunk
    slot = lambda i, waves_ref: (slot_of(k, per_chunk, i, waves_ref), 0, 0)
    whole = pl.BlockSpec(received.shape, lambda i, waves_ref: (0, 0, 0, 0))
    scratch = pltpu.VMEM((bands, depth * rows, lats), jnp.float32)
    return pl.pallas_call(
        functools.partial(column_kernel, k, per_chunk),
        grid_spec=pltpu.PrefetchScalarGridSpec(
            num_scalar_prefetch=1,
            grid=(steps,),
            in_specs=[
                whole,
                pl.BlockSpec((1, total, total), slot),
                pl.BlockSpec((1, depth, depth), slot),
            ],
            out_specs=whole,
            scratch_shapes=[scratch, scratch],
        ),
        out_shape=jax.ShapeDtypeStruct(received.shape, jnp.bfloat16),
        compiler_params=pltpu.CompilerParams(vmem_limit_bytes=VMEM_BYTES),
        cost_estimate=pl.CostEstimate(
            flops=4 * steps * 2 * depth * total * total,
            bytes_accessed=4 * received.size + 2 * steps * total * total,
            transcendentals=0,
        ),
        name="legendre_solve",
    )(waves, received, basis, solver)


def synthesis_kernel(chunks, *refs):
    parts, synth_ref, out_ref = refs[:chunks], refs[chunks], refs[chunks + 1]
    owners, levels, rows, lats = parts[0].shape
    half = synth_ref.shape[-1]
    for level in range(levels):
        sums = []
        for parity in range(2):
            total = None
            for k in range(chunks):
                found = parts[k][:, level, parity * (rows // 2) : (parity + 1) * (rows // 2), :]
                term = dot(found.reshape(owners * rows // 2, lats), synth_ref[parity, k], TN)
                total = term if total is None else total + term
            sums.append(total)
        out_ref[level, :, :half] = (sums[0] + sums[1]).astype(jnp.bfloat16)
        out_ref[level, :, half:] = (sums[0] - sums[1]).astype(jnp.bfloat16)


def run_synthesis(parts, synth):
    owners, levels, rows, lats = parts[0].shape
    lon_count = 2 * synth.shape[-1]
    chunks = len(parts)
    step = 2 if levels % 2 == 0 else 1
    return pl.pallas_call(
        functools.partial(synthesis_kernel, chunks),
        grid=(levels // step,),
        in_specs=[pl.BlockSpec((owners, step, rows, lats), lambda i: (0, i, 0, 0))] * chunks
        + [pl.BlockSpec(synth.shape, lambda i: (0, 0, 0, 0))],
        out_specs=pl.BlockSpec((step, lats, lon_count), lambda i: (i, 0, 0)),
        out_shape=jax.ShapeDtypeStruct((levels, lats, lon_count), jnp.bfloat16),
        compiler_params=pltpu.CompilerParams(vmem_limit_bytes=VMEM_BYTES),
        cost_estimate=pl.CostEstimate(
            flops=levels * lats * lon_count * lon_count,
            bytes_accessed=4 * levels * lats * lon_count,
            transcendentals=0,
        ),
        name="longitude_synthesis",
    )(*parts, synth)


def exchange(part):
    owners, levels, rows, lats = part.shape
    flat = part.reshape(owners, levels * rows, lats)
    return lax.all_to_all(flat, OWNERS, 0, 0, tiled=True).reshape(part.shape)


def chunked_shards(lat_bands, level_groups, chunks):
    owners = lat_bands * level_groups

    def shards(
        thermal_state_grid,
        thermal_forcing,
        spherical_basis_table,
        implicit_solver_matrix,
        fourier_order_holder,
    ):
        slots = spherical_basis_table.shape[0]
        per_chunk = slots // 2 // chunks
        sends, synth = run_analysis(
            owners, chunks, thermal_state_grid, thermal_forcing, fourier_order_holder
        )
        owner = lax.axis_index(OWNERS)
        waves = lax.dynamic_slice_in_dim(fourier_order_holder, owner * slots, slots)
        received = [exchange(part) for part in sends]
        solved = [
            run_columns(
                k,
                per_chunk,
                lat_bands,
                waves,
                received[k],
                spherical_basis_table,
                implicit_solver_matrix,
            )
            for k in range(chunks)
        ]
        returned = [exchange(part) for part in solved]
        return run_synthesis(returned, synth)

    return shards


def solution(mesh):
    shape = mesh.shape
    bands, groups = shape["lat"], shape["lev"] * shape["sub"]

    def shards(state, forcing, basis, solver, holder):
        levels, lats, lon_count = state.shape
        pairs = basis.shape[0] // 2
        tiled = pairs % (CHUNKS * TILE) == 0 and levels * groups % TILE == 0
        if tiled and lats % 128 == 0 and lon_count == 2 * holder.shape[0]:
            body = chunked_shards(bands, groups, CHUNKS)
        else:
            body = general_shards(bands, groups)
        return body(state, forcing, basis, solver, holder)

    return jax.shard_map(
        shards,
        mesh=mesh,
        in_specs=(
            P(("members", "lev", "sub"), "lat", None),
            P(("members", "lev", "sub"), "lat", None),
            P(OWNERS, None, None),
            P(OWNERS, None, None),
            P(),
        ),
        out_specs=P(("members", "lev", "sub"), "lat", None),
        check_vma=False,
    )
```

```python
import functools
import math

import jax
import jax.numpy as jnp
import numpy as np
from jax import lax
from jax.experimental import pallas as pl
from jax.experimental.pallas import tpu as pltpu
from jax.sharding import PartitionSpec as P

OWNERS = ("lat", "lev", "sub")
CHUNKS = 2


def raw_table(fourier_order_holder, lon_count):
    meridian_position = jnp.arange(lon_count, dtype=jnp.int32)
    phases = fourier_order_holder[:, None] * meridian_position[None, :] % lon_count
    angles = phases.astype(jnp.float32) * (2.0 * math.pi / lon_count)
    factor = 1.0 / math.sqrt(lon_count)
    stacked = jnp.stack([jnp.cos(angles), -jnp.sin(angles)], axis=1)
    return stacked.reshape(2 * fourier_order_holder.shape[0], lon_count) * factor


def general_shards(lat_bands, level_groups):
    def shards(
        thermal_state_grid,
        thermal_forcing,
        spherical_basis_table,
        implicit_solver_matrix,
        fourier_order_holder,
    ):
        levels, lats, lon_count = thermal_state_grid.shape
        slots, lat_total, wave_total = spherical_basis_table.shape
        owners = lat_bands * level_groups
        state = thermal_state_grid.astype(jnp.float32)
        explicit = (
            state
            + 0.5 * thermal_forcing.astype(jnp.float32)
            - 0.3 * state * state * state / (1.0 + state * state)
        ).astype(jnp.bfloat16)
        raw = raw_table(fourier_order_holder, lon_count)
        analysis = raw.astype(jnp.bfloat16)
        weights = jnp.where(fourier_order_holder == 0, 1.0, 2.0).astype(jnp.float32)
        synthesis = (raw * jnp.repeat(weights, 2)[:, None]).astype(jnp.bfloat16)
        spectral = jnp.einsum(
            "sj,lxj->slx", analysis, explicit, preferred_element_type=jnp.float32
        ).astype(jnp.bfloat16)
        spectral = spectral.reshape(owners, 2 * slots * levels, lats)
        spectral = lax.all_to_all(spectral, OWNERS, 0, 0, tiled=True)
        spectral = spectral.reshape(lat_bands, level_groups, slots, 2, levels, lats)
        spectral = spectral.transpose(2, 3, 1, 4, 0, 5)
        spectral = spectral.reshape(slots, 2 * level_groups * levels, lat_total)
        coeffs = jnp.einsum(
            "srx,sxn->srn", spectral, spherical_basis_table, preferred_element_type=jnp.float32
        ).astype(jnp.bfloat16)
        coeffs = coeffs.reshape(slots, 2, level_groups * levels, wave_total)
        solved = jnp.einsum(
            "skl,scln->sckn", implicit_solver_matrix, coeffs, preferred_element_type=jnp.float32
        )
        owner = lax.axis_index(OWNERS)
        waves = lax.dynamic_slice_in_dim(fourier_order_holder, owner * slots, slots)
        live = jnp.arange(wave_total, dtype=jnp.int32)[None, :] >= waves[:, None]
        solved = jnp.where(live[:, None, None, :], solved, 0.0).astype(jnp.bfloat16)
        solved = solved.reshape(slots, 2 * level_groups * levels, wave_total)
        back = jnp.einsum(
            "srn,sxn->srx", solved, spherical_basis_table, preferred_element_type=jnp.float32
        ).astype(jnp.bfloat16)
        back = back.reshape(slots, 2, level_groups, levels, lat_bands, lats)
        back = back.transpose(4, 2, 0, 1, 3, 5).reshape(owners, 2 * slots * levels, lats)
        back = lax.all_to_all(back, OWNERS, 0, 0, tiled=True)
        back = back.reshape(2 * slots * owners, levels, lats)
        return jnp.einsum(
            "slx,sj->lxj", back, synthesis, preferred_element_type=jnp.float32
        ).astype(jnp.bfloat16)

    return shards


TILE = 8
VMEM_BYTES = 60 * 1024 * 1024
NT = (((1,), (1,)), ((), ()))
TN = (((0,), (0,)), ((), ()))


def dot(a, b, dims=(((1,), (0,)), ((), ()))):
    return lax.dot_general(a, b, dims, preferred_element_type=jnp.float32)


def longitude_waves(lon_count):
    half = lon_count // 2
    waves = np.arange(half).reshape(half // 2, 2).T
    phases = waves[:, :, None] * np.arange(half)[None, None, :] % lon_count
    angles = phases.astype(np.float32) * np.float32(2.0 * math.pi / lon_count)
    table = np.stack([np.cos(angles), -np.sin(angles)], axis=1) / math.sqrt(lon_count)
    return table.astype(jnp.bfloat16)


def wave_rows(owners, chunks, k, holder_ref, waves_ref, parity):
    slots = holder_ref.shape[1]
    per_chunk = slots // 2 // owners // chunks
    wave = 2 * lax.broadcasted_iota(jnp.int32, (waves_ref.shape[2], slots), 0) + parity
    held = (holder_ref[...] == wave).astype(jnp.float32).astype(jnp.bfloat16)
    row = lax.broadcasted_iota(jnp.int32, (owners * per_chunk, slots), 0)
    pair = (lax.div(row, per_chunk) * chunks + k) * per_chunk + lax.rem(row, per_chunk)
    slot = lax.broadcasted_iota(jnp.int32, (owners * per_chunk, slots), 1)
    chosen = (lax.div(slot, 2) == pair).astype(jnp.float32).astype(jnp.bfloat16)
    pick = dot(chosen, held, NT)
    picked = pick.astype(jnp.bfloat16)
    parts = [
        dot(picked, waves_ref[parity, c]).reshape(owners, per_chunk, waves_ref.shape[3])
        for c in range(2)
    ]
    rows = jnp.concatenate(parts, axis=1).reshape(2 * per_chunk * owners, waves_ref.shape[3])
    return rows, pick[:, 0:1]


def analysis_kernel(
    owners, chunks, k, holder_ref, waves_ref, state_hbm, forcing_hbm, send_ref,
    table, state, forcing, folded, arrived,
):
    steps, levels, lats, lon_count = state.shape
    half = lon_count // 2
    i = pl.program_id(0)

    def copies(n):
        rows = pl.ds(n * levels, levels)
        return (
            pltpu.make_async_copy(state_hbm.at[rows], state.at[n], arrived.at[n, 0]),
            pltpu.make_async_copy(forcing_hbm.at[rows], forcing.at[n], arrived.at[n, 1]),
        )

    @pl.when(i == 0)
    def _():
        @pl.loop(0, steps)
        def _(n):
            for copy in copies(n):
                copy.start()

        for parity in range(2):
            rows, _ = wave_rows(owners, chunks, k, holder_ref, waves_ref, parity)
            table[parity] = rows.astype(jnp.bfloat16)

    @pl.when(i < steps)
    def _():
        for copy in copies(i):
            copy.wait()

    def step(now, last):
        n = jnp.minimum(i, steps - 1)
        for level in range(levels):
            s = state[n, level].astype(jnp.float32)
            f = forcing[n, level].astype(jnp.float32)
            explicit = 0.7 * s + 0.5 * f + 0.3 * s / (1.0 + s * s)
            low, high = explicit[:, :half], explicit[:, half:]
            rows = slice(level * lats, (level + 1) * lats)
            folded[now, 0, rows, :] = (low + high).astype(jnp.bfloat16)
            folded[now, 1, rows, :] = (low - high).astype(jnp.bfloat16)
        for parity in range(2):
            found = dot(table[parity], folded[last, parity], NT).astype(jnp.bfloat16)
            count = found.shape[0] // owners
            found = found.reshape(owners, count, levels * lats)
            rows = slice(parity * count, (parity + 1) * count)
            for level in range(levels):
                send_ref[:, level, rows, :] = found[:, :, level * lats : (level + 1) * lats]

    @pl.when(lax.rem(i, 2) == 0)
    def _():
        step(0, 1)

    @pl.when(lax.rem(i, 2) == 1)
    def _():
        step(1, 0)


def run_analysis(owners, chunks, k, state, forcing, holder, table):
    levels, lats, lon_count = state.shape
    slots = holder.shape[1]
    rows = 2 * slots // owners // chunks
    count = 2 if levels % 2 == 0 else 1
    steps = levels // count
    whole = lambda shape: pl.BlockSpec(shape, lambda i: (0,) * len(shape))
    kept = pltpu.VMEM((steps, count, lats, lon_count), jnp.bfloat16)
    return pl.pallas_call(
        functools.partial(analysis_kernel, owners, chunks, k),
        grid=(steps + 1,),
        in_specs=[whole(holder.shape), whole(table.shape)] + [pl.BlockSpec(memory_space=pl.ANY)] * 2,
        out_specs=pl.BlockSpec(
            (owners, count, rows, lats), lambda i: (0, jnp.maximum(i - 1, 0), 0, 0)
        ),
        out_shape=jax.ShapeDtypeStruct((owners, levels, rows, lats), jnp.bfloat16),
        scratch_shapes=[
            pltpu.VMEM((2, slots // chunks, lon_count // 2), jnp.bfloat16),
            kept,
            kept,
            pltpu.VMEM((2, 2, count * lats, lon_count // 2), jnp.bfloat16),
            pltpu.SemaphoreType.DMA((steps, 2)),
        ],
        compiler_params=pltpu.CompilerParams(vmem_limit_bytes=VMEM_BYTES),
        cost_estimate=pl.CostEstimate(
            flops=2 * levels * lats * lon_count * slots // chunks,
            bytes_accessed=6 * levels * lats * lon_count,
            transcendentals=0,
        ),
        name="longitude_analysis",
    )(holder, table, state, forcing)


def synthesis_rows_kernel(owners, chunks, holder_ref, waves_ref, out_ref):
    for parity in range(2):
        for k in range(chunks):
            rows, zero = wave_rows(owners, chunks, k, holder_ref, waves_ref, parity)
            if parity == 0:
                count = zero.shape[0] // owners
                weight = (2.0 - zero).reshape(owners, count, 1)
                weight = jnp.concatenate([weight, weight], axis=1).reshape(-1, 1)
            else:
                weight = 2.0
            out_ref[parity, k] = (rows * weight).astype(jnp.bfloat16)


def synthesis_rows(owners, chunks, holder, table):
    shape = (2, chunks, holder.shape[1] // chunks, table.shape[3])
    return pl.pallas_call(
        functools.partial(synthesis_rows_kernel, owners, chunks),
        out_shape=jax.ShapeDtypeStruct(shape, jnp.bfloat16),
        compiler_params=pltpu.CompilerParams(vmem_limit_bytes=VMEM_BYTES),
        cost_estimate=pl.CostEstimate(
            flops=8 * holder.shape[1] * table.shape[2] * table.shape[3],
            bytes_accessed=4 * holder.shape[1] * table.shape[3],
            transcendentals=0,
        ),
        name="synthesis_rows",
    )(holder, table)


def slot_of(k, per_chunk, i, waves):
    first = 2 * (k * per_chunk + lax.rem(i, per_chunk))
    odd = lax.rem(waves[first], 2)
    return first + lax.rem(odd + i // per_chunk, 2)


def column_kernel(
    k, per_chunk, waves_ref, recv_ref, basis_ref, solver_ref, send_ref, spread, back
):
    owners, levels, rows, lats = recv_ref.shape
    bands = spread.shape[0]
    groups = owners // bands
    depth = groups * levels
    total = basis_ref.shape[1]
    i = pl.program_id(0)

    @pl.when(i == 0)
    def _():
        for a in range(bands):
            for g in range(groups):
                part = recv_ref[a * groups + g].astype(jnp.float32)
                spread[a, g * levels * rows : (g + 1) * levels * rows, :] = part.reshape(
                    levels * rows, lats
                )

    wave = waves_ref[slot_of(k, per_chunk, i, waves_ref)]
    base = (i // per_chunk) * (2 * per_chunk) + lax.rem(i, per_chunk)
    starts = [base, base + per_chunk]

    def column(low):
        count = total - low
        taken = [
            jnp.concatenate(
                [spread[a, pl.ds(start, depth, stride=rows), :] for a in range(bands)], axis=1
            )
            for start in starts
        ]
        taken = jnp.concatenate(taken, axis=0).astype(jnp.bfloat16)
        basis = basis_ref[0, :, low:]
        coeffs = dot(taken, basis)
        coeffs = jnp.concatenate([coeffs[:depth], coeffs[depth:]], axis=1).astype(jnp.bfloat16)
        solved = dot(solver_ref[0], coeffs)
        degree = low + lax.broadcasted_iota(jnp.int32, (depth, count), 1)
        parts = [
            jnp.where(degree >= wave, solved[:, c * count : (c + 1) * count], 0.0)
            for c in range(2)
        ]
        solved = jnp.concatenate(parts, axis=0).astype(jnp.bfloat16)
        grid = dot(solved, basis, NT)
        for c in range(2):
            for a in range(bands):
                back[a, pl.ds(starts[c], depth, stride=rows), :] = grid[
                    c * depth : (c + 1) * depth, a * lats : (a + 1) * lats
                ]

    middle = total // 2

    @pl.when(wave < middle)
    def _():
        column(0)

    @pl.when(wave >= middle)
    def _():
        column(middle)

    @pl.when(i == pl.num_programs(0) - 1)
    def _():
        for a in range(bands):
            for g in range(groups):
                part = back[a, g * levels * rows : (g + 1) * levels * rows, :]
                send_ref[a * groups + g] = part.reshape(levels, rows, lats).astype(jnp.bfloat16)


def run_columns(k, per_chunk, bands, waves, received, basis, solver):
    owners, levels, rows, lats = received.shape
    depth = owners // bands * levels
    total = basis.shape[1]
    steps = 2 * per_chunk
    slot = lambda i, waves_ref: (slot_of(k, per_chunk, i, waves_ref), 0, 0)
    whole = pl.BlockSpec(received.shape, lambda i, waves_ref: (0, 0, 0, 0))
    scratch = pltpu.VMEM((bands, depth * rows, lats), jnp.float32)
    return pl.pallas_call(
        functools.partial(column_kernel, k, per_chunk),
        grid_spec=pltpu.PrefetchScalarGridSpec(
            num_scalar_prefetch=1,
            grid=(steps,),
            in_specs=[
                whole,
                pl.BlockSpec((1, total, total), slot),
                pl.BlockSpec((1, depth, depth), slot),
            ],
            out_specs=whole,
            scratch_shapes=[scratch, scratch],
        ),
        out_shape=jax.ShapeDtypeStruct(received.shape, jnp.bfloat16),
        compiler_params=pltpu.CompilerParams(vmem_limit_bytes=VMEM_BYTES),
        cost_estimate=pl.CostEstimate(
            flops=4 * steps * 2 * depth * total * total,
            bytes_accessed=4 * received.size + 2 * steps * total * total,
            transcendentals=0,
        ),
        name="legendre_solve",
    )(waves, received, basis, solver)


def synthesis_kernel(chunks, *refs):
    parts, (synth_ref, out_ref, kept, arrived) = refs[:chunks], refs[chunks:]
    steps, _, owners, levels, rows, lats = kept.shape
    half = synth_ref.shape[-1]
    i = pl.program_id(0)

    def copies(n):
        span = pl.ds(n * levels, levels)
        return [
            pltpu.make_async_copy(part.at[:, span], kept.at[n, k], arrived.at[n, k])
            for k, part in enumerate(parts)
        ]

    @pl.when(i == 0)
    def _():
        @pl.loop(0, steps)
        def _(n):
            for copy in copies(n):
                copy.start()

    for copy in copies(i):
        copy.wait()
    sums = []
    for parity in range(2):
        terms = []
        for k in range(chunks):
            found = kept[i, k, :, :, parity * (rows // 2) : (parity + 1) * (rows // 2), :]
            found = jnp.concatenate(
                [found[:, n].reshape(owners * rows // 2, lats) for n in range(levels)], axis=1
            )
            terms.append(dot(found, synth_ref[parity, k], TN))
        sums.append(sum(terms[1:], terms[0]))
    for n in range(levels):
        even, odd = [found[n * lats : (n + 1) * lats] for found in sums]
        out_ref[n, :, :half] = (even + odd).astype(jnp.bfloat16)
        out_ref[n, :, half:] = (even - odd).astype(jnp.bfloat16)


def run_synthesis(parts, synth):
    owners, levels, rows, lats = parts[0].shape
    lon_count = 2 * synth.shape[-1]
    chunks = len(parts)
    count = 2 if levels % 2 == 0 else 1
    steps = levels // count
    return pl.pallas_call(
        functools.partial(synthesis_kernel, chunks),
        grid=(steps,),
        in_specs=[pl.BlockSpec(memory_space=pl.ANY)] * chunks
        + [pl.BlockSpec(synth.shape, lambda i: (0, 0, 0, 0))],
        out_specs=pl.BlockSpec((count, lats, lon_count), lambda i: (i, 0, 0)),
        out_shape=jax.ShapeDtypeStruct((levels, lats, lon_count), jnp.bfloat16),
        scratch_shapes=[
            pltpu.VMEM((steps, chunks, owners, count, rows, lats), jnp.bfloat16),
            pltpu.SemaphoreType.DMA((steps, chunks)),
        ],
        compiler_params=pltpu.CompilerParams(vmem_limit_bytes=VMEM_BYTES),
        cost_estimate=pl.CostEstimate(
            flops=levels * lats * lon_count * lon_count,
            bytes_accessed=4 * levels * lats * lon_count,
            transcendentals=0,
        ),
        name="longitude_synthesis",
    )(*parts, synth)


def exchange(part):
    owners, levels, rows, lats = part.shape
    flat = part.reshape(owners, levels * rows, lats)
    return lax.all_to_all(flat, OWNERS, 0, 0, tiled=True).reshape(part.shape)


def chunked_shards(lat_bands, level_groups, chunks):
    owners = lat_bands * level_groups

    def shards(
        thermal_state_grid,
        thermal_forcing,
        spherical_basis_table,
        implicit_solver_matrix,
        fourier_order_holder,
    ):
        slots = spherical_basis_table.shape[0]
        per_chunk = slots // 2 // chunks
        table = jnp.asarray(longitude_waves(thermal_state_grid.shape[2]))
        holder = fourier_order_holder.reshape(1, -1)
        sends = [
            run_analysis(owners, chunks, k, thermal_state_grid, thermal_forcing, holder, table)
            for k in range(chunks)
        ]
        synth = synthesis_rows(owners, chunks, holder, table)
        owner = lax.axis_index(OWNERS)
        waves = lax.dynamic_slice_in_dim(fourier_order_holder, owner * slots, slots)
        received = [exchange(part) for part in sends]
        solved = [
            run_columns(
                k,
                per_chunk,
                lat_bands,
                waves,
                received[k],
                spherical_basis_table,
                implicit_solver_matrix,
            )
            for k in range(chunks)
        ]
        returned = [exchange(part) for part in solved]
        return run_synthesis(returned, synth)

    return shards


def solution(mesh):
    shape = mesh.shape
    bands, groups = shape["lat"], shape["lev"] * shape["sub"]

    def shards(state, forcing, basis, solver, holder):
        levels, lats, lon_count = state.shape
        pairs = basis.shape[0] // 2
        tiled = pairs % (CHUNKS * TILE) == 0 and levels * groups % TILE == 0
        if tiled and lats % 128 == 0 and lon_count == 2 * holder.shape[0]:
            body = chunked_shards(bands, groups, CHUNKS)
        else:
            body = general_shards(bands, groups)
        return body(state, forcing, basis, solver, holder)

    return jax.shard_map(
        shards,
        mesh=mesh,
        in_specs=(
            P(("members", "lev", "sub"), "lat", None),
            P(("members", "lev", "sub"), "lat", None),
            P(OWNERS, None, None),
            P(OWNERS, None, None),
            P(),
        ),
        out_specs=P(("members", "lev", "sub"), "lat", None),
        check_vma=False,
    )
```

```python
import functools
import math

import jax
import jax.numpy as jnp
import numpy as np
from jax import lax
from jax.experimental import pallas as pl
from jax.experimental.pallas import tpu as pltpu
from jax.sharding import PartitionSpec as P

OWNERS = ("lat", "lev", "sub")
CHUNKS = 2


def raw_table(fourier_order_holder, lon_count):
    meridian_position = jnp.arange(lon_count, dtype=jnp.int32)
    phases = fourier_order_holder[:, None] * meridian_position[None, :] % lon_count
    angles = phases.astype(jnp.float32) * (2.0 * math.pi / lon_count)
    factor = 1.0 / math.sqrt(lon_count)
    stacked = jnp.stack([jnp.cos(angles), -jnp.sin(angles)], axis=1)
    return stacked.reshape(2 * fourier_order_holder.shape[0], lon_count) * factor


def general_shards(lat_bands, level_groups):
    def shards(
        thermal_state_grid,
        thermal_forcing,
        spherical_basis_table,
        implicit_solver_matrix,
        fourier_order_holder,
    ):
        levels, lats, lon_count = thermal_state_grid.shape
        slots, lat_total, wave_total = spherical_basis_table.shape
        owners = lat_bands * level_groups
        state = thermal_state_grid.astype(jnp.float32)
        explicit = (
            state
            + 0.5 * thermal_forcing.astype(jnp.float32)
            - 0.3 * state * state * state / (1.0 + state * state)
        ).astype(jnp.bfloat16)
        raw = raw_table(fourier_order_holder, lon_count)
        analysis = raw.astype(jnp.bfloat16)
        weights = jnp.where(fourier_order_holder == 0, 1.0, 2.0).astype(jnp.float32)
        synthesis = (raw * jnp.repeat(weights, 2)[:, None]).astype(jnp.bfloat16)
        spectral = jnp.einsum(
            "sj,lxj->slx", analysis, explicit, preferred_element_type=jnp.float32
        ).astype(jnp.bfloat16)
        spectral = spectral.reshape(owners, 2 * slots * levels, lats)
        spectral = lax.all_to_all(spectral, OWNERS, 0, 0, tiled=True)
        spectral = spectral.reshape(lat_bands, level_groups, slots, 2, levels, lats)
        spectral = spectral.transpose(2, 3, 1, 4, 0, 5)
        spectral = spectral.reshape(slots, 2 * level_groups * levels, lat_total)
        coeffs = jnp.einsum(
            "srx,sxn->srn", spectral, spherical_basis_table, preferred_element_type=jnp.float32
        ).astype(jnp.bfloat16)
        coeffs = coeffs.reshape(slots, 2, level_groups * levels, wave_total)
        solved = jnp.einsum(
            "skl,scln->sckn", implicit_solver_matrix, coeffs, preferred_element_type=jnp.float32
        )
        owner = lax.axis_index(OWNERS)
        waves = lax.dynamic_slice_in_dim(fourier_order_holder, owner * slots, slots)
        live = jnp.arange(wave_total, dtype=jnp.int32)[None, :] >= waves[:, None]
        solved = jnp.where(live[:, None, None, :], solved, 0.0).astype(jnp.bfloat16)
        solved = solved.reshape(slots, 2 * level_groups * levels, wave_total)
        back = jnp.einsum(
            "srn,sxn->srx", solved, spherical_basis_table, preferred_element_type=jnp.float32
        ).astype(jnp.bfloat16)
        back = back.reshape(slots, 2, level_groups, levels, lat_bands, lats)
        back = back.transpose(4, 2, 0, 1, 3, 5).reshape(owners, 2 * slots * levels, lats)
        back = lax.all_to_all(back, OWNERS, 0, 0, tiled=True)
        back = back.reshape(2 * slots * owners, levels, lats)
        return jnp.einsum(
            "slx,sj->lxj", back, synthesis, preferred_element_type=jnp.float32
        ).astype(jnp.bfloat16)

    return shards


TILE = 8
VMEM_BYTES = 60 * 1024 * 1024
NT = (((1,), (1,)), ((), ()))
TN = (((0,), (0,)), ((), ()))


def dot(a, b, dims=(((1,), (0,)), ((), ()))):
    return lax.dot_general(a, b, dims, preferred_element_type=jnp.float32)


def longitude_waves(lon_count):
    half = lon_count // 2
    waves = np.arange(half).reshape(half // 2, 2).T
    phases = waves[:, :, None] * np.arange(half)[None, None, :] % lon_count
    angles = phases.astype(np.float32) * np.float32(2.0 * math.pi / lon_count)
    table = np.stack([np.cos(angles), -np.sin(angles)], axis=1) / math.sqrt(lon_count)
    return table.astype(jnp.bfloat16)


def wave_rows(owners, chunks, k, holder_ref, waves_ref, parity):
    slots = holder_ref.shape[1]
    per_chunk = slots // 2 // owners // chunks
    wave = 2 * lax.broadcasted_iota(jnp.int32, (waves_ref.shape[2], slots), 0) + parity
    held = (holder_ref[...] == wave).astype(jnp.float32).astype(jnp.bfloat16)
    row = lax.broadcasted_iota(jnp.int32, (owners * per_chunk, slots), 0)
    pair = (lax.div(row, per_chunk) * chunks + k) * per_chunk + lax.rem(row, per_chunk)
    slot = lax.broadcasted_iota(jnp.int32, (owners * per_chunk, slots), 1)
    chosen = (lax.div(slot, 2) == pair).astype(jnp.float32).astype(jnp.bfloat16)
    pick = dot(chosen, held, NT)
    picked = pick.astype(jnp.bfloat16)
    parts = [
        dot(picked, waves_ref[parity, c]).reshape(owners, per_chunk, waves_ref.shape[3])
        for c in range(2)
    ]
    rows = jnp.concatenate(parts, axis=1).reshape(2 * per_chunk * owners, waves_ref.shape[3])
    return rows, pick[:, 0:1]


def analysis_kernel(
    owners, chunks, k, holder_ref, waves_hbm, state_hbm, forcing_hbm, send_hbm,
    waves, table, state, forcing, folded, send, ready, arrived, left,
):
    steps, levels, lats, lon_count = state.shape
    half = lon_count // 2
    rows = send.shape[2]

    def copies(n):
        span = pl.ds(n * levels, levels)
        return (
            pltpu.make_async_copy(state_hbm.at[span], state.at[n], arrived.at[n, 0]),
            pltpu.make_async_copy(forcing_hbm.at[span], forcing.at[n], arrived.at[n, 1]),
        )

    def leaving(n):
        span = pl.ds(n * levels, levels)
        return pltpu.make_async_copy(send.at[:, span], send_hbm.at[:, span], left.at[n])

    fetch = pltpu.make_async_copy(waves_hbm, waves, ready)
    fetch.start()

    @pl.loop(0, steps)
    def _(n):
        for copy in copies(n):
            copy.start()

    fetch.wait()
    for parity in range(2):
        found, _ = wave_rows(owners, chunks, k, holder_ref, waves, parity)
        table[parity] = found.astype(jnp.bfloat16)

    def take(n):
        for copy in copies(n):
            copy.wait()

    def fold(n, now):
        for level in range(levels):
            s = state[n, level].astype(jnp.float32)
            f = forcing[n, level].astype(jnp.float32)
            explicit = 0.7 * s + 0.5 * f + 0.3 * s / (1.0 + s * s)
            low, high = explicit[:, :half], explicit[:, half:]
            span = slice(level * lats, (level + 1) * lats)
            folded[now, 0, span, :] = (low + high).astype(jnp.bfloat16)
            folded[now, 1, span, :] = (low - high).astype(jnp.bfloat16)

    def transform(n, now):
        for parity in range(2):
            found = dot(table[parity], folded[now, parity], NT).astype(jnp.bfloat16)
            found = found.reshape(owners, rows // 2, levels * lats)
            mine = slice(parity * (rows // 2), (parity + 1) * (rows // 2))
            for level in range(levels):
                send[:, n * levels + level, mine, :] = found[
                    :, :, level * lats : (level + 1) * lats
                ]
        leaving(n).start()

    take(0)
    fold(0, 0)

    @pl.loop(0, (steps - 1) // 2)
    def _(j):
        take(2 * j + 1)
        take(2 * j + 2)
        transform(2 * j, 0)
        fold(2 * j + 1, 1)
        transform(2 * j + 1, 1)
        fold(2 * j + 2, 0)

    if steps % 2 == 0:
        take(steps - 1)
        fold(steps - 1, 1)
        transform(steps - 2, 0)
    transform(steps - 1, (steps - 1) % 2)

    @pl.loop(0, steps)
    def _(n):
        leaving(n).wait()


def run_analysis(owners, chunks, k, state, forcing, holder, table):
    levels, lats, lon_count = state.shape
    slots = holder.shape[1]
    rows = 2 * slots // owners // chunks
    count = 2 if levels % 2 == 0 else 1
    steps = levels // count
    kept = pltpu.VMEM((steps, count, lats, lon_count), jnp.bfloat16)
    anywhere = pl.BlockSpec(memory_space=pl.ANY)
    return pl.pallas_call(
        functools.partial(analysis_kernel, owners, chunks, k),
        in_specs=[pl.BlockSpec(memory_space=pltpu.VMEM)] + [anywhere] * 3,
        out_specs=anywhere,
        out_shape=jax.ShapeDtypeStruct((owners, levels, rows, lats), jnp.bfloat16),
        scratch_shapes=[
            pltpu.VMEM(table.shape, jnp.bfloat16),
            pltpu.VMEM((2, slots // chunks, lon_count // 2), jnp.bfloat16),
            kept,
            kept,
            pltpu.VMEM((2, 2, count * lats, lon_count // 2), jnp.bfloat16),
            pltpu.VMEM((owners, levels, rows, lats), jnp.bfloat16),
            pltpu.SemaphoreType.DMA,
            pltpu.SemaphoreType.DMA((steps, 2)),
            pltpu.SemaphoreType.DMA((steps,)),
        ],
        compiler_params=pltpu.CompilerParams(vmem_limit_bytes=VMEM_BYTES),
        cost_estimate=pl.CostEstimate(
            flops=2 * levels * lats * lon_count * slots // chunks,
            bytes_accessed=6 * levels * lats * lon_count,
            transcendentals=0,
        ),
        name="longitude_analysis",
    )(holder, table, state, forcing)


def synthesis_rows_kernel(owners, chunks, holder_ref, waves_ref, out_ref):
    for parity in range(2):
        for k in range(chunks):
            rows, zero = wave_rows(owners, chunks, k, holder_ref, waves_ref, parity)
            if parity == 0:
                count = zero.shape[0] // owners
                weight = (2.0 - zero).reshape(owners, count, 1)
                weight = jnp.concatenate([weight, weight], axis=1).reshape(-1, 1)
            else:
                weight = 2.0
            out_ref[parity, k] = (rows * weight).astype(jnp.bfloat16)


def synthesis_rows(owners, chunks, holder, table):
    shape = (2, chunks, holder.shape[1] // chunks, table.shape[3])
    return pl.pallas_call(
        functools.partial(synthesis_rows_kernel, owners, chunks),
        out_shape=jax.ShapeDtypeStruct(shape, jnp.bfloat16),
        compiler_params=pltpu.CompilerParams(vmem_limit_bytes=VMEM_BYTES),
        cost_estimate=pl.CostEstimate(
            flops=8 * holder.shape[1] * table.shape[2] * table.shape[3],
            bytes_accessed=4 * holder.shape[1] * table.shape[3],
            transcendentals=0,
        ),
        name="synthesis_rows",
    )(holder, table)


def pair_slots(first, waves, middle):
    late = (waves[first] >= middle).astype(jnp.int32)
    return first + late, first + 1 - late


def column_kernel(
    bands, k, waves_ref, recv_ref, low_basis, high_basis, low_solver, high_solver, send_ref,
    spread, back,
):
    owners, levels, rows, lats = recv_ref.shape
    groups = owners // bands
    per_chunk = rows // 4
    depth = groups * levels
    total = low_basis.shape[1]
    middle = total // 2
    i = pl.program_id(0)

    def places():
        size = levels * (rows + TILE)
        for r in range(owners):
            yield r, r // groups, slice(r % groups * size, (r % groups + 1) * size)

    @pl.when(i == 0)
    def _():
        for r, band, span in places():
            part = recv_ref[r].astype(jnp.float32)
            part = jnp.concatenate([part, part[:, :TILE]], axis=1)
            spread[band, span, :] = part.reshape(-1, lats)

    slots = pair_slots(2 * (k * per_chunk + i), waves_ref, middle)
    waves = [waves_ref[slot] for slot in slots]
    bases = [lax.rem(wave, 2) * (2 * per_chunk) + i for wave in waves]
    basis = [low_basis[0], high_basis[0]]
    solvers = [low_solver[0], high_solver[0]]
    lows = [0, middle]
    taken, coeffs, solved, grid = [], [], [], []
    for w in range(2):
        parts = [
            jnp.concatenate(
                [
                    spread[a, pl.ds(bases[w] + c * per_chunk, depth, stride=rows + TILE), :]
                    for a in range(bands)
                ],
                axis=1,
            )
            for c in range(2)
        ]
        taken.append(jnp.concatenate(parts, axis=0).astype(jnp.bfloat16))
    for w in range(2):
        found = dot(taken[w], basis[w])
        coeffs.append(
            jnp.concatenate([found[:depth], found[depth:]], axis=1).astype(jnp.bfloat16)
        )
    for w in range(2):
        found = dot(solvers[w], coeffs[w])
        count = total - lows[w]
        degree = lows[w] + lax.broadcasted_iota(jnp.int32, (depth, count), 1)
        parts = [
            jnp.where(degree >= waves[w], found[:, c * count : (c + 1) * count], 0.0)
            for c in range(2)
        ]
        solved.append(jnp.concatenate(parts, axis=0).astype(jnp.bfloat16))
    for w in range(2):
        grid.append(dot(solved[w], basis[w], NT))
    for w in range(2):
        for c in range(2):
            for a in range(bands):
                back[a, pl.ds(bases[w] + c * per_chunk, depth, stride=rows + TILE), :] = grid[w][
                    c * depth : (c + 1) * depth, a * lats : (a + 1) * lats
                ]

    @pl.when(i == pl.num_programs(0) - 1)
    def _():
        for r, band, span in places():
            part = back[band, span, :].reshape(levels, rows + TILE, lats)
            send_ref[r] = part[:, :rows].astype(jnp.bfloat16)


def run_columns(k, bands, waves, received, basis, solver):
    owners, levels, rows, lats = received.shape
    depth = owners // bands * levels
    total = basis.shape[1]
    middle = total // 2
    steps = rows // 4
    first = lambda i: 2 * (k * steps + i)
    low = lambda i, waves_ref: (pair_slots(first(i), waves_ref, middle)[0], 0, 0)
    high = lambda i, waves_ref: (pair_slots(first(i), waves_ref, middle)[1], 0, 0)
    upper = lambda i, waves_ref: (pair_slots(first(i), waves_ref, middle)[1], 0, 1)
    whole = pl.BlockSpec(received.shape, lambda i, waves_ref: (0, 0, 0, 0))
    scratch = pltpu.VMEM((bands, depth * (rows + TILE), lats), jnp.float32)
    return pl.pallas_call(
        functools.partial(column_kernel, bands, k),
        grid_spec=pltpu.PrefetchScalarGridSpec(
            num_scalar_prefetch=1,
            grid=(steps,),
            in_specs=[
                whole,
                pl.BlockSpec((1, total, total), low),
                pl.BlockSpec((1, total, total - middle), upper),
                pl.BlockSpec((1, depth, depth), low),
                pl.BlockSpec((1, depth, depth), high),
            ],
            out_specs=whole,
            scratch_shapes=[scratch, scratch],
        ),
        out_shape=jax.ShapeDtypeStruct(received.shape, jnp.bfloat16),
        compiler_params=pltpu.CompilerParams(vmem_limit_bytes=VMEM_BYTES),
        cost_estimate=pl.CostEstimate(
            flops=6 * steps * 2 * depth * total * total,
            bytes_accessed=4 * received.size + 3 * steps * total * total,
            transcendentals=0,
        ),
        name="legendre_solve",
    )(waves, received, basis, basis, solver, solver)


def synthesis_kernel(chunks, *refs):
    parts, (synth_ref, out_hbm, kept, out, arrived, left) = refs[:chunks], refs[chunks:]
    steps, _, owners, levels, rows, lats = kept.shape
    half = synth_ref.shape[-1]

    def copies(n):
        span = pl.ds(n * levels, levels)
        return [
            pltpu.make_async_copy(part.at[:, span], kept.at[n, k], arrived.at[n, k])
            for k, part in enumerate(parts)
        ]

    def leaving(n):
        span = pl.ds(n * levels, levels)
        return pltpu.make_async_copy(out.at[span], out_hbm.at[span], left.at[n])

    @pl.loop(0, steps)
    def _(n):
        for copy in copies(n):
            copy.start()

    @pl.loop(0, steps)
    def _(i):
        for copy in copies(i):
            copy.wait()
        sums = []
        for parity in range(2):
            terms = []
            for k in range(chunks):
                found = kept[i, k, :, :, parity * (rows // 2) : (parity + 1) * (rows // 2), :]
                found = jnp.concatenate(
                    [found[:, n].reshape(owners * rows // 2, lats) for n in range(levels)], axis=1
                )
                terms.append(dot(found, synth_ref[parity, k], TN))
            sums.append(sum(terms[1:], terms[0]))
        for n in range(levels):
            even, odd = [found[n * lats : (n + 1) * lats] for found in sums]
            out[i * levels + n, :, :half] = (even + odd).astype(jnp.bfloat16)
            out[i * levels + n, :, half:] = (even - odd).astype(jnp.bfloat16)
        leaving(i).start()

    @pl.loop(0, steps)
    def _(n):
        leaving(n).wait()


def run_synthesis(parts, synth):
    owners, levels, rows, lats = parts[0].shape
    lon_count = 2 * synth.shape[-1]
    chunks = len(parts)
    count = 2 if levels % 2 == 0 else 1
    steps = levels // count
    anywhere = pl.BlockSpec(memory_space=pl.ANY)
    return pl.pallas_call(
        functools.partial(synthesis_kernel, chunks),
        in_specs=[anywhere] * chunks + [pl.BlockSpec(memory_space=pltpu.VMEM)],
        out_specs=anywhere,
        out_shape=jax.ShapeDtypeStruct((levels, lats, lon_count), jnp.bfloat16),
        scratch_shapes=[
            pltpu.VMEM((steps, chunks, owners, count, rows, lats), jnp.bfloat16),
            pltpu.VMEM((levels, lats, lon_count), jnp.bfloat16),
            pltpu.SemaphoreType.DMA((steps, chunks)),
            pltpu.SemaphoreType.DMA((steps,)),
        ],
        compiler_params=pltpu.CompilerParams(vmem_limit_bytes=VMEM_BYTES),
        cost_estimate=pl.CostEstimate(
            flops=levels * lats * lon_count * lon_count,
            bytes_accessed=4 * levels * lats * lon_count,
            transcendentals=0,
        ),
        name="longitude_synthesis",
    )(*parts, synth)


def exchange(part):
    owners, levels, rows, lats = part.shape
    flat = part.reshape(owners, levels * rows, lats)
    return lax.all_to_all(flat, OWNERS, 0, 0, tiled=True).reshape(part.shape)


def chunked_shards(lat_bands, level_groups, chunks):
    owners = lat_bands * level_groups

    def shards(
        thermal_state_grid,
        thermal_forcing,
        spherical_basis_table,
        implicit_solver_matrix,
        fourier_order_holder,
    ):
        slots = spherical_basis_table.shape[0]
        table = jnp.asarray(longitude_waves(thermal_state_grid.shape[2]))
        holder = fourier_order_holder.reshape(1, -1)
        sends = [
            run_analysis(owners, chunks, k, thermal_state_grid, thermal_forcing, holder, table)
            for k in range(chunks)
        ]
        synth = synthesis_rows(owners, chunks, holder, table)
        owner = lax.axis_index(OWNERS)
        waves = lax.dynamic_slice_in_dim(fourier_order_holder, owner * slots, slots)
        received = [exchange(part) for part in sends]
        solved = [
            run_columns(
                k,
                lat_bands,
                waves,
                received[k],
                spherical_basis_table,
                implicit_solver_matrix,
            )
            for k in range(chunks)
        ]
        returned = [exchange(part) for part in solved]
        return run_synthesis(returned, synth)

    return shards


def solution(mesh):
    shape = mesh.shape
    bands, groups = shape["lat"], shape["lev"] * shape["sub"]

    def shards(state, forcing, basis, solver, holder):
        levels, lats, lon_count = state.shape
        pairs = basis.shape[0] // 2
        tiled = pairs % (CHUNKS * TILE) == 0 and levels * groups % TILE == 0
        if tiled and lats % 128 == 0 and lon_count == 2 * holder.shape[0]:
            body = chunked_shards(bands, groups, CHUNKS)
        else:
            body = general_shards(bands, groups)
        return body(state, forcing, basis, solver, holder)

    return jax.shard_map(
        shards,
        mesh=mesh,
        in_specs=(
            P(("members", "lev", "sub"), "lat", None),
            P(("members", "lev", "sub"), "lat", None),
            P(OWNERS, None, None),
            P(OWNERS, None, None),
            P(),
        ),
        out_specs=P(("members", "lev", "sub"), "lat", None),
        check_vma=False,
    )
```

```python
import functools
import math

import jax
import jax.numpy as jnp
import numpy as np
from jax import lax
from jax.experimental import pallas as pl
from jax.experimental.pallas import tpu as pltpu
from jax.sharding import PartitionSpec as P

OWNERS = ("lat", "lev", "sub")
CHUNKS = 2
HINT = 33
FEW = 4


def raw_table(fourier_order_holder, lon_count):
    meridian_position = jnp.arange(lon_count, dtype=jnp.int32)
    phases = fourier_order_holder[:, None] * meridian_position[None, :] % lon_count
    angles = phases.astype(jnp.float32) * (2.0 * math.pi / lon_count)
    factor = 1.0 / math.sqrt(lon_count)
    stacked = jnp.stack([jnp.cos(angles), -jnp.sin(angles)], axis=1)
    return stacked.reshape(2 * fourier_order_holder.shape[0], lon_count) * factor


def general_shards(lat_bands, level_groups):
    def shards(
        thermal_state_grid,
        thermal_forcing,
        spherical_basis_table,
        implicit_solver_matrix,
        fourier_order_holder,
    ):
        levels, lats, lon_count = thermal_state_grid.shape
        slots, lat_total, wave_total = spherical_basis_table.shape
        owners = lat_bands * level_groups
        state = thermal_state_grid.astype(jnp.float32)
        explicit = (
            state
            + 0.5 * thermal_forcing.astype(jnp.float32)
            - 0.3 * state * state * state / (1.0 + state * state)
        ).astype(jnp.bfloat16)
        raw = raw_table(fourier_order_holder, lon_count)
        analysis = raw.astype(jnp.bfloat16)
        weights = jnp.where(fourier_order_holder == 0, 1.0, 2.0).astype(jnp.float32)
        synthesis = (raw * jnp.repeat(weights, 2)[:, None]).astype(jnp.bfloat16)
        spectral = jnp.einsum(
            "sj,lxj->slx", analysis, explicit, preferred_element_type=jnp.float32
        ).astype(jnp.bfloat16)
        spectral = spectral.reshape(owners, 2 * slots * levels, lats)
        spectral = lax.all_to_all(spectral, OWNERS, 0, 0, tiled=True)
        spectral = spectral.reshape(lat_bands, level_groups, slots, 2, levels, lats)
        spectral = spectral.transpose(2, 3, 1, 4, 0, 5)
        spectral = spectral.reshape(slots, 2 * level_groups * levels, lat_total)
        coeffs = jnp.einsum(
            "srx,sxn->srn", spectral, spherical_basis_table, preferred_element_type=jnp.float32
        ).astype(jnp.bfloat16)
        coeffs = coeffs.reshape(slots, 2, level_groups * levels, wave_total)
        solved = jnp.einsum(
            "skl,scln->sckn", implicit_solver_matrix, coeffs, preferred_element_type=jnp.float32
        )
        owner = lax.axis_index(OWNERS)
        waves = lax.dynamic_slice_in_dim(fourier_order_holder, owner * slots, slots)
        live = jnp.arange(wave_total, dtype=jnp.int32)[None, :] >= waves[:, None]
        solved = jnp.where(live[:, None, None, :], solved, 0.0).astype(jnp.bfloat16)
        solved = solved.reshape(slots, 2 * level_groups * levels, wave_total)
        back = jnp.einsum(
            "srn,sxn->srx", solved, spherical_basis_table, preferred_element_type=jnp.float32
        ).astype(jnp.bfloat16)
        back = back.reshape(slots, 2, level_groups, levels, lat_bands, lats)
        back = back.transpose(4, 2, 0, 1, 3, 5).reshape(owners, 2 * slots * levels, lats)
        back = lax.all_to_all(back, OWNERS, 0, 0, tiled=True)
        back = back.reshape(2 * slots * owners, levels, lats)
        return jnp.einsum(
            "slx,sj->lxj", back, synthesis, preferred_element_type=jnp.float32
        ).astype(jnp.bfloat16)

    return shards


TILE = 8
VMEM_BYTES = 60 * 1024 * 1024
NT = (((1,), (1,)), ((), ()))
TN = (((0,), (0,)), ((), ()))


def dot(a, b, dims=(((1,), (0,)), ((), ()))):
    return lax.dot_general(a, b, dims, preferred_element_type=jnp.float32)


def longitude_waves(lon_count):
    half = lon_count // 2
    waves = np.arange(half).reshape(half // 2, 2).T
    phases = waves[:, :, None] * np.arange(half)[None, None, :] % lon_count
    angles = phases.astype(np.float32) * np.float32(2.0 * math.pi / lon_count)
    table = np.stack([np.cos(angles), -np.sin(angles)], axis=1) / math.sqrt(lon_count)
    return table.astype(jnp.bfloat16)


def wave_rows(owners, chunks, k, holder_ref, waves_ref, parity, me=0):
    slots = holder_ref.shape[1]
    per_chunk = slots // 2 // owners // chunks
    wave = 2 * lax.broadcasted_iota(jnp.int32, (waves_ref.shape[2], slots), 0) + parity
    held = (holder_ref[...] == wave).astype(jnp.float32).astype(jnp.bfloat16)
    row = lax.broadcasted_iota(jnp.int32, (owners * per_chunk, slots), 0)
    owner = lax.bitwise_xor(lax.div(row, per_chunk), me)
    pair = (owner * chunks + k) * per_chunk + lax.rem(row, per_chunk)
    slot = lax.broadcasted_iota(jnp.int32, (owners * per_chunk, slots), 1)
    chosen = (lax.div(slot, 2) == pair).astype(jnp.float32).astype(jnp.bfloat16)
    pick = dot(chosen, held, NT)
    picked = pick.astype(jnp.bfloat16)
    parts = [
        dot(picked, waves_ref[parity, c]).reshape(owners, per_chunk, waves_ref.shape[3])
        for c in range(2)
    ]
    rows = jnp.concatenate(parts, axis=1).reshape(2 * per_chunk * owners, waves_ref.shape[3])
    return rows, pick[:, 0:1]


def analysis_kernel(
    owners, chunks, k, begin, apart, holder_ref, waves_hbm, state_hbm, forcing_hbm, *refs
):
    send_hbm, waves, table, state, forcing, folded, send, ready, arrived, left = refs[-10:]
    steps, levels, lats, lon_count = state.shape
    half = lon_count // 2
    rows = send.shape[2]

    def copies(n):
        span = pl.ds(begin + n * levels, levels)
        return (
            pltpu.make_async_copy(state_hbm.at[span], state.at[n], arrived.at[n, 0]),
            pltpu.make_async_copy(forcing_hbm.at[span], forcing.at[n], arrived.at[n, 1]),
        )

    def leaving(n):
        span = pl.ds(n * levels, levels)
        return pltpu.make_async_copy(send.at[:, span], send_hbm.at[:, span], left.at[n])

    fetch = pltpu.make_async_copy(waves_hbm, waves, ready)
    fetch.start()

    @pl.loop(0, steps)
    def _(n):
        for copy in copies(n):
            copy.start()

    fetch.wait()
    for parity in range(2):
        me = lax.axis_index(OWNERS) if apart else 0
        found, _ = wave_rows(owners, chunks, k, holder_ref, waves, parity, me)
        table[parity] = found.astype(jnp.bfloat16)

    def take(n):
        for copy in copies(n):
            copy.wait()

    def fold(n, now):
        for level in range(levels):
            s = state[n, level].astype(jnp.float32)
            f = forcing[n, level].astype(jnp.float32)
            explicit = 0.7 * s + 0.5 * f + 0.3 * s / (1.0 + s * s)
            low, high = explicit[:, :half], explicit[:, half:]
            span = slice(level * lats, (level + 1) * lats)
            folded[now, 0, span, :] = (low + high).astype(jnp.bfloat16)
            folded[now, 1, span, :] = (low - high).astype(jnp.bfloat16)

    def transform(n, now):
        for parity in range(2):
            found = dot(table[parity], folded[now, parity], NT).astype(jnp.bfloat16)
            found = found.reshape(owners, rows // 2, levels * lats)
            mine = slice(parity * (rows // 2), (parity + 1) * (rows // 2))
            for level in range(levels):
                send[:, n * levels + level, mine, :] = found[
                    :, :, level * lats : (level + 1) * lats
                ]
        leaving(n).start()

    take(0)
    fold(0, 0)

    @pl.loop(0, (steps - 1) // 2)
    def _(j):
        take(2 * j + 1)
        take(2 * j + 2)
        transform(2 * j, 0)
        fold(2 * j + 1, 1)
        transform(2 * j + 1, 1)
        fold(2 * j + 2, 0)

    if steps % 2 == 0:
        take(steps - 1)
        fold(steps - 1, 1)
        transform(steps - 2, 0)
    transform(steps - 1, (steps - 1) % 2)

    @pl.loop(0, steps)
    def _(n):
        leaving(n).wait()


def run_analysis(owners, chunks, k, piece, state, forcing, holder, table, before):
    begin, end, apart = piece
    _, lats, lon_count = state.shape
    levels = end - begin
    slots = holder.shape[1]
    rows = 2 * slots // owners // chunks
    count = 2 if levels % 2 == 0 else 1
    steps = levels // count
    kept = pltpu.VMEM((steps, count, lats, lon_count), jnp.bfloat16)
    anywhere = pl.BlockSpec(memory_space=pl.ANY)
    return pl.pallas_call(
        functools.partial(analysis_kernel, owners, chunks, k, begin, apart),
        in_specs=[pl.BlockSpec(memory_space=pltpu.VMEM)] + [anywhere] * (3 + len(before)),
        out_specs=anywhere,
        out_shape=jax.ShapeDtypeStruct((owners, levels, rows, lats), jnp.bfloat16),
        scratch_shapes=[
            pltpu.VMEM(table.shape, jnp.bfloat16),
            pltpu.VMEM((2, slots // chunks, lon_count // 2), jnp.bfloat16),
            kept,
            kept,
            pltpu.VMEM((2, 2, count * lats, lon_count // 2), jnp.bfloat16),
            pltpu.VMEM((owners, levels, rows, lats), jnp.bfloat16),
            pltpu.SemaphoreType.DMA,
            pltpu.SemaphoreType.DMA((steps, 2)),
            pltpu.SemaphoreType.DMA((steps,)),
        ],
        compiler_params=pltpu.CompilerParams(vmem_limit_bytes=VMEM_BYTES),
        cost_estimate=pl.CostEstimate(
            flops=2 * levels * lats * lon_count * slots // chunks,
            bytes_accessed=6 * levels * lats * lon_count,
            transcendentals=0,
        ),
        name="longitude_analysis",
    )(holder, table, state, forcing, *before)


def synthesis_rows_kernel(owners, chunks, holder_ref, waves_ref, out_ref):
    for parity in range(2):
        for k in range(chunks):
            rows, zero = wave_rows(owners, chunks, k, holder_ref, waves_ref, parity)
            if parity == 0:
                count = zero.shape[0] // owners
                weight = (2.0 - zero).reshape(owners, count, 1)
                weight = jnp.concatenate([weight, weight], axis=1).reshape(-1, 1)
            else:
                weight = 2.0
            out_ref[parity, k] = (rows * weight).astype(jnp.bfloat16)


def synthesis_rows(owners, chunks, holder, table):
    shape = (2, chunks, holder.shape[1] // chunks, table.shape[3])
    return pl.pallas_call(
        functools.partial(synthesis_rows_kernel, owners, chunks),
        out_shape=jax.ShapeDtypeStruct(shape, jnp.bfloat16),
        compiler_params=pltpu.CompilerParams(vmem_limit_bytes=VMEM_BYTES),
        cost_estimate=pl.CostEstimate(
            flops=8 * 200 * holder.shape[1] * table.shape[2] * table.shape[3],
            bytes_accessed=4 * holder.shape[1] * table.shape[3],
            transcendentals=0,
        ),
        name="synthesis_rows",
    )(holder, table)


def pair_slots(first, waves, middle):
    late = (waves[first] >= middle).astype(jnp.int32)
    return first + late, first + 1 - late


def owner_blocks(owners, bands, levels, refs, pieces):
    groups = owners // bands
    blocks = 0
    for ref, (begin, end, apart) in zip(refs, pieces):
        rows = ref.shape[2] + TILE
        for r in range(ref.shape[0]):
            place = (blocks + r) % owners
            owner = lax.bitwise_xor(lax.axis_index(OWNERS), place) if apart else r
            start = (lax.rem(owner, groups) * levels + begin) * rows
            if apart:
                start = pl.multiple_of(start, TILE)
            yield ref.at[r], lax.div(owner, groups), pl.ds(start, (end - begin) * rows)
        blocks += ref.shape[0]


def column_kernel(owners, bands, k, pieces_in, pieces_out, waves_ref, *refs):
    received, refs = refs[: len(pieces_in)], refs[len(pieces_in) :]
    low_basis, high_basis, low_solver, high_solver = refs[:4]
    sends, (spread, back) = refs[-2 - len(pieces_out) : -2], refs[-2:]
    levels = pieces_in[-1][1]
    rows, lats = received[0].shape[-2:]
    per_chunk = rows // 4
    depth = owners // bands * levels
    total = low_basis.shape[1]
    middle = total // 2
    i = pl.program_id(0)

    @pl.when(i == 0)
    def _():
        for ref, band, span in owner_blocks(owners, bands, levels, received, pieces_in):
            part = ref[...].astype(jnp.float32)
            part = jnp.concatenate([part, part[:, :TILE]], axis=1)
            spread[band, span, :] = part.reshape(-1, lats)

    slots = pair_slots(2 * (k * per_chunk + i), waves_ref, middle)
    waves = [waves_ref[slot] for slot in slots]
    bases = [lax.rem(wave, 2) * (2 * per_chunk) + i for wave in waves]
    basis = [low_basis[0], high_basis[0]]
    solvers = [low_solver[0], high_solver[0]]
    lows = [0, middle]
    taken, coeffs, solved, grid = [], [], [], []
    for w in range(2):
        parts = [
            jnp.concatenate(
                [
                    spread[a, pl.ds(bases[w] + c * per_chunk, depth, stride=rows + TILE), :]
                    for a in range(bands)
                ],
                axis=1,
            )
            for c in range(2)
        ]
        taken.append(jnp.concatenate(parts, axis=0).astype(jnp.bfloat16))
    for w in range(2):
        found = dot(taken[w], basis[w])
        coeffs.append(
            jnp.concatenate([found[:depth], found[depth:]], axis=1).astype(jnp.bfloat16)
        )
    for w in range(2):
        found = dot(solvers[w], coeffs[w])
        count = total - lows[w]
        degree = lows[w] + lax.broadcasted_iota(jnp.int32, (depth, count), 1)
        parts = [
            jnp.where(degree >= waves[w], found[:, c * count : (c + 1) * count], 0.0)
            for c in range(2)
        ]
        solved.append(jnp.concatenate(parts, axis=0).astype(jnp.bfloat16))
    for w in range(2):
        grid.append(dot(solved[w], basis[w], NT))
    for w in range(2):
        for c in range(2):
            for a in range(bands):
                back[a, pl.ds(bases[w] + c * per_chunk, depth, stride=rows + TILE), :] = grid[w][
                    c * depth : (c + 1) * depth, a * lats : (a + 1) * lats
                ]

    @pl.when(i == pl.num_programs(0) - 1)
    def _():
        for ref, band, span in owner_blocks(owners, bands, levels, sends, pieces_out):
            part = back[band, span, :].reshape(ref.shape[0], rows + TILE, lats)
            ref[...] = part[:, :rows].astype(jnp.bfloat16)


def run_columns(k, owners, bands, pieces_in, pieces_out, waves, received, before, basis, solver):
    rows, lats = received[0].shape[-2:]
    levels = pieces_in[-1][1]
    depth = owners // bands * levels
    total = basis.shape[1]
    middle = total // 2
    steps = rows // 4
    first = lambda i: 2 * (k * steps + i)
    low = lambda i, waves_ref: (pair_slots(first(i), waves_ref, middle)[0], 0, 0)
    high = lambda i, waves_ref: (pair_slots(first(i), waves_ref, middle)[1], 0, 0)
    upper = lambda i, waves_ref: (pair_slots(first(i), waves_ref, middle)[1], 0, 1)
    whole = lambda shape: pl.BlockSpec(shape, lambda i, waves_ref: (0, 0, 0, 0))
    sizes = [(owners, end - begin, rows, lats) for begin, end, _ in pieces_out]
    scratch = pltpu.VMEM((bands, depth * (rows + TILE), lats), jnp.float32)
    return pl.pallas_call(
        functools.partial(column_kernel, owners, bands, k, pieces_in, pieces_out),
        grid_spec=pltpu.PrefetchScalarGridSpec(
            num_scalar_prefetch=1,
            grid=(steps,),
            in_specs=[whole(part.shape) for part in received]
            + [
                pl.BlockSpec((1, total, total), low),
                pl.BlockSpec((1, total, total - middle), upper),
                pl.BlockSpec((1, depth, depth), low),
                pl.BlockSpec((1, depth, depth), high),
            ]
            + [pl.BlockSpec(memory_space=pl.ANY)] * len(before),
            out_specs=[whole(size) for size in sizes],
            scratch_shapes=[scratch, scratch],
        ),
        out_shape=[jax.ShapeDtypeStruct(size, jnp.bfloat16) for size in sizes],
        compiler_params=pltpu.CompilerParams(vmem_limit_bytes=VMEM_BYTES),
        cost_estimate=pl.CostEstimate(
            flops=HINT * 6 * steps * 2 * depth * total * total,
            bytes_accessed=4 * bands * depth * rows * lats + 3 * steps * total * total,
            transcendentals=0,
        ),
        name="legendre_solve",
    )(waves, *received, basis, basis, solver, solver, *before)


def synthesis_kernel(owners, pieces, *refs):
    taking = sum(len(some) for some in pieces)
    parts, (synth_ref, out_hbm, kept, out, arrived, left) = refs[:taking], refs[taking:]
    steps, chunks, _, levels, rows, lats = kept.shape
    half = synth_ref.shape[-1]
    me = lax.axis_index(OWNERS)
    cuts = sorted({end // levels for some in pieces for _, end, _ in some})

    def copies(n, first, entire):
        left = parts
        for k, some in enumerate(pieces):
            for part, (begin, end, apart) in zip(left, some):
                if not begin <= first * levels < end:
                    continue
                span = pl.ds(n * levels - begin, levels)
                if apart and not entire:
                    for r in range(owners):
                        place = kept.at[n, k, lax.bitwise_xor(me, r)]
                        yield pltpu.make_async_copy(part.at[r, span], place, arrived.at[n, k])
                else:
                    yield pltpu.make_async_copy(part.at[:, span], kept.at[n, k], arrived.at[n, k])
            left = left[len(some) :]

    def leaving(n):
        span = pl.ds(n * levels, levels)
        return pltpu.make_async_copy(out.at[span], out_hbm.at[span], left.at[n])

    for first, last in zip([0] + cuts, cuts):

        @pl.loop(first, last)
        def _(n, first=first):
            for copy in copies(n, first, False):
                copy.start()

    def step(i, first):
        for copy in copies(i, first, True):
            copy.wait()
        sums = []
        for parity in range(2):
            terms = []
            for k in range(chunks):
                found = kept[i, k, :, :, parity * (rows // 2) : (parity + 1) * (rows // 2), :]
                found = jnp.concatenate(
                    [found[:, n].reshape(owners * rows // 2, lats) for n in range(levels)], axis=1
                )
                terms.append(dot(found, synth_ref[parity, k], TN))
            sums.append(sum(terms[1:], terms[0]))
        for n in range(levels):
            even, odd = [found[n * lats : (n + 1) * lats] for found in sums]
            out[i * levels + n, :, :half] = (even + odd).astype(jnp.bfloat16)
            out[i * levels + n, :, half:] = (even - odd).astype(jnp.bfloat16)
        leaving(i).start()

    for first, last in zip([0] + cuts, cuts):
        pl.loop(first, last)(functools.partial(step, first=first))

    @pl.loop(0, steps)
    def _(n):
        leaving(n).wait()


def run_synthesis(pieces, parts, synth):
    owners, _, rows, lats = parts[0].shape
    levels = pieces[0][-1][1]
    lon_count = 2 * synth.shape[-1]
    chunks = len(pieces)
    count = 2 if levels % 2 == 0 else 1
    steps = levels // count
    anywhere = pl.BlockSpec(memory_space=pl.ANY)
    return pl.pallas_call(
        functools.partial(synthesis_kernel, owners, pieces),
        in_specs=[anywhere] * len(parts) + [pl.BlockSpec(memory_space=pltpu.VMEM)],
        out_specs=anywhere,
        out_shape=jax.ShapeDtypeStruct((levels, lats, lon_count), jnp.bfloat16),
        scratch_shapes=[
            pltpu.VMEM((steps, chunks, owners, count, rows, lats), jnp.bfloat16),
            pltpu.VMEM((levels, lats, lon_count), jnp.bfloat16),
            pltpu.SemaphoreType.DMA((steps, chunks)),
            pltpu.SemaphoreType.DMA((steps,)),
        ],
        compiler_params=pltpu.CompilerParams(vmem_limit_bytes=VMEM_BYTES),
        cost_estimate=pl.CostEstimate(
            flops=levels * lats * lon_count * lon_count,
            bytes_accessed=4 * levels * lats * lon_count,
            transcendentals=0,
        ),
        name="longitude_synthesis",
    )(*parts, synth)


def exchange(part):
    owners, levels, rows, lats = part.shape
    flat = part.reshape(owners, levels * rows, lats)
    return lax.all_to_all(flat, OWNERS, 0, 0, tiled=True).reshape(part.shape)


def swap(part, bits):
    owners = part.shape[0]
    for bit in bits:
        halves = part.reshape((owners // 2 // bit, 2, bit) + part.shape[1:])
        given = lax.ppermute(halves[:, 1], OWNERS, [(o, o ^ bit) for o in range(owners)])
        part = jnp.stack([halves[:, 0], given], axis=1).reshape(part.shape)
    return halves[0, 0], given[0]


def chunked_shards(lat_bands, level_groups, chunks):
    owners = lat_bands * level_groups
    far, near = owners // 2, [2**n for n in range(int(math.log2(owners)) - 1)]

    def shards(
        thermal_state_grid,
        thermal_forcing,
        spherical_basis_table,
        implicit_solver_matrix,
        fourier_order_holder,
    ):
        levels = thermal_state_grid.shape[0]
        slots = spherical_basis_table.shape[0]
        table = jnp.asarray(longitude_waves(thermal_state_grid.shape[2]))
        holder = fourier_order_holder.reshape(1, -1)
        owner = lax.axis_index(OWNERS)
        waves = lax.dynamic_slice_in_dim(fourier_order_holder, owner * slots, slots)

        def analyse(k, piece, before):
            return run_analysis(
                owners, chunks, k, piece, thermal_state_grid, thermal_forcing, holder, table, before
            )

        def columns(k, pieces_in, pieces_out, received, before):
            return run_columns(
                k, owners, lat_bands, pieces_in, pieces_out, waves, received, before,
                spherical_basis_table, implicit_solver_matrix,
            )

        whole = [(0, levels, False)]
        few = levels * FEW // 34 // 2 * 2
        cut, last = levels - 2 * few, levels - few
        first = exchange(analyse(0, whole[0], []))
        main = analyse(1, (0, cut, False), [])
        rest = analyse(1, (cut, levels, True), [main])
        early, late = rest[:, :few], rest[:, few:]
        early = swap(early, near + [far])
        second = exchange(main)
        pieces = [(0, last, False), (last, levels, True)]
        solved, aside = columns(0, whole, pieces, [first], early[1:])
        solved, late = lax.optimization_barrier((solved, late))
        late = swap(late, near + [far])
        first = exchange(solved)
        split = [(0, cut, False)] + [(cut, last, True)] * 2 + [(last, levels, True)] * 2
        (solved,) = columns(1, split, whole, [second, *early, *late], [])
        solved, aside = lax.optimization_barrier((solved, aside))
        aside = jnp.concatenate(swap(aside, near + [far]))
        second = exchange(solved)
        synth = synthesis_rows(owners, chunks, holder, table)
        return run_synthesis([pieces, whole], [first, aside, second], synth)

    return shards


def solution(mesh):
    shape = mesh.shape
    bands, groups = shape["lat"], shape["lev"] * shape["sub"]

    def shards(state, forcing, basis, solver, holder):
        levels, lats, lon_count = state.shape
        pairs = basis.shape[0] // 2
        tiled = pairs % (CHUNKS * TILE) == 0 and levels * groups % TILE == 0
        tiled = tiled and bands > 1 and bands * groups == 2 ** int(math.log2(bands * groups))
        if tiled and levels % 2 == 0 and lats % 128 == 0 and lon_count == 2 * holder.shape[0]:
            body = chunked_shards(bands, groups, CHUNKS)
        else:
            body = general_shards(bands, groups)
        return body(state, forcing, basis, solver, holder)

    return jax.shard_map(
        shards,
        mesh=mesh,
        in_specs=(
            P(("members", "lev", "sub"), "lat", None),
            P(("members", "lev", "sub"), "lat", None),
            P(OWNERS, None, None),
            P(OWNERS, None, None),
            P(),
        ),
        out_specs=P(("members", "lev", "sub"), "lat", None),
        check_vma=False,
    )
```

```python
import functools
import math

import jax
import jax.numpy as jnp
import numpy as np
from jax import lax
from jax.experimental import pallas as pl
from jax.experimental.pallas import tpu as pltpu
from jax.sharding import PartitionSpec as P

OWNERS = ("lat", "lev", "sub")
CHUNKS = 2
HINT = 33
FEW = 6


def raw_table(fourier_order_holder, lon_count):
    meridian_position = jnp.arange(lon_count, dtype=jnp.int32)
    phases = fourier_order_holder[:, None] * meridian_position[None, :] % lon_count
    angles = phases.astype(jnp.float32) * (2.0 * math.pi / lon_count)
    factor = 1.0 / math.sqrt(lon_count)
    stacked = jnp.stack([jnp.cos(angles), -jnp.sin(angles)], axis=1)
    return stacked.reshape(2 * fourier_order_holder.shape[0], lon_count) * factor


def general_shards(lat_bands, level_groups):
    def shards(
        thermal_state_grid,
        thermal_forcing,
        spherical_basis_table,
        implicit_solver_matrix,
        fourier_order_holder,
    ):
        levels, lats, lon_count = thermal_state_grid.shape
        slots, lat_total, wave_total = spherical_basis_table.shape
        owners = lat_bands * level_groups
        state = thermal_state_grid.astype(jnp.float32)
        explicit = (
            state
            + 0.5 * thermal_forcing.astype(jnp.float32)
            - 0.3 * state * state * state / (1.0 + state * state)
        ).astype(jnp.bfloat16)
        raw = raw_table(fourier_order_holder, lon_count)
        analysis = raw.astype(jnp.bfloat16)
        weights = jnp.where(fourier_order_holder == 0, 1.0, 2.0).astype(jnp.float32)
        synthesis = (raw * jnp.repeat(weights, 2)[:, None]).astype(jnp.bfloat16)
        spectral = jnp.einsum(
            "sj,lxj->slx", analysis, explicit, preferred_element_type=jnp.float32
        ).astype(jnp.bfloat16)
        spectral = spectral.reshape(owners, 2 * slots * levels, lats)
        spectral = lax.all_to_all(spectral, OWNERS, 0, 0, tiled=True)
        spectral = spectral.reshape(lat_bands, level_groups, slots, 2, levels, lats)
        spectral = spectral.transpose(2, 3, 1, 4, 0, 5)
        spectral = spectral.reshape(slots, 2 * level_groups * levels, lat_total)
        coeffs = jnp.einsum(
            "srx,sxn->srn", spectral, spherical_basis_table, preferred_element_type=jnp.float32
        ).astype(jnp.bfloat16)
        coeffs = coeffs.reshape(slots, 2, level_groups * levels, wave_total)
        solved = jnp.einsum(
            "skl,scln->sckn", implicit_solver_matrix, coeffs, preferred_element_type=jnp.float32
        )
        owner = lax.axis_index(OWNERS)
        waves = lax.dynamic_slice_in_dim(fourier_order_holder, owner * slots, slots)
        live = jnp.arange(wave_total, dtype=jnp.int32)[None, :] >= waves[:, None]
        solved = jnp.where(live[:, None, None, :], solved, 0.0).astype(jnp.bfloat16)
        solved = solved.reshape(slots, 2 * level_groups * levels, wave_total)
        back = jnp.einsum(
            "srn,sxn->srx", solved, spherical_basis_table, preferred_element_type=jnp.float32
        ).astype(jnp.bfloat16)
        back = back.reshape(slots, 2, level_groups, levels, lat_bands, lats)
        back = back.transpose(4, 2, 0, 1, 3, 5).reshape(owners, 2 * slots * levels, lats)
        back = lax.all_to_all(back, OWNERS, 0, 0, tiled=True)
        back = back.reshape(2 * slots * owners, levels, lats)
        return jnp.einsum(
            "slx,sj->lxj", back, synthesis, preferred_element_type=jnp.float32
        ).astype(jnp.bfloat16)

    return shards


TILE = 8
VMEM_BYTES = 60 * 1024 * 1024
NT = (((1,), (1,)), ((), ()))
TN = (((0,), (0,)), ((), ()))


def dot(a, b, dims=(((1,), (0,)), ((), ()))):
    return lax.dot_general(a, b, dims, preferred_element_type=jnp.float32)


def longitude_waves(lon_count):
    half = lon_count // 2
    waves = np.arange(half).reshape(half // 2, 2).T
    phases = waves[:, :, None] * np.arange(half)[None, None, :] % lon_count
    angles = phases.astype(np.float32) * np.float32(2.0 * math.pi / lon_count)
    table = np.stack([np.cos(angles), -np.sin(angles)], axis=1) / math.sqrt(lon_count)
    return table.astype(jnp.bfloat16)


def wave_rows(owners, chunks, k, holder_ref, waves_ref, parity, me=0):
    slots = holder_ref.shape[1]
    per_chunk = slots // 2 // owners // chunks
    wave = 2 * lax.broadcasted_iota(jnp.int32, (waves_ref.shape[2], slots), 0) + parity
    held = (holder_ref[...] == wave).astype(jnp.float32).astype(jnp.bfloat16)
    row = lax.broadcasted_iota(jnp.int32, (owners * per_chunk, slots), 0)
    owner = lax.bitwise_xor(lax.div(row, per_chunk), me)
    pair = (owner * chunks + k) * per_chunk + lax.rem(row, per_chunk)
    slot = lax.broadcasted_iota(jnp.int32, (owners * per_chunk, slots), 1)
    chosen = (lax.div(slot, 2) == pair).astype(jnp.float32).astype(jnp.bfloat16)
    pick = dot(chosen, held, NT)
    picked = pick.astype(jnp.bfloat16)
    parts = [
        dot(picked, waves_ref[parity, c]).reshape(owners, per_chunk, waves_ref.shape[3])
        for c in range(2)
    ]
    rows = jnp.concatenate(parts, axis=1).reshape(2 * per_chunk * owners, waves_ref.shape[3])
    return rows, pick[:, 0:1]


def analysis_kernel(
    owners, chunks, k, begin, apart, holder_ref, waves_hbm, state_hbm, forcing_hbm, *refs
):
    send_hbm, waves, table, state, forcing, folded, send, ready, arrived, left = refs[-10:]
    steps, levels, lats, lon_count = state.shape
    half = lon_count // 2
    rows = send.shape[2]

    def copies(n):
        span = pl.ds(begin + n * levels, levels)
        return (
            pltpu.make_async_copy(state_hbm.at[span], state.at[n], arrived.at[n, 0]),
            pltpu.make_async_copy(forcing_hbm.at[span], forcing.at[n], arrived.at[n, 1]),
        )

    def leaving(n):
        span = pl.ds(n * levels, levels)
        return pltpu.make_async_copy(send.at[:, span], send_hbm.at[:, span], left.at[n])

    fetch = pltpu.make_async_copy(waves_hbm, waves, ready)
    fetch.start()

    @pl.loop(0, steps)
    def _(n):
        for copy in copies(n):
            copy.start()

    fetch.wait()
    for parity in range(2):
        me = lax.axis_index(OWNERS) if apart else 0
        found, _ = wave_rows(owners, chunks, k, holder_ref, waves, parity, me)
        table[parity] = found.astype(jnp.bfloat16)

    def take(n):
        for copy in copies(n):
            copy.wait()

    def fold(n, now):
        for level in range(levels):
            s = state[n, level].astype(jnp.float32)
            f = forcing[n, level].astype(jnp.float32)
            explicit = 0.7 * s + 0.5 * f + 0.3 * s / (1.0 + s * s)
            low, high = explicit[:, :half], explicit[:, half:]
            span = slice(level * lats, (level + 1) * lats)
            folded[now, 0, span, :] = (low + high).astype(jnp.bfloat16)
            folded[now, 1, span, :] = (low - high).astype(jnp.bfloat16)

    def transform(n, now):
        for parity in range(2):
            found = dot(table[parity], folded[now, parity], NT).astype(jnp.bfloat16)
            found = found.reshape(owners, rows // 2, levels * lats)
            mine = slice(parity * (rows // 2), (parity + 1) * (rows // 2))
            for level in range(levels):
                send[:, n * levels + level, mine, :] = found[
                    :, :, level * lats : (level + 1) * lats
                ]
        leaving(n).start()

    take(0)
    fold(0, 0)

    @pl.loop(0, (steps - 1) // 2)
    def _(j):
        take(2 * j + 1)
        take(2 * j + 2)
        transform(2 * j, 0)
        fold(2 * j + 1, 1)
        transform(2 * j + 1, 1)
        fold(2 * j + 2, 0)

    if steps % 2 == 0:
        take(steps - 1)
        fold(steps - 1, 1)
        transform(steps - 2, 0)
    transform(steps - 1, (steps - 1) % 2)

    @pl.loop(0, steps)
    def _(n):
        leaving(n).wait()


def run_analysis(owners, chunks, k, piece, state, forcing, holder, table, before):
    begin, end, apart = piece
    _, lats, lon_count = state.shape
    levels = end - begin
    slots = holder.shape[1]
    rows = 2 * slots // owners // chunks
    count = 2 if levels % 2 == 0 else 1
    steps = levels // count
    kept = pltpu.VMEM((steps, count, lats, lon_count), jnp.bfloat16)
    anywhere = pl.BlockSpec(memory_space=pl.ANY)
    return pl.pallas_call(
        functools.partial(analysis_kernel, owners, chunks, k, begin, apart),
        in_specs=[pl.BlockSpec(memory_space=pltpu.VMEM)] + [anywhere] * (3 + len(before)),
        out_specs=anywhere,
        out_shape=jax.ShapeDtypeStruct((owners, levels, rows, lats), jnp.bfloat16),
        scratch_shapes=[
            pltpu.VMEM(table.shape, jnp.bfloat16),
            pltpu.VMEM((2, slots // chunks, lon_count // 2), jnp.bfloat16),
            kept,
            kept,
            pltpu.VMEM((2, 2, count * lats, lon_count // 2), jnp.bfloat16),
            pltpu.VMEM((owners, levels, rows, lats), jnp.bfloat16),
            pltpu.SemaphoreType.DMA,
            pltpu.SemaphoreType.DMA((steps, 2)),
            pltpu.SemaphoreType.DMA((steps,)),
        ],
        compiler_params=pltpu.CompilerParams(vmem_limit_bytes=VMEM_BYTES),
        cost_estimate=pl.CostEstimate(
            flops=2 * levels * lats * lon_count * slots // chunks,
            bytes_accessed=6 * levels * lats * lon_count,
            transcendentals=0,
        ),
        name="longitude_analysis",
    )(holder, table, state, forcing, *before)


def synthesis_rows_kernel(owners, chunks, holder_ref, waves_ref, out_ref):
    for parity in range(2):
        for k in range(chunks):
            rows, zero = wave_rows(owners, chunks, k, holder_ref, waves_ref, parity)
            if parity == 0:
                count = zero.shape[0] // owners
                weight = (2.0 - zero).reshape(owners, count, 1)
                weight = jnp.concatenate([weight, weight], axis=1).reshape(-1, 1)
            else:
                weight = 2.0
            out_ref[parity, k] = (rows * weight).astype(jnp.bfloat16)


def synthesis_rows(owners, chunks, holder, table):
    shape = (2, chunks, holder.shape[1] // chunks, table.shape[3])
    return pl.pallas_call(
        functools.partial(synthesis_rows_kernel, owners, chunks),
        out_shape=jax.ShapeDtypeStruct(shape, jnp.bfloat16),
        compiler_params=pltpu.CompilerParams(vmem_limit_bytes=VMEM_BYTES),
        cost_estimate=pl.CostEstimate(
            flops=8 * 200 * holder.shape[1] * table.shape[2] * table.shape[3],
            bytes_accessed=4 * holder.shape[1] * table.shape[3],
            transcendentals=0,
        ),
        name="synthesis_rows",
    )(holder, table)


def pair_slots(first, waves, middle):
    late = (waves[first] >= middle).astype(jnp.int32)
    return first + late, first + 1 - late


def owner_blocks(owners, bands, levels, refs, pieces):
    groups = owners // bands
    blocks = 0
    for ref, (begin, end, apart) in zip(refs, pieces):
        rows = ref.shape[2] + TILE
        for r in range(ref.shape[0]):
            place = (blocks + r) % owners
            owner = lax.bitwise_xor(lax.axis_index(OWNERS), place) if apart else r
            start = (lax.rem(owner, groups) * levels + begin) * rows
            if apart:
                start = pl.multiple_of(start, TILE)
            yield ref.at[r], lax.div(owner, groups), pl.ds(start, (end - begin) * rows)
        blocks += ref.shape[0]


def column_kernel(owners, bands, k, pieces_in, pieces_out, waves_ref, *refs):
    received, refs = refs[: len(pieces_in)], refs[len(pieces_in) :]
    low_basis, high_basis, low_solver, high_solver = refs[:4]
    sends, (spread, back) = refs[-2 - len(pieces_out) : -2], refs[-2:]
    levels = pieces_in[-1][1]
    rows, lats = received[0].shape[-2:]
    per_chunk = rows // 4
    depth = owners // bands * levels
    total = low_basis.shape[1]
    middle = total // 2
    i = pl.program_id(0)

    @pl.when(i == 0)
    def _():
        for ref, band, span in owner_blocks(owners, bands, levels, received, pieces_in):
            part = ref[...].astype(jnp.float32)
            part = jnp.concatenate([part, part[:, :TILE]], axis=1)
            spread[band, span, :] = part.reshape(-1, lats)

    slots = pair_slots(2 * (k * per_chunk + i), waves_ref, middle)
    waves = [waves_ref[slot] for slot in slots]
    bases = [lax.rem(wave, 2) * (2 * per_chunk) + i for wave in waves]
    basis = [low_basis[0], high_basis[0]]
    solvers = [low_solver[0], high_solver[0]]
    lows = [0, middle]
    taken, coeffs, solved, grid = [], [], [], []
    for w in range(2):
        parts = [
            jnp.concatenate(
                [
                    spread[a, pl.ds(bases[w] + c * per_chunk, depth, stride=rows + TILE), :]
                    for a in range(bands)
                ],
                axis=1,
            )
            for c in range(2)
        ]
        taken.append(jnp.concatenate(parts, axis=0).astype(jnp.bfloat16))
    for w in range(2):
        found = dot(taken[w], basis[w])
        coeffs.append(
            jnp.concatenate([found[:depth], found[depth:]], axis=1).astype(jnp.bfloat16)
        )
    for w in range(2):
        found = dot(solvers[w], coeffs[w])
        count = total - lows[w]
        degree = lows[w] + lax.broadcasted_iota(jnp.int32, (depth, count), 1)
        parts = [
            jnp.where(degree >= waves[w], found[:, c * count : (c + 1) * count], 0.0)
            for c in range(2)
        ]
        solved.append(jnp.concatenate(parts, axis=0).astype(jnp.bfloat16))
    for w in range(2):
        grid.append(dot(solved[w], basis[w], NT))
    for w in range(2):
        for c in range(2):
            for a in range(bands):
                back[a, pl.ds(bases[w] + c * per_chunk, depth, stride=rows + TILE), :] = grid[w][
                    c * depth : (c + 1) * depth, a * lats : (a + 1) * lats
                ]

    @pl.when(i == pl.num_programs(0) - 1)
    def _():
        for ref, band, span in owner_blocks(owners, bands, levels, sends, pieces_out):
            part = back[band, span, :].reshape(ref.shape[0], rows + TILE, lats)
            ref[...] = part[:, :rows].astype(jnp.bfloat16)


def run_columns(k, owners, bands, pieces_in, pieces_out, waves, received, before, basis, solver):
    rows, lats = received[0].shape[-2:]
    levels = pieces_in[-1][1]
    depth = owners // bands * levels
    total = basis.shape[1]
    middle = total // 2
    steps = rows // 4
    first = lambda i: 2 * (k * steps + i)
    low = lambda i, waves_ref: (pair_slots(first(i), waves_ref, middle)[0], 0, 0)
    high = lambda i, waves_ref: (pair_slots(first(i), waves_ref, middle)[1], 0, 0)
    upper = lambda i, waves_ref: (pair_slots(first(i), waves_ref, middle)[1], 0, 1)
    whole = lambda shape: pl.BlockSpec(shape, lambda i, waves_ref: (0, 0, 0, 0))
    sizes = [(owners, end - begin, rows, lats) for begin, end, _ in pieces_out]
    scratch = pltpu.VMEM((bands, depth * (rows + TILE), lats), jnp.float32)
    return pl.pallas_call(
        functools.partial(column_kernel, owners, bands, k, pieces_in, pieces_out),
        grid_spec=pltpu.PrefetchScalarGridSpec(
            num_scalar_prefetch=1,
            grid=(steps,),
            in_specs=[whole(part.shape) for part in received]
            + [
                pl.BlockSpec((1, total, total), low),
                pl.BlockSpec((1, total, total - middle), upper),
                pl.BlockSpec((1, depth, depth), low),
                pl.BlockSpec((1, depth, depth), high),
            ]
            + [pl.BlockSpec(memory_space=pl.ANY)] * len(before),
            out_specs=[whole(size) for size in sizes],
            scratch_shapes=[scratch, scratch],
        ),
        out_shape=[jax.ShapeDtypeStruct(size, jnp.bfloat16) for size in sizes],
        compiler_params=pltpu.CompilerParams(vmem_limit_bytes=VMEM_BYTES),
        cost_estimate=pl.CostEstimate(
            flops=HINT * 6 * steps * 2 * depth * total * total,
            bytes_accessed=4 * bands * depth * rows * lats + 3 * steps * total * total,
            transcendentals=0,
        ),
        name="legendre_solve",
    )(waves, *received, basis, basis, solver, solver, *before)


def synthesis_kernel(owners, begin, pieces, *refs):
    parts, synth_ref, (out_hbm, kept, out, arrived, left) = (
        refs[: len(pieces)],
        refs[len(pieces)],
        refs[-5:],
    )
    steps, chunks, _, levels, rows, lats = kept.shape
    half = synth_ref.shape[-1]
    me = lax.axis_index(OWNERS)

    def copies(n, entire):
        for k, (part, (start, apart)) in enumerate(zip(parts, pieces)):
            span = pl.ds(begin - start + n * levels, levels)
            if apart and not entire:
                for r in range(owners):
                    place = kept.at[n, k, lax.bitwise_xor(me, r)]
                    yield pltpu.make_async_copy(part.at[r, span], place, arrived.at[n, k])
            else:
                yield pltpu.make_async_copy(part.at[:, span], kept.at[n, k], arrived.at[n, k])

    def leaving(n):
        mine = pl.ds(n * levels, levels)
        span = pl.ds(begin + n * levels, levels)
        return pltpu.make_async_copy(out.at[mine], out_hbm.at[span], left.at[n])

    @pl.loop(0, steps)
    def _(n):
        for copy in copies(n, False):
            copy.start()

    @pl.loop(0, steps)
    def _(i):
        for copy in copies(i, True):
            copy.wait()
        sums = []
        for parity in range(2):
            terms = []
            for k in range(chunks):
                found = kept[i, k, :, :, parity * (rows // 2) : (parity + 1) * (rows // 2), :]
                found = jnp.concatenate(
                    [found[:, n].reshape(owners * rows // 2, lats) for n in range(levels)], axis=1
                )
                terms.append(dot(found, synth_ref[parity, k], TN))
            sums.append(sum(terms[1:], terms[0]))
        for n in range(levels):
            even, odd = [found[n * lats : (n + 1) * lats] for found in sums]
            out[i * levels + n, :, :half] = (even + odd).astype(jnp.bfloat16)
            out[i * levels + n, :, half:] = (even - odd).astype(jnp.bfloat16)
        leaving(i).start()

    @pl.loop(0, steps)
    def _(n):
        leaving(n).wait()


def run_synthesis(begin, end, levels, pieces, parts, synth, before):
    owners, _, rows, lats = parts[0].shape
    lon_count = 2 * synth.shape[-1]
    chunks = len(pieces)
    count = 2 if (end - begin) % 2 == 0 else 1
    steps = (end - begin) // count
    given = [] if before is None else [before]
    anywhere = pl.BlockSpec(memory_space=pl.ANY)
    return pl.pallas_call(
        functools.partial(synthesis_kernel, owners, begin, pieces),
        in_specs=[anywhere] * len(parts)
        + [pl.BlockSpec(memory_space=pltpu.VMEM)]
        + [anywhere] * len(given),
        out_specs=anywhere,
        out_shape=jax.ShapeDtypeStruct((levels, lats, lon_count), jnp.bfloat16),
        scratch_shapes=[
            pltpu.VMEM((steps, chunks, owners, count, rows, lats), jnp.bfloat16),
            pltpu.VMEM((end - begin, lats, lon_count), jnp.bfloat16),
            pltpu.SemaphoreType.DMA((steps, chunks)),
            pltpu.SemaphoreType.DMA((steps,)),
        ],
        compiler_params=pltpu.CompilerParams(vmem_limit_bytes=VMEM_BYTES),
        cost_estimate=pl.CostEstimate(
            flops=(end - begin) * lats * lon_count * lon_count,
            bytes_accessed=4 * (end - begin) * lats * lon_count,
            transcendentals=0,
        ),
        input_output_aliases={len(parts) + 1: 0} if given else {},
        name="longitude_synthesis",
    )(*parts, synth, *given)


def exchange(part):
    owners, levels, rows, lats = part.shape
    flat = part.reshape(owners, levels * rows, lats)
    return lax.all_to_all(flat, OWNERS, 0, 0, tiled=True).reshape(part.shape)


def swap(part, bits):
    owners = part.shape[0]
    for bit in bits:
        halves = part.reshape((owners // 2 // bit, 2, bit) + part.shape[1:])
        given = lax.ppermute(halves[:, 1], OWNERS, [(o, o ^ bit) for o in range(owners)])
        part = jnp.stack([halves[:, 0], given], axis=1).reshape(part.shape)
    return halves[0, 0], given[0]


def chunked_shards(lat_bands, level_groups, chunks):
    owners = lat_bands * level_groups
    far, near = owners // 2, [2**n for n in range(int(math.log2(owners)) - 1)]

    def shards(
        thermal_state_grid,
        thermal_forcing,
        spherical_basis_table,
        implicit_solver_matrix,
        fourier_order_holder,
    ):
        levels = thermal_state_grid.shape[0]
        slots = spherical_basis_table.shape[0]
        table = jnp.asarray(longitude_waves(thermal_state_grid.shape[2]))
        holder = fourier_order_holder.reshape(1, -1)
        owner = lax.axis_index(OWNERS)
        waves = lax.dynamic_slice_in_dim(fourier_order_holder, owner * slots, slots)

        def analyse(k, piece, before):
            return run_analysis(
                owners, chunks, k, piece, thermal_state_grid, thermal_forcing, holder, table, before
            )

        def columns(k, pieces_in, pieces_out, received, before):
            return run_columns(
                k, owners, lat_bands, pieces_in, pieces_out, waves, received, before,
                spherical_basis_table, implicit_solver_matrix,
            )

        whole = [(0, levels, False)]
        cut = levels - levels * FEW // 34 // 2 * 2
        split = [(0, cut, False), (cut, levels, True)]
        first = exchange(analyse(0, split[0], []))
        main = analyse(1, split[0], [])
        early = swap(analyse(0, split[1], [main]), near + [far])
        late = analyse(1, split[1], [main])
        second = exchange(main)
        arriving = split[:1] + split[1:] * 2
        (solved,) = columns(0, arriving, whole, [first, *early], [])
        solved, late = lax.optimization_barrier((solved, late))
        late = swap(late, near + [far])
        first = exchange(solved)
        solved, aside = columns(1, arriving, split, [second, *late], [])
        solved, aside = lax.optimization_barrier((solved, aside))
        aside = jnp.concatenate(swap(aside, near + [far]))
        second = exchange(solved)
        synth = synthesis_rows(owners, chunks, holder, table)
        result = run_synthesis(
            cut, levels, levels, [(0, False), (cut, True)], [first, aside], synth, None
        )
        return run_synthesis(
            0, cut, levels, [(0, False), (0, False)], [first, second], synth, result
        )

    return shards


def solution(mesh):
    shape = mesh.shape
    bands, groups = shape["lat"], shape["lev"] * shape["sub"]

    def shards(state, forcing, basis, solver, holder):
        levels, lats, lon_count = state.shape
        pairs = basis.shape[0] // 2
        tiled = pairs % (CHUNKS * TILE) == 0 and levels * groups % TILE == 0
        tiled = tiled and bands > 1 and bands * groups == 2 ** int(math.log2(bands * groups))
        if tiled and levels % 2 == 0 and lats % 128 == 0 and lon_count == 2 * holder.shape[0]:
            body = chunked_shards(bands, groups, CHUNKS)
        else:
            body = general_shards(bands, groups)
        return body(state, forcing, basis, solver, holder)

    return jax.shard_map(
        shards,
        mesh=mesh,
        in_specs=(
            P(("members", "lev", "sub"), "lat", None),
            P(("members", "lev", "sub"), "lat", None),
            P(OWNERS, None, None),
            P(OWNERS, None, None),
            P(),
        ),
        out_specs=P(("members", "lev", "sub"), "lat", None),
        check_vma=False,
    )
```

```python
import functools
import math

import jax
import jax.numpy as jnp
import numpy as np
from jax import lax
from jax.experimental import pallas as pl
from jax.experimental.pallas import tpu as pltpu
from jax.sharding import PartitionSpec as P

OWNERS = ("lat", "lev", "sub")
CHUNKS = 2
HINT = 33
HEAD, EARLY, LATE, LAST = 6, 4, 6, 6


def raw_table(fourier_order_holder, lon_count):
    meridian_position = jnp.arange(lon_count, dtype=jnp.int32)
    phases = fourier_order_holder[:, None] * meridian_position[None, :] % lon_count
    angles = phases.astype(jnp.float32) * (2.0 * math.pi / lon_count)
    factor = 1.0 / math.sqrt(lon_count)
    stacked = jnp.stack([jnp.cos(angles), -jnp.sin(angles)], axis=1)
    return stacked.reshape(2 * fourier_order_holder.shape[0], lon_count) * factor


def general_shards(lat_bands, level_groups):
    def shards(
        thermal_state_grid,
        thermal_forcing,
        spherical_basis_table,
        implicit_solver_matrix,
        fourier_order_holder,
    ):
        levels, lats, lon_count = thermal_state_grid.shape
        slots, lat_total, wave_total = spherical_basis_table.shape
        owners = lat_bands * level_groups
        state = thermal_state_grid.astype(jnp.float32)
        explicit = (
            state
            + 0.5 * thermal_forcing.astype(jnp.float32)
            - 0.3 * state * state * state / (1.0 + state * state)
        ).astype(jnp.bfloat16)
        raw = raw_table(fourier_order_holder, lon_count)
        analysis = raw.astype(jnp.bfloat16)
        weights = jnp.where(fourier_order_holder == 0, 1.0, 2.0).astype(jnp.float32)
        synthesis = (raw * jnp.repeat(weights, 2)[:, None]).astype(jnp.bfloat16)
        spectral = jnp.einsum(
            "sj,lxj->slx", analysis, explicit, preferred_element_type=jnp.float32
        ).astype(jnp.bfloat16)
        spectral = spectral.reshape(owners, 2 * slots * levels, lats)
        spectral = lax.all_to_all(spectral, OWNERS, 0, 0, tiled=True)
        spectral = spectral.reshape(lat_bands, level_groups, slots, 2, levels, lats)
        spectral = spectral.transpose(2, 3, 1, 4, 0, 5)
        spectral = spectral.reshape(slots, 2 * level_groups * levels, lat_total)
        coeffs = jnp.einsum(
            "srx,sxn->srn", spectral, spherical_basis_table, preferred_element_type=jnp.float32
        ).astype(jnp.bfloat16)
        coeffs = coeffs.reshape(slots, 2, level_groups * levels, wave_total)
        solved = jnp.einsum(
            "skl,scln->sckn", implicit_solver_matrix, coeffs, preferred_element_type=jnp.float32
        )
        owner = lax.axis_index(OWNERS)
        waves = lax.dynamic_slice_in_dim(fourier_order_holder, owner * slots, slots)
        live = jnp.arange(wave_total, dtype=jnp.int32)[None, :] >= waves[:, None]
        solved = jnp.where(live[:, None, None, :], solved, 0.0).astype(jnp.bfloat16)
        solved = solved.reshape(slots, 2 * level_groups * levels, wave_total)
        back = jnp.einsum(
            "srn,sxn->srx", solved, spherical_basis_table, preferred_element_type=jnp.float32
        ).astype(jnp.bfloat16)
        back = back.reshape(slots, 2, level_groups, levels, lat_bands, lats)
        back = back.transpose(4, 2, 0, 1, 3, 5).reshape(owners, 2 * slots * levels, lats)
        back = lax.all_to_all(back, OWNERS, 0, 0, tiled=True)
        back = back.reshape(2 * slots * owners, levels, lats)
        return jnp.einsum(
            "slx,sj->lxj", back, synthesis, preferred_element_type=jnp.float32
        ).astype(jnp.bfloat16)

    return shards


TILE = 8
VMEM_BYTES = 60 * 1024 * 1024
NT = (((1,), (1,)), ((), ()))
TN = (((0,), (0,)), ((), ()))


def dot(a, b, dims=(((1,), (0,)), ((), ()))):
    return lax.dot_general(a, b, dims, preferred_element_type=jnp.float32)


def longitude_waves(lon_count):
    half = lon_count // 2
    waves = np.arange(half).reshape(half // 2, 2).T
    phases = waves[:, :, None] * np.arange(half)[None, None, :] % lon_count
    angles = phases.astype(np.float32) * np.float32(2.0 * math.pi / lon_count)
    table = np.stack([np.cos(angles), -np.sin(angles)], axis=1) / math.sqrt(lon_count)
    return table.astype(jnp.bfloat16)


def wave_rows(owners, chunks, k, holder_ref, waves_ref, parity, me=0):
    slots = holder_ref.shape[1]
    per_chunk = slots // 2 // owners // chunks
    wave = 2 * lax.broadcasted_iota(jnp.int32, (waves_ref.shape[2], slots), 0) + parity
    held = (holder_ref[...] == wave).astype(jnp.float32).astype(jnp.bfloat16)
    row = lax.broadcasted_iota(jnp.int32, (owners * per_chunk, slots), 0)
    owner = lax.bitwise_xor(lax.div(row, per_chunk), me)
    pair = (owner * chunks + k) * per_chunk + lax.rem(row, per_chunk)
    slot = lax.broadcasted_iota(jnp.int32, (owners * per_chunk, slots), 1)
    chosen = (lax.div(slot, 2) == pair).astype(jnp.float32).astype(jnp.bfloat16)
    pick = dot(chosen, held, NT)
    picked = pick.astype(jnp.bfloat16)
    parts = [
        dot(picked, waves_ref[parity, c]).reshape(owners, per_chunk, waves_ref.shape[3])
        for c in range(2)
    ]
    rows = jnp.concatenate(parts, axis=1).reshape(2 * per_chunk * owners, waves_ref.shape[3])
    return rows, pick[:, 0:1]


def analysis_kernel(
    owners, chunks, k, begin, apart, holder_ref, waves_hbm, state_hbm, forcing_hbm, *refs
):
    send_hbm, waves, table, state, forcing, folded, send, ready, arrived, left = refs[-10:]
    steps, levels, lats, lon_count = state.shape
    half = lon_count // 2
    rows = send.shape[2]

    def copies(n):
        span = pl.ds(begin + n * levels, levels)
        return (
            pltpu.make_async_copy(state_hbm.at[span], state.at[n], arrived.at[n, 0]),
            pltpu.make_async_copy(forcing_hbm.at[span], forcing.at[n], arrived.at[n, 1]),
        )

    def leaving(n):
        span = pl.ds(n * levels, levels)
        return pltpu.make_async_copy(send.at[:, span], send_hbm.at[:, span], left.at[n])

    fetch = pltpu.make_async_copy(waves_hbm, waves, ready)
    fetch.start()

    @pl.loop(0, steps)
    def _(n):
        for copy in copies(n):
            copy.start()

    fetch.wait()
    for parity in range(2):
        me = lax.axis_index(OWNERS) if apart else 0
        found, _ = wave_rows(owners, chunks, k, holder_ref, waves, parity, me)
        table[parity] = found.astype(jnp.bfloat16)

    def take(n):
        for copy in copies(n):
            copy.wait()

    def fold(n, now):
        for level in range(levels):
            s = state[n, level].astype(jnp.float32)
            f = forcing[n, level].astype(jnp.float32)
            explicit = 0.7 * s + 0.5 * f + 0.3 * s / (1.0 + s * s)
            low, high = explicit[:, :half], explicit[:, half:]
            span = slice(level * lats, (level + 1) * lats)
            folded[now, 0, span, :] = (low + high).astype(jnp.bfloat16)
            folded[now, 1, span, :] = (low - high).astype(jnp.bfloat16)

    def transform(n, now):
        for parity in range(2):
            found = dot(table[parity], folded[now, parity], NT).astype(jnp.bfloat16)
            found = found.reshape(owners, rows // 2, levels * lats)
            mine = slice(parity * (rows // 2), (parity + 1) * (rows // 2))
            for level in range(levels):
                send[:, n * levels + level, mine, :] = found[
                    :, :, level * lats : (level + 1) * lats
                ]
        leaving(n).start()

    take(0)
    fold(0, 0)

    @pl.loop(0, (steps - 1) // 2)
    def _(j):
        take(2 * j + 1)
        take(2 * j + 2)
        transform(2 * j, 0)
        fold(2 * j + 1, 1)
        transform(2 * j + 1, 1)
        fold(2 * j + 2, 0)

    if steps % 2 == 0:
        take(steps - 1)
        fold(steps - 1, 1)
        transform(steps - 2, 0)
    transform(steps - 1, (steps - 1) % 2)

    @pl.loop(0, steps)
    def _(n):
        leaving(n).wait()


def run_analysis(owners, chunks, k, piece, state, forcing, holder, table, before):
    begin, end, apart = piece
    _, lats, lon_count = state.shape
    levels = end - begin
    slots = holder.shape[1]
    rows = 2 * slots // owners // chunks
    count = 2 if levels % 2 == 0 else 1
    steps = levels // count
    kept = pltpu.VMEM((steps, count, lats, lon_count), jnp.bfloat16)
    anywhere = pl.BlockSpec(memory_space=pl.ANY)
    return pl.pallas_call(
        functools.partial(analysis_kernel, owners, chunks, k, begin, apart),
        in_specs=[pl.BlockSpec(memory_space=pltpu.VMEM)] + [anywhere] * (3 + len(before)),
        out_specs=anywhere,
        out_shape=jax.ShapeDtypeStruct((owners, levels, rows, lats), jnp.bfloat16),
        scratch_shapes=[
            pltpu.VMEM(table.shape, jnp.bfloat16),
            pltpu.VMEM((2, slots // chunks, lon_count // 2), jnp.bfloat16),
            kept,
            kept,
            pltpu.VMEM((2, 2, count * lats, lon_count // 2), jnp.bfloat16),
            pltpu.VMEM((owners, levels, rows, lats), jnp.bfloat16),
            pltpu.SemaphoreType.DMA,
            pltpu.SemaphoreType.DMA((steps, 2)),
            pltpu.SemaphoreType.DMA((steps,)),
        ],
        compiler_params=pltpu.CompilerParams(vmem_limit_bytes=VMEM_BYTES),
        cost_estimate=pl.CostEstimate(
            flops=30 * 2 * levels * lats * lon_count * slots // chunks,
            bytes_accessed=6 * levels * lats * lon_count,
            transcendentals=0,
        ),
        name="longitude_analysis",
    )(holder, table, state, forcing, *before)


def synthesis_rows_kernel(owners, chunks, holder_ref, waves_ref, out_ref):
    for parity in range(2):
        for k in range(chunks):
            rows, zero = wave_rows(owners, chunks, k, holder_ref, waves_ref, parity)
            if parity == 0:
                count = zero.shape[0] // owners
                weight = (2.0 - zero).reshape(owners, count, 1)
                weight = jnp.concatenate([weight, weight], axis=1).reshape(-1, 1)
            else:
                weight = 2.0
            out_ref[parity, k] = (rows * weight).astype(jnp.bfloat16)


def synthesis_rows(owners, chunks, holder, table):
    shape = (2, chunks, holder.shape[1] // chunks, table.shape[3])
    return pl.pallas_call(
        functools.partial(synthesis_rows_kernel, owners, chunks),
        out_shape=jax.ShapeDtypeStruct(shape, jnp.bfloat16),
        compiler_params=pltpu.CompilerParams(vmem_limit_bytes=VMEM_BYTES),
        cost_estimate=pl.CostEstimate(
            flops=8 * 200 * holder.shape[1] * table.shape[2] * table.shape[3],
            bytes_accessed=4 * holder.shape[1] * table.shape[3],
            transcendentals=0,
        ),
        name="synthesis_rows",
    )(holder, table)


def pair_slots(first, waves, middle):
    late = (waves[first] >= middle).astype(jnp.int32)
    return first + late, first + 1 - late


def owner_blocks(owners, bands, levels, refs, pieces):
    groups = owners // bands
    blocks = 0
    for ref, (begin, end, apart) in zip(refs, pieces):
        rows = ref.shape[2] + TILE
        for r in range(ref.shape[0]):
            place = (blocks + r) % owners
            owner = lax.bitwise_xor(lax.axis_index(OWNERS), place) if apart else r
            start = (lax.rem(owner, groups) * levels + begin) * rows
            if apart:
                start = pl.multiple_of(start, TILE)
            yield ref.at[r], lax.div(owner, groups), pl.ds(start, (end - begin) * rows)
        blocks += ref.shape[0]


def column_kernel(owners, bands, k, pieces_in, pieces_out, waves_ref, *refs):
    received, refs = refs[: len(pieces_in)], refs[len(pieces_in) :]
    low_basis, high_basis, low_solver, high_solver = refs[:4]
    sends, (spread, back) = refs[-2 - len(pieces_out) : -2], refs[-2:]
    levels = pieces_in[-1][1]
    rows, lats = received[0].shape[-2:]
    per_chunk = rows // 4
    depth = owners // bands * levels
    total = low_basis.shape[1]
    middle = total // 2
    i = pl.program_id(0)

    @pl.when(i == 0)
    def _():
        for ref, band, span in owner_blocks(owners, bands, levels, received, pieces_in):
            part = ref[...].astype(jnp.float32)
            part = jnp.concatenate([part, part[:, :TILE]], axis=1)
            spread[band, span, :] = part.reshape(-1, lats)

    slots = pair_slots(2 * (k * per_chunk + i), waves_ref, middle)
    waves = [waves_ref[slot] for slot in slots]
    bases = [lax.rem(wave, 2) * (2 * per_chunk) + i for wave in waves]
    basis = [low_basis[0], high_basis[0]]
    solvers = [low_solver[0], high_solver[0]]
    lows = [0, middle]
    taken, coeffs, solved, grid = [], [], [], []
    for w in range(2):
        parts = [
            jnp.concatenate(
                [
                    spread[a, pl.ds(bases[w] + c * per_chunk, depth, stride=rows + TILE), :]
                    for a in range(bands)
                ],
                axis=1,
            )
            for c in range(2)
        ]
        taken.append(jnp.concatenate(parts, axis=0).astype(jnp.bfloat16))
    for w in range(2):
        found = dot(taken[w], basis[w])
        coeffs.append(
            jnp.concatenate([found[:depth], found[depth:]], axis=1).astype(jnp.bfloat16)
        )
    for w in range(2):
        found = dot(solvers[w], coeffs[w])
        count = total - lows[w]
        degree = lows[w] + lax.broadcasted_iota(jnp.int32, (depth, count), 1)
        parts = [
            jnp.where(degree >= waves[w], found[:, c * count : (c + 1) * count], 0.0)
            for c in range(2)
        ]
        solved.append(jnp.concatenate(parts, axis=0).astype(jnp.bfloat16))
    for w in range(2):
        grid.append(dot(solved[w], basis[w], NT))
    for w in range(2):
        for c in range(2):
            for a in range(bands):
                back[a, pl.ds(bases[w] + c * per_chunk, depth, stride=rows + TILE), :] = grid[w][
                    c * depth : (c + 1) * depth, a * lats : (a + 1) * lats
                ]

    @pl.when(i == pl.num_programs(0) - 1)
    def _():
        for ref, band, span in owner_blocks(owners, bands, levels, sends, pieces_out):
            part = back[band, span, :].reshape(ref.shape[0], rows + TILE, lats)
            ref[...] = part[:, :rows].astype(jnp.bfloat16)


def run_columns(k, owners, bands, pieces_in, pieces_out, waves, received, before, basis, solver):
    rows, lats = received[0].shape[-2:]
    levels = pieces_in[-1][1]
    depth = owners // bands * levels
    total = basis.shape[1]
    middle = total // 2
    steps = rows // 4
    first = lambda i: 2 * (k * steps + i)
    low = lambda i, waves_ref: (pair_slots(first(i), waves_ref, middle)[0], 0, 0)
    high = lambda i, waves_ref: (pair_slots(first(i), waves_ref, middle)[1], 0, 0)
    upper = lambda i, waves_ref: (pair_slots(first(i), waves_ref, middle)[1], 0, 1)
    whole = lambda shape: pl.BlockSpec(shape, lambda i, waves_ref: (0, 0, 0, 0))
    sizes = [(owners, end - begin, rows, lats) for begin, end, _ in pieces_out]
    scratch = pltpu.VMEM((bands, depth * (rows + TILE), lats), jnp.float32)
    return pl.pallas_call(
        functools.partial(column_kernel, owners, bands, k, pieces_in, pieces_out),
        grid_spec=pltpu.PrefetchScalarGridSpec(
            num_scalar_prefetch=1,
            grid=(steps,),
            in_specs=[whole(part.shape) for part in received]
            + [
                pl.BlockSpec((1, total, total), low),
                pl.BlockSpec((1, total, total - middle), upper),
                pl.BlockSpec((1, depth, depth), low),
                pl.BlockSpec((1, depth, depth), high),
            ]
            + [pl.BlockSpec(memory_space=pl.ANY)] * len(before),
            out_specs=[whole(size) for size in sizes],
            scratch_shapes=[scratch, scratch],
        ),
        out_shape=[jax.ShapeDtypeStruct(size, jnp.bfloat16) for size in sizes],
        compiler_params=pltpu.CompilerParams(vmem_limit_bytes=VMEM_BYTES),
        cost_estimate=pl.CostEstimate(
            flops=HINT * 6 * steps * 2 * depth * total * total,
            bytes_accessed=4 * bands * depth * rows * lats + 3 * steps * total * total,
            transcendentals=0,
        ),
        name="legendre_solve",
    )(waves, *received, basis, basis, solver, solver, *before)


def synthesis_kernel(owners, begin, pieces, *refs):
    parts, synth_ref, (out_hbm, kept, out, arrived, left) = (
        refs[: len(pieces)],
        refs[len(pieces)],
        refs[-5:],
    )
    steps, chunks, _, levels, rows, lats = kept.shape
    half = synth_ref.shape[-1]
    me = lax.axis_index(OWNERS)

    def copies(n, entire):
        for k, (part, (start, apart)) in enumerate(zip(parts, pieces)):
            span = pl.ds(begin - start + n * levels, levels)
            if apart and not entire:
                for r in range(owners):
                    place = kept.at[n, k, lax.bitwise_xor(me, r)]
                    yield pltpu.make_async_copy(part.at[r, span], place, arrived.at[n, k])
            else:
                yield pltpu.make_async_copy(part.at[:, span], kept.at[n, k], arrived.at[n, k])

    def leaving(n):
        mine = pl.ds(n * levels, levels)
        span = pl.ds(begin + n * levels, levels)
        return pltpu.make_async_copy(out.at[mine], out_hbm.at[span], left.at[n])

    @pl.loop(0, steps)
    def _(n):
        for copy in copies(n, False):
            copy.start()

    @pl.loop(0, steps)
    def _(i):
        for copy in copies(i, True):
            copy.wait()
        sums = []
        for parity in range(2):
            terms = []
            for k in range(chunks):
                found = kept[i, k, :, :, parity * (rows // 2) : (parity + 1) * (rows // 2), :]
                found = jnp.concatenate(
                    [found[:, n].reshape(owners * rows // 2, lats) for n in range(levels)], axis=1
                )
                terms.append(dot(found, synth_ref[parity, k], TN))
            sums.append(sum(terms[1:], terms[0]))
        for n in range(levels):
            even, odd = [found[n * lats : (n + 1) * lats] for found in sums]
            out[i * levels + n, :, :half] = (even + odd).astype(jnp.bfloat16)
            out[i * levels + n, :, half:] = (even - odd).astype(jnp.bfloat16)
        leaving(i).start()

    @pl.loop(0, steps)
    def _(n):
        leaving(n).wait()


def run_synthesis(begin, end, levels, pieces, parts, synth, before):
    owners, _, rows, lats = parts[0].shape
    lon_count = 2 * synth.shape[-1]
    chunks = len(pieces)
    count = 2 if (end - begin) % 2 == 0 else 1
    steps = (end - begin) // count
    given = [] if before is None else [before]
    anywhere = pl.BlockSpec(memory_space=pl.ANY)
    return pl.pallas_call(
        functools.partial(synthesis_kernel, owners, begin, pieces),
        in_specs=[anywhere] * len(parts)
        + [pl.BlockSpec(memory_space=pltpu.VMEM)]
        + [anywhere] * len(given),
        out_specs=anywhere,
        out_shape=jax.ShapeDtypeStruct((levels, lats, lon_count), jnp.bfloat16),
        scratch_shapes=[
            pltpu.VMEM((steps, chunks, owners, count, rows, lats), jnp.bfloat16),
            pltpu.VMEM((end - begin, lats, lon_count), jnp.bfloat16),
            pltpu.SemaphoreType.DMA((steps, chunks)),
            pltpu.SemaphoreType.DMA((steps,)),
        ],
        compiler_params=pltpu.CompilerParams(vmem_limit_bytes=VMEM_BYTES),
        cost_estimate=pl.CostEstimate(
            flops=(end - begin) * lats * lon_count * lon_count,
            bytes_accessed=4 * (end - begin) * lats * lon_count,
            transcendentals=0,
        ),
        input_output_aliases={len(parts) + 1: 0} if given else {},
        name="longitude_synthesis",
    )(*parts, synth, *given)


def exchange(part):
    owners, levels, rows, lats = part.shape
    flat = part.reshape(owners, levels * rows, lats)
    return lax.all_to_all(flat, OWNERS, 0, 0, tiled=True).reshape(part.shape)


def give(part, bit):
    owners = part.shape[0]
    halves = part.reshape((owners // 2 // bit, 2, bit) + part.shape[1:])
    given = lax.ppermute(halves[:, 1], OWNERS, [(o, o ^ bit) for o in range(owners)])
    return halves[:, 0], given


def swap(part, bits):
    for bit in bits:
        part = jnp.stack(give(part, bit), axis=1).reshape(part.shape)
    return part


def chunked_shards(lat_bands, level_groups, chunks):
    owners = lat_bands * level_groups
    far, near = owners // 2, [2**n for n in range(int(math.log2(owners)) - 1)]

    def shards(
        thermal_state_grid,
        thermal_forcing,
        spherical_basis_table,
        implicit_solver_matrix,
        fourier_order_holder,
    ):
        levels = thermal_state_grid.shape[0]
        slots = spherical_basis_table.shape[0]
        table = jnp.asarray(longitude_waves(thermal_state_grid.shape[2]))
        holder = fourier_order_holder.reshape(1, -1)
        owner = lax.axis_index(OWNERS)
        waves = lax.dynamic_slice_in_dim(fourier_order_holder, owner * slots, slots)

        def analyse(k, piece, before):
            return run_analysis(
                owners, chunks, k, piece, thermal_state_grid, thermal_forcing, holder, table, before
            )

        def columns(k, pieces_in, pieces_out, received, before):
            return run_columns(
                k, owners, lat_bands, pieces_in, pieces_out, waves, received, before,
                spherical_basis_table, implicit_solver_matrix,
            )

        def share(count):
            return levels * count // 34 // 2 * 2

        def across(part):
            return [half[0] for half in give(part, far)]

        whole = [(0, levels, False)]
        head_cut, last_cut = levels - share(HEAD), levels - share(LAST)
        late_cut = levels - share(LATE)
        early_cut = late_cut - share(EARLY)
        head = analyse(0, (head_cut, levels, True), [])
        main = analyse(0, (0, head_cut, False), [head])
        head = swap(head, [far])
        first = exchange(main)
        main = analyse(1, (0, early_cut, False), [])
        rest = analyse(1, (early_cut, levels, True), [main])
        early, late = rest[:, : late_cut - early_cut], rest[:, late_cut - early_cut :]
        both = swap(jnp.concatenate([head, early], axis=1), near)
        head, early = both[:, : levels - head_cut], across(both[:, levels - head_cut :])
        second = exchange(main)
        pieces = [(0, head_cut, False), (head_cut, levels, True)]
        (solved,) = columns(0, pieces, whole, [first, head], early[1:])
        solved, late = lax.optimization_barrier((solved, late))
        late = across(swap(late, near))
        first = exchange(solved)
        pieces = [(0, early_cut, False)]
        pieces += [(early_cut, late_cut, True)] * 2 + [(late_cut, levels, True)] * 2
        split = [(0, last_cut, False), (last_cut, levels, True)]
        solved, aside = columns(1, pieces, split, [second, *early, *late], [])
        solved, aside = lax.optimization_barrier((solved, aside))
        aside = jnp.concatenate(across(swap(aside, near)))
        second = exchange(solved)
        synth = synthesis_rows(owners, chunks, holder, table)
        result = run_synthesis(
            last_cut, levels, levels, [(0, False), (last_cut, True)], [first, aside], synth, None
        )
        return run_synthesis(
            0, last_cut, levels, [(0, False), (0, False)], [first, second], synth, result
        )

    return shards


def solution(mesh):
    shape = mesh.shape
    bands, groups = shape["lat"], shape["lev"] * shape["sub"]

    def shards(state, forcing, basis, solver, holder):
        levels, lats, lon_count = state.shape
        pairs = basis.shape[0] // 2
        tiled = pairs % (CHUNKS * TILE) == 0 and levels * groups % TILE == 0
        tiled = tiled and bands > 1 and bands * groups == 2 ** int(math.log2(bands * groups))
        if tiled and levels % 2 == 0 and lats % 128 == 0 and lon_count == 2 * holder.shape[0]:
            body = chunked_shards(bands, groups, CHUNKS)
        else:
            body = general_shards(bands, groups)
        return body(state, forcing, basis, solver, holder)

    return jax.shard_map(
        shards,
        mesh=mesh,
        in_specs=(
            P(("members", "lev", "sub"), "lat", None),
            P(("members", "lev", "sub"), "lat", None),
            P(OWNERS, None, None),
            P(OWNERS, None, None),
            P(),
        ),
        out_specs=P(("members", "lev", "sub"), "lat", None),
        check_vma=False,
    )
```

```python
import functools
import math

import jax
import jax.numpy as jnp
import numpy as np
from jax import lax
from jax.experimental import pallas as pl
from jax.experimental.pallas import tpu as pltpu
from jax.sharding import PartitionSpec as P

OWNERS = ("lat", "lev", "sub")
CHUNKS = 2
HINT = 33
HEAD, EARLY, LATE, LAST = 6, 4, 6, 6


def raw_table(fourier_order_holder, lon_count):
    meridian_position = jnp.arange(lon_count, dtype=jnp.int32)
    phases = fourier_order_holder[:, None] * meridian_position[None, :] % lon_count
    angles = phases.astype(jnp.float32) * (2.0 * math.pi / lon_count)
    factor = 1.0 / math.sqrt(lon_count)
    stacked = jnp.stack([jnp.cos(angles), -jnp.sin(angles)], axis=1)
    return stacked.reshape(2 * fourier_order_holder.shape[0], lon_count) * factor


def general_shards(lat_bands, level_groups):
    def shards(
        thermal_state_grid,
        thermal_forcing,
        spherical_basis_table,
        implicit_solver_matrix,
        fourier_order_holder,
    ):
        levels, lats, lon_count = thermal_state_grid.shape
        slots, lat_total, wave_total = spherical_basis_table.shape
        owners = lat_bands * level_groups
        state = thermal_state_grid.astype(jnp.float32)
        explicit = (
            state
            + 0.5 * thermal_forcing.astype(jnp.float32)
            - 0.3 * state * state * state / (1.0 + state * state)
        ).astype(jnp.bfloat16)
        raw = raw_table(fourier_order_holder, lon_count)
        analysis = raw.astype(jnp.bfloat16)
        weights = jnp.where(fourier_order_holder == 0, 1.0, 2.0).astype(jnp.float32)
        synthesis = (raw * jnp.repeat(weights, 2)[:, None]).astype(jnp.bfloat16)
        spectral = jnp.einsum(
            "sj,lxj->slx", analysis, explicit, preferred_element_type=jnp.float32
        ).astype(jnp.bfloat16)
        spectral = spectral.reshape(owners, 2 * slots * levels, lats)
        spectral = lax.all_to_all(spectral, OWNERS, 0, 0, tiled=True)
        spectral = spectral.reshape(lat_bands, level_groups, slots, 2, levels, lats)
        spectral = spectral.transpose(2, 3, 1, 4, 0, 5)
        spectral = spectral.reshape(slots, 2 * level_groups * levels, lat_total)
        coeffs = jnp.einsum(
            "srx,sxn->srn", spectral, spherical_basis_table, preferred_element_type=jnp.float32
        ).astype(jnp.bfloat16)
        coeffs = coeffs.reshape(slots, 2, level_groups * levels, wave_total)
        solved = jnp.einsum(
            "skl,scln->sckn", implicit_solver_matrix, coeffs, preferred_element_type=jnp.float32
        )
        owner = lax.axis_index(OWNERS)
        waves = lax.dynamic_slice_in_dim(fourier_order_holder, owner * slots, slots)
        live = jnp.arange(wave_total, dtype=jnp.int32)[None, :] >= waves[:, None]
        solved = jnp.where(live[:, None, None, :], solved, 0.0).astype(jnp.bfloat16)
        solved = solved.reshape(slots, 2 * level_groups * levels, wave_total)
        back = jnp.einsum(
            "srn,sxn->srx", solved, spherical_basis_table, preferred_element_type=jnp.float32
        ).astype(jnp.bfloat16)
        back = back.reshape(slots, 2, level_groups, levels, lat_bands, lats)
        back = back.transpose(4, 2, 0, 1, 3, 5).reshape(owners, 2 * slots * levels, lats)
        back = lax.all_to_all(back, OWNERS, 0, 0, tiled=True)
        back = back.reshape(2 * slots * owners, levels, lats)
        return jnp.einsum(
            "slx,sj->lxj", back, synthesis, preferred_element_type=jnp.float32
        ).astype(jnp.bfloat16)

    return shards


TILE = 8
VMEM_BYTES = 60 * 1024 * 1024
NT = (((1,), (1,)), ((), ()))
TN = (((0,), (0,)), ((), ()))


def dot(a, b, dims=(((1,), (0,)), ((), ()))):
    return lax.dot_general(a, b, dims, preferred_element_type=jnp.float32)


def longitude_waves(lon_count):
    half = lon_count // 2
    waves = np.arange(half).reshape(half // 2, 2).T
    phases = waves[:, :, None] * np.arange(half)[None, None, :] % lon_count
    angles = phases.astype(np.float32) * np.float32(2.0 * math.pi / lon_count)
    table = np.stack([np.cos(angles), -np.sin(angles)], axis=1) / math.sqrt(lon_count)
    return table.astype(jnp.bfloat16)


def wave_rows(owners, chunks, k, holder_ref, waves_ref, parity, me=0):
    slots = holder_ref.shape[1]
    per_chunk = slots // 2 // owners // chunks
    wave = 2 * lax.broadcasted_iota(jnp.int32, (waves_ref.shape[2], slots), 0) + parity
    held = (holder_ref[...] == wave).astype(jnp.float32).astype(jnp.bfloat16)
    row = lax.broadcasted_iota(jnp.int32, (owners * per_chunk, slots), 0)
    owner = lax.bitwise_xor(lax.div(row, per_chunk), me)
    pair = (owner * chunks + k) * per_chunk + lax.rem(row, per_chunk)
    slot = lax.broadcasted_iota(jnp.int32, (owners * per_chunk, slots), 1)
    chosen = (lax.div(slot, 2) == pair).astype(jnp.float32).astype(jnp.bfloat16)
    pick = dot(chosen, held, NT)
    picked = pick.astype(jnp.bfloat16)
    parts = [
        dot(picked, waves_ref[parity, c]).reshape(owners, per_chunk, waves_ref.shape[3])
        for c in range(2)
    ]
    rows = jnp.concatenate(parts, axis=1).reshape(2 * per_chunk * owners, waves_ref.shape[3])
    return rows, pick[:, 0:1]


def analysis_kernel(
    owners, chunks, k, begin, apart, holder_ref, waves_hbm, state_hbm, forcing_hbm, *refs
):
    send_hbm, waves, table, state, forcing, folded, send, ready, arrived, left = refs[-10:]
    steps, levels, lats, lon_count = state.shape
    half = lon_count // 2
    rows = send.shape[2]

    def copies(n):
        span = pl.ds(begin + n * levels, levels)
        return (
            pltpu.make_async_copy(state_hbm.at[span], state.at[n], arrived.at[n, 0]),
            pltpu.make_async_copy(forcing_hbm.at[span], forcing.at[n], arrived.at[n, 1]),
        )

    def leaving(n):
        span = pl.ds(n * levels, levels)
        return pltpu.make_async_copy(send.at[:, span], send_hbm.at[:, span], left.at[n])

    fetch = pltpu.make_async_copy(waves_hbm, waves, ready)
    fetch.start()

    @pl.loop(0, steps)
    def _(n):
        for copy in copies(n):
            copy.start()

    fetch.wait()
    for parity in range(2):
        me = lax.axis_index(OWNERS) if apart else 0
        found, _ = wave_rows(owners, chunks, k, holder_ref, waves, parity, me)
        table[parity] = found.astype(jnp.bfloat16)

    def take(n):
        for copy in copies(n):
            copy.wait()

    def fold(n, now):
        for level in range(levels):
            s = state[n, level].astype(jnp.float32)
            f = forcing[n, level].astype(jnp.float32)
            explicit = 0.7 * s + 0.5 * f + 0.3 * s / (1.0 + s * s)
            low, high = explicit[:, :half], explicit[:, half:]
            span = slice(level * lats, (level + 1) * lats)
            folded[now, 0, span, :] = (low + high).astype(jnp.bfloat16)
            folded[now, 1, span, :] = (low - high).astype(jnp.bfloat16)

    def transform(n, now):
        for parity in range(2):
            found = dot(table[parity], folded[now, parity], NT).astype(jnp.bfloat16)
            found = found.reshape(owners, rows // 2, levels * lats)
            mine = slice(parity * (rows // 2), (parity + 1) * (rows // 2))
            for level in range(levels):
                send[:, n * levels + level, mine, :] = found[
                    :, :, level * lats : (level + 1) * lats
                ]
        leaving(n).start()

    take(0)
    fold(0, 0)

    @pl.loop(0, (steps - 1) // 2)
    def _(j):
        take(2 * j + 1)
        take(2 * j + 2)
        transform(2 * j, 0)
        fold(2 * j + 1, 1)
        transform(2 * j + 1, 1)
        fold(2 * j + 2, 0)

    if steps % 2 == 0:
        take(steps - 1)
        fold(steps - 1, 1)
        transform(steps - 2, 0)
    transform(steps - 1, (steps - 1) % 2)

    @pl.loop(0, steps)
    def _(n):
        leaving(n).wait()


def run_analysis(owners, chunks, k, piece, state, forcing, holder, table, before):
    begin, end, apart = piece
    _, lats, lon_count = state.shape
    levels = end - begin
    slots = holder.shape[1]
    rows = 2 * slots // owners // chunks
    count = 2 if levels % 2 == 0 else 1
    steps = levels // count
    kept = pltpu.VMEM((steps, count, lats, lon_count), jnp.bfloat16)
    anywhere = pl.BlockSpec(memory_space=pl.ANY)
    return pl.pallas_call(
        functools.partial(analysis_kernel, owners, chunks, k, begin, apart),
        in_specs=[pl.BlockSpec(memory_space=pltpu.VMEM)] + [anywhere] * (3 + len(before)),
        out_specs=anywhere,
        out_shape=jax.ShapeDtypeStruct((owners, levels, rows, lats), jnp.bfloat16),
        scratch_shapes=[
            pltpu.VMEM(table.shape, jnp.bfloat16),
            pltpu.VMEM((2, slots // chunks, lon_count // 2), jnp.bfloat16),
            kept,
            kept,
            pltpu.VMEM((2, 2, count * lats, lon_count // 2), jnp.bfloat16),
            pltpu.VMEM((owners, levels, rows, lats), jnp.bfloat16),
            pltpu.SemaphoreType.DMA,
            pltpu.SemaphoreType.DMA((steps, 2)),
            pltpu.SemaphoreType.DMA((steps,)),
        ],
        compiler_params=pltpu.CompilerParams(vmem_limit_bytes=VMEM_BYTES),
        cost_estimate=pl.CostEstimate(
            flops=30 * 2 * levels * lats * lon_count * slots // chunks,
            bytes_accessed=6 * levels * lats * lon_count,
            transcendentals=0,
        ),
        name="longitude_analysis",
    )(holder, table, state, forcing, *before)


def synthesis_rows_kernel(owners, chunks, holder_ref, waves_ref, out_ref):
    for parity in range(2):
        for k in range(chunks):
            rows, zero = wave_rows(owners, chunks, k, holder_ref, waves_ref, parity)
            if parity == 0:
                count = zero.shape[0] // owners
                weight = (2.0 - zero).reshape(owners, count, 1)
                weight = jnp.concatenate([weight, weight], axis=1).reshape(-1, 1)
            else:
                weight = 2.0
            out_ref[parity, k] = (rows * weight).astype(jnp.bfloat16)


def synthesis_rows(owners, chunks, holder, table):
    shape = (2, chunks, holder.shape[1] // chunks, table.shape[3])
    return pl.pallas_call(
        functools.partial(synthesis_rows_kernel, owners, chunks),
        out_shape=jax.ShapeDtypeStruct(shape, jnp.bfloat16),
        compiler_params=pltpu.CompilerParams(vmem_limit_bytes=VMEM_BYTES),
        cost_estimate=pl.CostEstimate(
            flops=8 * 200 * holder.shape[1] * table.shape[2] * table.shape[3],
            bytes_accessed=4 * holder.shape[1] * table.shape[3],
            transcendentals=0,
        ),
        name="synthesis_rows",
    )(holder, table)


def pair_slots(first, waves, middle):
    late = (waves[first] >= middle).astype(jnp.int32)
    return first + late, first + 1 - late


def owner_blocks(owners, bands, levels, refs, pieces):
    groups = owners // bands
    blocks = 0
    for ref, (begin, end, apart) in zip(refs, pieces):
        rows = ref.shape[2] + TILE
        for r in range(ref.shape[0]):
            place = (blocks + r) % owners
            owner = lax.bitwise_xor(lax.axis_index(OWNERS), place) if apart else r
            start = (lax.rem(owner, groups) * levels + begin) * rows
            if apart:
                start = pl.multiple_of(start, TILE)
            yield ref.at[r], lax.div(owner, groups), pl.ds(start, (end - begin) * rows)
        blocks += ref.shape[0]


def column_kernel(owners, bands, k, pieces_in, pieces_out, waves_ref, *refs):
    received, refs = refs[: len(pieces_in)], refs[len(pieces_in) :]
    low_basis, high_basis, low_solver, high_solver = refs[:4]
    sends, (spread, back) = refs[-2 - len(pieces_out) : -2], refs[-2:]
    levels = pieces_in[-1][1]
    rows, lats = received[0].shape[-2:]
    per_chunk = rows // 4
    depth = owners // bands * levels
    total = low_basis.shape[1]
    middle = total // 2
    i = pl.program_id(0)

    @pl.when(i == 0)
    def _():
        for ref, band, span in owner_blocks(owners, bands, levels, received, pieces_in):
            part = ref[...].astype(jnp.float32)
            part = jnp.concatenate([part, part[:, :TILE]], axis=1)
            spread[band, span, :] = part.reshape(-1, lats)

    slots = pair_slots(2 * (k * per_chunk + i), waves_ref, middle)
    waves = [waves_ref[slot] for slot in slots]
    bases = [lax.rem(wave, 2) * (2 * per_chunk) + i for wave in waves]
    basis = [low_basis[0], high_basis[0]]
    solvers = [low_solver[0], high_solver[0]]
    lows = [0, middle]
    taken, coeffs, solved, grid = [], [], [], []
    for w in range(2):
        parts = [
            jnp.concatenate(
                [
                    spread[a, pl.ds(bases[w] + c * per_chunk, depth, stride=rows + TILE), :]
                    for a in range(bands)
                ],
                axis=1,
            )
            for c in range(2)
        ]
        taken.append(jnp.concatenate(parts, axis=0).astype(jnp.bfloat16))
    for w in range(2):
        found = dot(taken[w], basis[w])
        coeffs.append(
            jnp.concatenate([found[:depth], found[depth:]], axis=1).astype(jnp.bfloat16)
        )
    for w in range(2):
        found = dot(solvers[w], coeffs[w])
        count = total - lows[w]
        degree = lows[w] + lax.broadcasted_iota(jnp.int32, (depth, count), 1)
        parts = [
            jnp.where(degree >= waves[w], found[:, c * count : (c + 1) * count], 0.0)
            for c in range(2)
        ]
        solved.append(jnp.concatenate(parts, axis=0).astype(jnp.bfloat16))
    for w in range(2):
        grid.append(dot(solved[w], basis[w], NT))
    for w in range(2):
        for c in range(2):
            for a in range(bands):
                back[a, pl.ds(bases[w] + c * per_chunk, depth, stride=rows + TILE), :] = grid[w][
                    c * depth : (c + 1) * depth, a * lats : (a + 1) * lats
                ]

    @pl.when(i == pl.num_programs(0) - 1)
    def _():
        for ref, band, span in owner_blocks(owners, bands, levels, sends, pieces_out):
            part = back[band, span, :].reshape(ref.shape[0], rows + TILE, lats)
            ref[...] = part[:, :rows].astype(jnp.bfloat16)


def run_columns(k, owners, bands, pieces_in, pieces_out, waves, received, before, basis, solver):
    rows, lats = received[0].shape[-2:]
    levels = pieces_in[-1][1]
    depth = owners // bands * levels
    total = basis.shape[1]
    middle = total // 2
    steps = rows // 4
    first = lambda i: 2 * (k * steps + i)
    low = lambda i, waves_ref: (pair_slots(first(i), waves_ref, middle)[0], 0, 0)
    high = lambda i, waves_ref: (pair_slots(first(i), waves_ref, middle)[1], 0, 0)
    upper = lambda i, waves_ref: (pair_slots(first(i), waves_ref, middle)[1], 0, 1)
    whole = lambda shape: pl.BlockSpec(shape, lambda i, waves_ref: (0, 0, 0, 0))
    sizes = [(owners, end - begin, rows, lats) for begin, end, _ in pieces_out]
    scratch = pltpu.VMEM((bands, depth * (rows + TILE), lats), jnp.float32)
    return pl.pallas_call(
        functools.partial(column_kernel, owners, bands, k, pieces_in, pieces_out),
        grid_spec=pltpu.PrefetchScalarGridSpec(
            num_scalar_prefetch=1,
            grid=(steps,),
            in_specs=[whole(part.shape) for part in received]
            + [
                pl.BlockSpec((1, total, total), low),
                pl.BlockSpec((1, total, total - middle), upper),
                pl.BlockSpec((1, depth, depth), low),
                pl.BlockSpec((1, depth, depth), high),
            ]
            + [pl.BlockSpec(memory_space=pl.ANY)] * len(before),
            out_specs=[whole(size) for size in sizes],
            scratch_shapes=[scratch, scratch],
        ),
        out_shape=[jax.ShapeDtypeStruct(size, jnp.bfloat16) for size in sizes],
        compiler_params=pltpu.CompilerParams(vmem_limit_bytes=VMEM_BYTES),
        cost_estimate=pl.CostEstimate(
            flops=HINT * 6 * steps * 2 * depth * total * total,
            bytes_accessed=4 * bands * depth * rows * lats + 3 * steps * total * total,
            transcendentals=0,
        ),
        name="legendre_solve",
    )(waves, *received, basis, basis, solver, solver, *before)


def synthesis_kernel(owners, begin, pieces, *refs):
    parts, synth_ref, (out_hbm, kept, out, arrived, left) = (
        refs[: len(pieces)],
        refs[len(pieces)],
        refs[-5:],
    )
    steps, chunks, _, levels, rows, lats = kept.shape
    half = synth_ref.shape[-1]
    me = lax.axis_index(OWNERS)

    def copies(n, entire):
        for k, (part, (start, apart)) in enumerate(zip(parts, pieces)):
            span = pl.ds(begin - start + n * levels, levels)
            if apart and not entire:
                for r in range(owners):
                    place = kept.at[n, k, lax.bitwise_xor(me, r)]
                    yield pltpu.make_async_copy(part.at[r, span], place, arrived.at[n, k])
            else:
                yield pltpu.make_async_copy(part.at[:, span], kept.at[n, k], arrived.at[n, k])

    def leaving(n):
        mine = pl.ds(n * levels, levels)
        span = pl.ds(begin + n * levels, levels)
        return pltpu.make_async_copy(out.at[mine], out_hbm.at[span], left.at[n])

    @pl.loop(0, steps)
    def _(n):
        for copy in copies(n, False):
            copy.start()

    @pl.loop(0, steps)
    def _(i):
        for copy in copies(i, True):
            copy.wait()
        sums = []
        for parity in range(2):
            terms = []
            for k in range(chunks):
                found = kept[i, k, :, :, parity * (rows // 2) : (parity + 1) * (rows // 2), :]
                found = jnp.concatenate(
                    [found[:, n].reshape(owners * rows // 2, lats) for n in range(levels)], axis=1
                )
                terms.append(dot(found, synth_ref[parity, k], TN))
            sums.append(sum(terms[1:], terms[0]))
        for n in range(levels):
            even, odd = [found[n * lats : (n + 1) * lats] for found in sums]
            out[i * levels + n, :, :half] = (even + odd).astype(jnp.bfloat16)
            out[i * levels + n, :, half:] = (even - odd).astype(jnp.bfloat16)
        leaving(i).start()

    @pl.loop(0, steps)
    def _(n):
        leaving(n).wait()


def run_synthesis(begin, end, levels, pieces, parts, synth, before):
    owners, _, rows, lats = parts[0].shape
    lon_count = 2 * synth.shape[-1]
    chunks = len(pieces)
    count = next(count for count in (4, 2, 1) if (end - begin) % count == 0)
    steps = (end - begin) // count
    given = [] if before is None else [before]
    anywhere = pl.BlockSpec(memory_space=pl.ANY)
    return pl.pallas_call(
        functools.partial(synthesis_kernel, owners, begin, pieces),
        in_specs=[anywhere] * len(parts)
        + [pl.BlockSpec(memory_space=pltpu.VMEM)]
        + [anywhere] * len(given),
        out_specs=anywhere,
        out_shape=jax.ShapeDtypeStruct((levels, lats, lon_count), jnp.bfloat16),
        scratch_shapes=[
            pltpu.VMEM((steps, chunks, owners, count, rows, lats), jnp.bfloat16),
            pltpu.VMEM((end - begin, lats, lon_count), jnp.bfloat16),
            pltpu.SemaphoreType.DMA((steps, chunks)),
            pltpu.SemaphoreType.DMA((steps,)),
        ],
        compiler_params=pltpu.CompilerParams(vmem_limit_bytes=VMEM_BYTES),
        cost_estimate=pl.CostEstimate(
            flops=(end - begin) * lats * lon_count * lon_count,
            bytes_accessed=4 * (end - begin) * lats * lon_count,
            transcendentals=0,
        ),
        input_output_aliases={len(parts) + 1: 0} if given else {},
        name="longitude_synthesis",
    )(*parts, synth, *given)


def exchange(part):
    owners, levels, rows, lats = part.shape
    flat = part.reshape(owners, levels * rows, lats)
    return lax.all_to_all(flat, OWNERS, 0, 0, tiled=True).reshape(part.shape)


def give(part, bit):
    owners = part.shape[0]
    halves = part.reshape((owners // 2 // bit, 2, bit) + part.shape[1:])
    given = lax.ppermute(halves[:, 1], OWNERS, [(o, o ^ bit) for o in range(owners)])
    return halves[:, 0], given


def swap(part, bits):
    for bit in bits:
        part = jnp.stack(give(part, bit), axis=1).reshape(part.shape)
    return part


def chunked_shards(lat_bands, level_groups, chunks):
    owners = lat_bands * level_groups
    far, near = owners // 2, [2**n for n in range(int(math.log2(owners)) - 1)]

    def shards(
        thermal_state_grid,
        thermal_forcing,
        spherical_basis_table,
        implicit_solver_matrix,
        fourier_order_holder,
    ):
        levels = thermal_state_grid.shape[0]
        slots = spherical_basis_table.shape[0]
        table = jnp.asarray(longitude_waves(thermal_state_grid.shape[2]))
        holder = fourier_order_holder.reshape(1, -1)
        owner = lax.axis_index(OWNERS)
        waves = lax.dynamic_slice_in_dim(fourier_order_holder, owner * slots, slots)

        def analyse(k, piece, before):
            return run_analysis(
                owners, chunks, k, piece, thermal_state_grid, thermal_forcing, holder, table, before
            )

        def columns(k, pieces_in, pieces_out, received, before):
            return run_columns(
                k, owners, lat_bands, pieces_in, pieces_out, waves, received, before,
                spherical_basis_table, implicit_solver_matrix,
            )

        def share(count):
            return levels * count // 34 // 2 * 2

        def across(part):
            return [half[0] for half in give(part, far)]

        whole = [(0, levels, False)]
        head_cut, last_cut = levels - share(HEAD), levels - share(LAST)
        late_cut = levels - share(LATE)
        early_cut = late_cut - share(EARLY)
        head = analyse(0, (head_cut, levels, True), [])
        main = analyse(0, (0, head_cut, False), [head])
        head = swap(head, [far])
        first = exchange(main)
        main = analyse(1, (0, early_cut, False), [])
        rest = analyse(1, (early_cut, levels, True), [main])
        early, late = rest[:, : late_cut - early_cut], rest[:, late_cut - early_cut :]
        both = swap(jnp.concatenate([head, early], axis=1), near)
        head, early = both[:, : levels - head_cut], across(both[:, levels - head_cut :])
        second = exchange(main)
        pieces = [(0, head_cut, False), (head_cut, levels, True)]
        (solved,) = columns(0, pieces, whole, [first, head], early[1:])
        solved, late = lax.optimization_barrier((solved, late))
        late = across(swap(late, near))
        first = exchange(solved)
        pieces = [(0, early_cut, False)]
        pieces += [(early_cut, late_cut, True)] * 2 + [(late_cut, levels, True)] * 2
        split = [(0, last_cut, False), (last_cut, levels, True)]
        solved, aside = columns(1, pieces, split, [second, *early, *late], [])
        solved, aside = lax.optimization_barrier((solved, aside))
        aside = jnp.concatenate(across(swap(aside, near)))
        second = exchange(solved)
        synth = synthesis_rows(owners, chunks, holder, table)
        result = run_synthesis(
            last_cut, levels, levels, [(0, False), (last_cut, True)], [first, aside], synth, None
        )
        return run_synthesis(
            0, last_cut, levels, [(0, False), (0, False)], [first, second], synth, result
        )

    return shards


def solution(mesh):
    shape = mesh.shape
    bands, groups = shape["lat"], shape["lev"] * shape["sub"]

    def shards(state, forcing, basis, solver, holder):
        levels, lats, lon_count = state.shape
        pairs = basis.shape[0] // 2
        tiled = pairs % (CHUNKS * TILE) == 0 and levels * groups % TILE == 0
        tiled = tiled and bands > 1 and bands * groups == 2 ** int(math.log2(bands * groups))
        if tiled and levels % 2 == 0 and lats % 128 == 0 and lon_count == 2 * holder.shape[0]:
            body = chunked_shards(bands, groups, CHUNKS)
        else:
            body = general_shards(bands, groups)
        return body(state, forcing, basis, solver, holder)

    return jax.shard_map(
        shards,
        mesh=mesh,
        in_specs=(
            P(("members", "lev", "sub"), "lat", None),
            P(("members", "lev", "sub"), "lat", None),
            P(OWNERS, None, None),
            P(OWNERS, None, None),
            P(),
        ),
        out_specs=P(("members", "lev", "sub"), "lat", None),
        check_vma=False,
    )
```

```python
import functools
import math

import jax
import jax.numpy as jnp
import numpy as np
from jax import lax
from jax.experimental import pallas as pl
from jax.experimental.pallas import tpu as pltpu
from jax.sharding import PartitionSpec as P

OWNERS = ("lat", "lev", "sub")
CHUNKS = 2
HINT, ANALYSIS_HINT = 33, 30
HEAD, EARLY, LATE, LAST = 6, 4, 6, 6


def raw_table(fourier_order_holder, lon_count):
    meridian_position = jnp.arange(lon_count, dtype=jnp.int32)
    phases = fourier_order_holder[:, None] * meridian_position[None, :] % lon_count
    angles = phases.astype(jnp.float32) * (2.0 * math.pi / lon_count)
    factor = 1.0 / math.sqrt(lon_count)
    stacked = jnp.stack([jnp.cos(angles), -jnp.sin(angles)], axis=1)
    return stacked.reshape(2 * fourier_order_holder.shape[0], lon_count) * factor


def general_shards(lat_bands, level_groups):
    def shards(
        thermal_state_grid,
        thermal_forcing,
        spherical_basis_table,
        implicit_solver_matrix,
        fourier_order_holder,
    ):
        levels, lats, lon_count = thermal_state_grid.shape
        slots, lat_total, wave_total = spherical_basis_table.shape
        owners = lat_bands * level_groups
        state = thermal_state_grid.astype(jnp.float32)
        explicit = (
            state
            + 0.5 * thermal_forcing.astype(jnp.float32)
            - 0.3 * state * state * state / (1.0 + state * state)
        ).astype(jnp.bfloat16)
        raw = raw_table(fourier_order_holder, lon_count)
        analysis = raw.astype(jnp.bfloat16)
        weights = jnp.where(fourier_order_holder == 0, 1.0, 2.0).astype(jnp.float32)
        synthesis = (raw * jnp.repeat(weights, 2)[:, None]).astype(jnp.bfloat16)
        spectral = jnp.einsum(
            "sj,lxj->slx", analysis, explicit, preferred_element_type=jnp.float32
        ).astype(jnp.bfloat16)
        spectral = spectral.reshape(owners, 2 * slots * levels, lats)
        spectral = lax.all_to_all(spectral, OWNERS, 0, 0, tiled=True)
        spectral = spectral.reshape(lat_bands, level_groups, slots, 2, levels, lats)
        spectral = spectral.transpose(2, 3, 1, 4, 0, 5)
        spectral = spectral.reshape(slots, 2 * level_groups * levels, lat_total)
        coeffs = jnp.einsum(
            "srx,sxn->srn", spectral, spherical_basis_table, preferred_element_type=jnp.float32
        ).astype(jnp.bfloat16)
        coeffs = coeffs.reshape(slots, 2, level_groups * levels, wave_total)
        solved = jnp.einsum(
            "skl,scln->sckn", implicit_solver_matrix, coeffs, preferred_element_type=jnp.float32
        )
        owner = lax.axis_index(OWNERS)
        waves = lax.dynamic_slice_in_dim(fourier_order_holder, owner * slots, slots)
        live = jnp.arange(wave_total, dtype=jnp.int32)[None, :] >= waves[:, None]
        solved = jnp.where(live[:, None, None, :], solved, 0.0).astype(jnp.bfloat16)
        solved = solved.reshape(slots, 2 * level_groups * levels, wave_total)
        back = jnp.einsum(
            "srn,sxn->srx", solved, spherical_basis_table, preferred_element_type=jnp.float32
        ).astype(jnp.bfloat16)
        back = back.reshape(slots, 2, level_groups, levels, lat_bands, lats)
        back = back.transpose(4, 2, 0, 1, 3, 5).reshape(owners, 2 * slots * levels, lats)
        back = lax.all_to_all(back, OWNERS, 0, 0, tiled=True)
        back = back.reshape(2 * slots * owners, levels, lats)
        return jnp.einsum(
            "slx,sj->lxj", back, synthesis, preferred_element_type=jnp.float32
        ).astype(jnp.bfloat16)

    return shards


TILE = 8
VMEM_BYTES = 60 * 1024 * 1024
NT = (((1,), (1,)), ((), ()))
TN = (((0,), (0,)), ((), ()))


def dot(a, b, dims=(((1,), (0,)), ((), ()))):
    return lax.dot_general(a, b, dims, preferred_element_type=jnp.float32)


def longitude_waves(lon_count):
    half = lon_count // 2
    waves = np.arange(half).reshape(half // 2, 2).T
    phases = waves[:, :, None] * np.arange(half)[None, None, :] % lon_count
    angles = phases.astype(np.float32) * np.float32(2.0 * math.pi / lon_count)
    table = np.stack([np.cos(angles), -np.sin(angles)], axis=1) / math.sqrt(lon_count)
    return table.astype(jnp.bfloat16)


def wave_rows(owners, chunks, k, holder_ref, waves_ref, parity, me=0):
    slots = holder_ref.shape[1]
    per_chunk = slots // 2 // owners // chunks
    wave = 2 * lax.broadcasted_iota(jnp.int32, (waves_ref.shape[2], slots), 0) + parity
    held = (holder_ref[...] == wave).astype(jnp.float32).astype(jnp.bfloat16)
    row = lax.broadcasted_iota(jnp.int32, (owners * per_chunk, slots), 0)
    owner = lax.bitwise_xor(lax.div(row, per_chunk), me)
    pair = (owner * chunks + k) * per_chunk + lax.rem(row, per_chunk)
    slot = lax.broadcasted_iota(jnp.int32, (owners * per_chunk, slots), 1)
    chosen = (lax.div(slot, 2) == pair).astype(jnp.float32).astype(jnp.bfloat16)
    pick = dot(chosen, held, NT)
    picked = pick.astype(jnp.bfloat16)
    parts = [
        dot(picked, waves_ref[parity, c]).reshape(owners, per_chunk, waves_ref.shape[3])
        for c in range(2)
    ]
    rows = jnp.concatenate(parts, axis=1).reshape(2 * per_chunk * owners, waves_ref.shape[3])
    return rows, pick[:, 0:1]


def analysis_kernel(
    owners, chunks, k, begin, apart, holder_ref, waves_hbm, state_hbm, forcing_hbm, *refs
):
    send_hbm, waves, table, state, forcing, folded, send, ready, arrived, left = refs[-10:]
    steps, levels, lats, lon_count = state.shape
    half = lon_count // 2
    rows = send.shape[2]

    def copies(n):
        span = pl.ds(begin + n * levels, levels)
        return (
            pltpu.make_async_copy(state_hbm.at[span], state.at[n], arrived.at[n, 0]),
            pltpu.make_async_copy(forcing_hbm.at[span], forcing.at[n], arrived.at[n, 1]),
        )

    def leaving(n):
        span = pl.ds(n * levels, levels)
        return pltpu.make_async_copy(send.at[:, span], send_hbm.at[:, span], left.at[n])

    fetch = pltpu.make_async_copy(waves_hbm, waves, ready)
    fetch.start()

    @pl.loop(0, steps)
    def _(n):
        for copy in copies(n):
            copy.start()

    fetch.wait()
    for parity in range(2):
        me = lax.axis_index(OWNERS) if apart else 0
        found, _ = wave_rows(owners, chunks, k, holder_ref, waves, parity, me)
        table[parity] = found.astype(jnp.bfloat16)

    def take(n):
        for copy in copies(n):
            copy.wait()

    def fold(n, now):
        for level in range(levels):
            s = state[n, level].astype(jnp.float32)
            f = forcing[n, level].astype(jnp.float32)
            explicit = s * (0.7 + 0.3 / (1.0 + s * s)) + 0.5 * f
            low, high = explicit[:, :half], explicit[:, half:]
            span = slice(level * lats, (level + 1) * lats)
            folded[now, 0, span, :] = (low + high).astype(jnp.bfloat16)
            folded[now, 1, span, :] = (low - high).astype(jnp.bfloat16)

    def transform(n, now):
        for parity in range(2):
            found = dot(table[parity], folded[now, parity], NT).astype(jnp.bfloat16)
            found = found.reshape(owners, rows // 2, levels * lats)
            mine = slice(parity * (rows // 2), (parity + 1) * (rows // 2))
            for level in range(levels):
                send[:, n * levels + level, mine, :] = found[
                    :, :, level * lats : (level + 1) * lats
                ]
        leaving(n).start()

    take(0)
    fold(0, 0)

    @pl.loop(0, (steps - 1) // 2)
    def _(j):
        take(2 * j + 1)
        take(2 * j + 2)
        transform(2 * j, 0)
        fold(2 * j + 1, 1)
        transform(2 * j + 1, 1)
        fold(2 * j + 2, 0)

    if steps % 2 == 0:
        take(steps - 1)
        fold(steps - 1, 1)
        transform(steps - 2, 0)
    transform(steps - 1, (steps - 1) % 2)

    @pl.loop(0, steps)
    def _(n):
        leaving(n).wait()


def run_analysis(owners, chunks, k, piece, state, forcing, holder, table, before):
    begin, end, apart = piece
    _, lats, lon_count = state.shape
    levels = end - begin
    slots = holder.shape[1]
    rows = 2 * slots // owners // chunks
    count = 2 if levels % 2 == 0 else 1
    steps = levels // count
    kept = pltpu.VMEM((steps, count, lats, lon_count), jnp.bfloat16)
    anywhere = pl.BlockSpec(memory_space=pl.ANY)
    return pl.pallas_call(
        functools.partial(analysis_kernel, owners, chunks, k, begin, apart),
        in_specs=[pl.BlockSpec(memory_space=pltpu.VMEM)] + [anywhere] * (3 + len(before)),
        out_specs=anywhere,
        out_shape=jax.ShapeDtypeStruct((owners, levels, rows, lats), jnp.bfloat16),
        scratch_shapes=[
            pltpu.VMEM(table.shape, jnp.bfloat16),
            pltpu.VMEM((2, slots // chunks, lon_count // 2), jnp.bfloat16),
            kept,
            kept,
            pltpu.VMEM((2, 2, count * lats, lon_count // 2), jnp.bfloat16),
            pltpu.VMEM((owners, levels, rows, lats), jnp.bfloat16),
            pltpu.SemaphoreType.DMA,
            pltpu.SemaphoreType.DMA((steps, 2)),
            pltpu.SemaphoreType.DMA((steps,)),
        ],
        compiler_params=pltpu.CompilerParams(vmem_limit_bytes=VMEM_BYTES),
        cost_estimate=pl.CostEstimate(
            flops=ANALYSIS_HINT * 2 * levels * lats * lon_count * slots // chunks,
            bytes_accessed=6 * levels * lats * lon_count,
            transcendentals=0,
        ),
        name="longitude_analysis",
    )(holder, table, state, forcing, *before)


def synthesis_rows_kernel(owners, chunks, holder_ref, waves_ref, out_ref):
    for parity in range(2):
        for k in range(chunks):
            rows, zero = wave_rows(owners, chunks, k, holder_ref, waves_ref, parity)
            if parity == 0:
                count = zero.shape[0] // owners
                weight = (2.0 - zero).reshape(owners, count, 1)
                weight = jnp.concatenate([weight, weight], axis=1).reshape(-1, 1)
            else:
                weight = 2.0
            out_ref[parity, k] = (rows * weight).astype(jnp.bfloat16)


def synthesis_rows(owners, chunks, holder, table):
    shape = (2, chunks, holder.shape[1] // chunks, table.shape[3])
    return pl.pallas_call(
        functools.partial(synthesis_rows_kernel, owners, chunks),
        out_shape=jax.ShapeDtypeStruct(shape, jnp.bfloat16),
        compiler_params=pltpu.CompilerParams(vmem_limit_bytes=VMEM_BYTES),
        cost_estimate=pl.CostEstimate(
            flops=8 * 200 * holder.shape[1] * table.shape[2] * table.shape[3],
            bytes_accessed=4 * holder.shape[1] * table.shape[3],
            transcendentals=0,
        ),
        name="synthesis_rows",
    )(holder, table)


def pair_slots(first, waves, middle):
    late = (waves[first] >= middle).astype(jnp.int32)
    return first + late, first + 1 - late


def owner_blocks(owners, bands, levels, refs, pieces):
    groups = owners // bands
    blocks = 0
    for ref, (begin, end, apart) in zip(refs, pieces):
        rows = ref.shape[2] + TILE
        for r in range(ref.shape[0]):
            place = (blocks + r) % owners
            owner = lax.bitwise_xor(lax.axis_index(OWNERS), place) if apart else r
            start = (lax.rem(owner, groups) * levels + begin) * rows
            if apart:
                start = pl.multiple_of(start, TILE)
            yield ref.at[r], lax.div(owner, groups), pl.ds(start, (end - begin) * rows)
        blocks += ref.shape[0]


def column_kernel(owners, bands, k, pieces_in, pieces_out, waves_ref, *refs):
    received, refs = refs[: len(pieces_in)], refs[len(pieces_in) :]
    low_basis, high_basis, low_solver, high_solver = refs[:4]
    sends, (spread, back) = refs[-2 - len(pieces_out) : -2], refs[-2:]
    levels = pieces_in[-1][1]
    rows, lats = received[0].shape[-2:]
    per_chunk = rows // 4
    depth = owners // bands * levels
    total = low_basis.shape[1]
    middle = total // 2
    i = pl.program_id(0)

    @pl.when(i == 0)
    def _():
        for ref, band, span in owner_blocks(owners, bands, levels, received, pieces_in):
            part = ref[...].astype(jnp.float32)
            part = jnp.concatenate([part, part[:, :TILE]], axis=1)
            spread[band, span, :] = part.reshape(-1, lats)

    slots = pair_slots(2 * (k * per_chunk + i), waves_ref, middle)
    waves = [waves_ref[slot] for slot in slots]
    bases = [lax.rem(wave, 2) * (2 * per_chunk) + i for wave in waves]
    basis = [low_basis[0], high_basis[0]]
    solvers = [low_solver[0], high_solver[0]]
    lows = [0, middle]
    taken, coeffs, solved, grid = [], [], [], []
    for w in range(2):
        parts = [
            jnp.concatenate(
                [
                    spread[a, pl.ds(bases[w] + c * per_chunk, depth, stride=rows + TILE), :]
                    for a in range(bands)
                ],
                axis=1,
            )
            for c in range(2)
        ]
        taken.append(jnp.concatenate(parts, axis=0).astype(jnp.bfloat16))
    for w in range(2):
        found = dot(taken[w], basis[w])
        coeffs.append(
            jnp.concatenate([found[:depth], found[depth:]], axis=1).astype(jnp.bfloat16)
        )
    for w in range(2):
        found = dot(solvers[w], coeffs[w])
        count = total - lows[w]
        degree = lows[w] + lax.broadcasted_iota(jnp.int32, (depth, count), 1)
        parts = [
            jnp.where(degree >= waves[w], found[:, c * count : (c + 1) * count], 0.0)
            for c in range(2)
        ]
        solved.append(jnp.concatenate(parts, axis=0).astype(jnp.bfloat16))
    for w in range(2):
        grid.append(dot(solved[w], basis[w], NT))
    for w in range(2):
        for c in range(2):
            for a in range(bands):
                back[a, pl.ds(bases[w] + c * per_chunk, depth, stride=rows + TILE), :] = grid[w][
                    c * depth : (c + 1) * depth, a * lats : (a + 1) * lats
                ]

    @pl.when(i == pl.num_programs(0) - 1)
    def _():
        for ref, band, span in owner_blocks(owners, bands, levels, sends, pieces_out):
            part = back[band, span, :].reshape(ref.shape[0], rows + TILE, lats)
            ref[...] = part[:, :rows].astype(jnp.bfloat16)


def run_columns(k, owners, bands, pieces_in, pieces_out, waves, received, before, basis, solver):
    rows, lats = received[0].shape[-2:]
    levels = pieces_in[-1][1]
    depth = owners // bands * levels
    total = basis.shape[1]
    middle = total // 2
    steps = rows // 4
    first = lambda i: 2 * (k * steps + i)
    low = lambda i, waves_ref: (pair_slots(first(i), waves_ref, middle)[0], 0, 0)
    high = lambda i, waves_ref: (pair_slots(first(i), waves_ref, middle)[1], 0, 0)
    upper = lambda i, waves_ref: (pair_slots(first(i), waves_ref, middle)[1], 0, 1)
    whole = lambda shape: pl.BlockSpec(shape, lambda i, waves_ref: (0, 0, 0, 0))
    sizes = [(owners, end - begin, rows, lats) for begin, end, _ in pieces_out]
    scratch = pltpu.VMEM((bands, (depth + 1) * (rows + TILE), lats), jnp.float32)
    return pl.pallas_call(
        functools.partial(column_kernel, owners, bands, k, pieces_in, pieces_out),
        grid_spec=pltpu.PrefetchScalarGridSpec(
            num_scalar_prefetch=1,
            grid=(steps,),
            in_specs=[whole(part.shape) for part in received]
            + [
                pl.BlockSpec((1, total, total), low),
                pl.BlockSpec((1, total, total - middle), upper),
                pl.BlockSpec((1, depth, depth), low),
                pl.BlockSpec((1, depth, depth), high),
            ]
            + [pl.BlockSpec(memory_space=pl.ANY)] * len(before),
            out_specs=[whole(size) for size in sizes],
            scratch_shapes=[scratch, scratch],
        ),
        out_shape=[jax.ShapeDtypeStruct(size, jnp.bfloat16) for size in sizes],
        compiler_params=pltpu.CompilerParams(vmem_limit_bytes=VMEM_BYTES),
        cost_estimate=pl.CostEstimate(
            flops=HINT * 6 * steps * 2 * depth * total * total,
            bytes_accessed=4 * bands * depth * rows * lats + 3 * steps * total * total,
            transcendentals=0,
        ),
        name="legendre_solve",
    )(waves, *received, basis, basis, solver, solver, *before)


def synthesis_kernel(owners, begin, pieces, *refs):
    parts, synth_ref, (out_hbm, kept, out, arrived, left) = (
        refs[: len(pieces)],
        refs[len(pieces)],
        refs[-5:],
    )
    steps, chunks, _, levels, rows, lats = kept.shape
    half = synth_ref.shape[-1]
    me = lax.axis_index(OWNERS)

    def copies(n, entire):
        for k, (part, (start, apart)) in enumerate(zip(parts, pieces)):
            span = pl.ds(begin - start + n * levels, levels)
            if apart and not entire:
                for r in range(owners):
                    place = kept.at[n, k, lax.bitwise_xor(me, r)]
                    yield pltpu.make_async_copy(part.at[r, span], place, arrived.at[n, k])
            else:
                yield pltpu.make_async_copy(part.at[:, span], kept.at[n, k], arrived.at[n, k])

    def leaving(n):
        mine = pl.ds(n * levels, levels)
        span = pl.ds(begin + n * levels, levels)
        return pltpu.make_async_copy(out.at[mine], out_hbm.at[span], left.at[n])

    @pl.loop(0, steps)
    def _(n):
        for copy in copies(n, False):
            copy.start()

    @pl.loop(0, steps)
    def _(i):
        for copy in copies(i, True):
            copy.wait()
        sums = []
        for parity in range(2):
            terms = []
            for k in range(chunks):
                found = kept[i, k, :, :, parity * (rows // 2) : (parity + 1) * (rows // 2), :]
                found = jnp.concatenate(
                    [found[:, n].reshape(owners * rows // 2, lats) for n in range(levels)], axis=1
                )
                terms.append(dot(found, synth_ref[parity, k], TN))
            sums.append(sum(terms[1:], terms[0]))
        for n in range(levels):
            even, odd = [found[n * lats : (n + 1) * lats] for found in sums]
            out[i * levels + n, :, :half] = (even + odd).astype(jnp.bfloat16)
            out[i * levels + n, :, half:] = (even - odd).astype(jnp.bfloat16)
        leaving(i).start()

    @pl.loop(0, steps)
    def _(n):
        leaving(n).wait()


def run_synthesis(begin, end, levels, pieces, parts, synth, before):
    owners, _, rows, lats = parts[0].shape
    lon_count = 2 * synth.shape[-1]
    chunks = len(pieces)
    count = next(count for count in (4, 2, 1) if (end - begin) % count == 0)
    steps = (end - begin) // count
    given = [] if before is None else [before]
    anywhere = pl.BlockSpec(memory_space=pl.ANY)
    return pl.pallas_call(
        functools.partial(synthesis_kernel, owners, begin, pieces),
        in_specs=[anywhere] * len(parts)
        + [pl.BlockSpec(memory_space=pltpu.VMEM)]
        + [anywhere] * len(given),
        out_specs=anywhere,
        out_shape=jax.ShapeDtypeStruct((levels, lats, lon_count), jnp.bfloat16),
        scratch_shapes=[
            pltpu.VMEM((steps, chunks, owners, count, rows, lats), jnp.bfloat16),
            pltpu.VMEM((end - begin, lats, lon_count), jnp.bfloat16),
            pltpu.SemaphoreType.DMA((steps, chunks)),
            pltpu.SemaphoreType.DMA((steps,)),
        ],
        compiler_params=pltpu.CompilerParams(vmem_limit_bytes=VMEM_BYTES),
        cost_estimate=pl.CostEstimate(
            flops=(end - begin) * lats * lon_count * lon_count,
            bytes_accessed=4 * (end - begin) * lats * lon_count,
            transcendentals=0,
        ),
        input_output_aliases={len(parts) + 1: 0} if given else {},
        name="longitude_synthesis",
    )(*parts, synth, *given)


def exchange(part):
    owners, levels, rows, lats = part.shape
    flat = part.reshape(owners, levels * rows, lats)
    return lax.all_to_all(flat, OWNERS, 0, 0, tiled=True).reshape(part.shape)


def give(part, bit):
    owners = part.shape[0]
    halves = part.reshape((owners // 2 // bit, 2, bit) + part.shape[1:])
    given = lax.ppermute(halves[:, 1], OWNERS, [(o, o ^ bit) for o in range(owners)])
    return halves[:, 0], given


def swap(part, bits):
    for bit in bits:
        part = jnp.stack(give(part, bit), axis=1).reshape(part.shape)
    return part


def chunked_shards(lat_bands, level_groups, chunks):
    owners = lat_bands * level_groups
    far, near = owners // 2, [2**n for n in range(int(math.log2(owners)) - 1)]

    def shards(
        thermal_state_grid,
        thermal_forcing,
        spherical_basis_table,
        implicit_solver_matrix,
        fourier_order_holder,
    ):
        levels = thermal_state_grid.shape[0]
        slots = spherical_basis_table.shape[0]
        table = jnp.asarray(longitude_waves(thermal_state_grid.shape[2]))
        holder = fourier_order_holder.reshape(1, -1)
        owner = lax.axis_index(OWNERS)
        waves = lax.dynamic_slice_in_dim(fourier_order_holder, owner * slots, slots)

        def analyse(k, piece, before):
            return run_analysis(
                owners, chunks, k, piece, thermal_state_grid, thermal_forcing, holder, table, before
            )

        def columns(k, pieces_in, pieces_out, received, before):
            return run_columns(
                k, owners, lat_bands, pieces_in, pieces_out, waves, received, before,
                spherical_basis_table, implicit_solver_matrix,
            )

        def share(count):
            return levels * count // 34 // 2 * 2

        def across(part):
            return [half[0] for half in give(part, far)]

        whole = [(0, levels, False)]
        head_cut, last_cut = levels - share(HEAD), levels - share(LAST)
        late_cut = levels - share(LATE)
        early_cut = late_cut - share(EARLY)
        head = analyse(0, (head_cut, levels, True), [])
        main = analyse(0, (0, head_cut, False), [head])
        head = swap(head, [far])
        first = exchange(main)
        main = analyse(1, (0, early_cut, False), [])
        rest = analyse(1, (early_cut, levels, True), [main])
        early, late = rest[:, : late_cut - early_cut], rest[:, late_cut - early_cut :]
        both = swap(jnp.concatenate([head, early], axis=1), near)
        head, early = both[:, : levels - head_cut], across(both[:, levels - head_cut :])
        second = exchange(main)
        pieces = [(0, head_cut, False), (head_cut, levels, True)]
        (solved,) = columns(0, pieces, whole, [first, head], early[1:])
        solved, late = lax.optimization_barrier((solved, late))
        late = across(swap(late, near))
        first = exchange(solved)
        pieces = [(0, early_cut, False)]
        pieces += [(early_cut, late_cut, True)] * 2 + [(late_cut, levels, True)] * 2
        split = [(0, last_cut, False), (last_cut, levels, True)]
        solved, aside = columns(1, pieces, split, [second, *early, *late], [])
        solved, aside = lax.optimization_barrier((solved, aside))
        aside = jnp.concatenate(across(swap(aside, near)))
        second = exchange(solved)
        synth = synthesis_rows(owners, chunks, holder, table)
        result = run_synthesis(
            last_cut, levels, levels, [(0, False), (last_cut, True)], [first, aside], synth, None
        )
        return run_synthesis(
            0, last_cut, levels, [(0, False), (0, False)], [first, second], synth, result
        )

    return shards


def solution(mesh):
    shape = mesh.shape
    bands, groups = shape["lat"], shape["lev"] * shape["sub"]

    def shards(state, forcing, basis, solver, holder):
        levels, lats, lon_count = state.shape
        pairs = basis.shape[0] // 2
        tiled = pairs % (CHUNKS * TILE) == 0 and levels * groups % TILE == 0
        tiled = tiled and bands > 1 and bands * groups == 2 ** int(math.log2(bands * groups))
        if tiled and levels % 2 == 0 and lats % 128 == 0 and lon_count == 2 * holder.shape[0]:
            body = chunked_shards(bands, groups, CHUNKS)
        else:
            body = general_shards(bands, groups)
        return body(state, forcing, basis, solver, holder)

    return jax.shard_map(
        shards,
        mesh=mesh,
        in_specs=(
            P(("members", "lev", "sub"), "lat", None),
            P(("members", "lev", "sub"), "lat", None),
            P(OWNERS, None, None),
            P(OWNERS, None, None),
            P(),
        ),
        out_specs=P(("members", "lev", "sub"), "lat", None),
        check_vma=False,
    )
```

```python
import functools
import math

import jax
import jax.numpy as jnp
import numpy as np
from jax import lax
from jax.experimental import pallas as pl
from jax.experimental.pallas import tpu as pltpu
from jax.sharding import PartitionSpec as P

OWNERS = ("lat", "lev", "sub")
CHUNKS = 2
HINT, ANALYSIS_HINT = 33, 30
HEAD, EARLY, LATE, LAST = 6, 2, 6, 6


def raw_table(fourier_order_holder, lon_count):
    meridian_position = jnp.arange(lon_count, dtype=jnp.int32)
    phases = fourier_order_holder[:, None] * meridian_position[None, :] % lon_count
    angles = phases.astype(jnp.float32) * (2.0 * math.pi / lon_count)
    factor = 1.0 / math.sqrt(lon_count)
    stacked = jnp.stack([jnp.cos(angles), -jnp.sin(angles)], axis=1)
    return stacked.reshape(2 * fourier_order_holder.shape[0], lon_count) * factor


def general_shards(lat_bands, level_groups):
    def shards(
        thermal_state_grid,
        thermal_forcing,
        spherical_basis_table,
        implicit_solver_matrix,
        fourier_order_holder,
    ):
        levels, lats, lon_count = thermal_state_grid.shape
        slots, lat_total, wave_total = spherical_basis_table.shape
        owners = lat_bands * level_groups
        state = thermal_state_grid.astype(jnp.float32)
        explicit = (
            state
            + 0.5 * thermal_forcing.astype(jnp.float32)
            - 0.3 * state * state * state / (1.0 + state * state)
        ).astype(jnp.bfloat16)
        raw = raw_table(fourier_order_holder, lon_count)
        analysis = raw.astype(jnp.bfloat16)
        weights = jnp.where(fourier_order_holder == 0, 1.0, 2.0).astype(jnp.float32)
        synthesis = (raw * jnp.repeat(weights, 2)[:, None]).astype(jnp.bfloat16)
        spectral = jnp.einsum(
            "sj,lxj->slx", analysis, explicit, preferred_element_type=jnp.float32
        ).astype(jnp.bfloat16)
        spectral = spectral.reshape(owners, 2 * slots * levels, lats)
        spectral = lax.all_to_all(spectral, OWNERS, 0, 0, tiled=True)
        spectral = spectral.reshape(lat_bands, level_groups, slots, 2, levels, lats)
        spectral = spectral.transpose(2, 3, 1, 4, 0, 5)
        spectral = spectral.reshape(slots, 2 * level_groups * levels, lat_total)
        coeffs = jnp.einsum(
            "srx,sxn->srn", spectral, spherical_basis_table, preferred_element_type=jnp.float32
        ).astype(jnp.bfloat16)
        coeffs = coeffs.reshape(slots, 2, level_groups * levels, wave_total)
        solved = jnp.einsum(
            "skl,scln->sckn", implicit_solver_matrix, coeffs, preferred_element_type=jnp.float32
        )
        owner = lax.axis_index(OWNERS)
        waves = lax.dynamic_slice_in_dim(fourier_order_holder, owner * slots, slots)
        live = jnp.arange(wave_total, dtype=jnp.int32)[None, :] >= waves[:, None]
        solved = jnp.where(live[:, None, None, :], solved, 0.0).astype(jnp.bfloat16)
        solved = solved.reshape(slots, 2 * level_groups * levels, wave_total)
        back = jnp.einsum(
            "srn,sxn->srx", solved, spherical_basis_table, preferred_element_type=jnp.float32
        ).astype(jnp.bfloat16)
        back = back.reshape(slots, 2, level_groups, levels, lat_bands, lats)
        back = back.transpose(4, 2, 0, 1, 3, 5).reshape(owners, 2 * slots * levels, lats)
        back = lax.all_to_all(back, OWNERS, 0, 0, tiled=True)
        back = back.reshape(2 * slots * owners, levels, lats)
        return jnp.einsum(
            "slx,sj->lxj", back, synthesis, preferred_element_type=jnp.float32
        ).astype(jnp.bfloat16)

    return shards


TILE = 8
VMEM_BYTES = 60 * 1024 * 1024
NT = (((1,), (1,)), ((), ()))
TN = (((0,), (0,)), ((), ()))


def dot(a, b, dims=(((1,), (0,)), ((), ()))):
    return lax.dot_general(a, b, dims, preferred_element_type=jnp.float32)


def longitude_waves(lon_count):
    half = lon_count // 2
    waves = np.arange(half).reshape(half // 2, 2).T
    phases = waves[:, :, None] * np.arange(half)[None, None, :] % lon_count
    angles = phases.astype(np.float32) * np.float32(2.0 * math.pi / lon_count)
    table = np.stack([np.cos(angles), -np.sin(angles)], axis=1) / math.sqrt(lon_count)
    return table.astype(jnp.bfloat16)


def wave_rows(owners, chunks, k, holder_ref, waves_ref, parity, me=0):
    slots = holder_ref.shape[1]
    per_chunk = slots // 2 // owners // chunks
    wave = 2 * lax.broadcasted_iota(jnp.int32, (waves_ref.shape[2], slots), 0) + parity
    held = (holder_ref[...] == wave).astype(jnp.float32).astype(jnp.bfloat16)
    row = lax.broadcasted_iota(jnp.int32, (owners * per_chunk, slots), 0)
    owner = lax.bitwise_xor(lax.div(row, per_chunk), me)
    pair = (owner * chunks + k) * per_chunk + lax.rem(row, per_chunk)
    slot = lax.broadcasted_iota(jnp.int32, (owners * per_chunk, slots), 1)
    chosen = (lax.div(slot, 2) == pair).astype(jnp.float32).astype(jnp.bfloat16)
    pick = dot(chosen, held, NT)
    picked = pick.astype(jnp.bfloat16)
    parts = [
        dot(picked, waves_ref[parity, c]).reshape(owners, per_chunk, waves_ref.shape[3])
        for c in range(2)
    ]
    rows = jnp.concatenate(parts, axis=1).reshape(2 * per_chunk * owners, waves_ref.shape[3])
    return rows, pick[:, 0:1]


def analysis_kernel(
    owners, chunks, k, begin, apart, holder_ref, waves_hbm, state_hbm, forcing_hbm, *refs
):
    send_hbm, waves, table, state, forcing, folded, send, ready, arrived, left = refs[-10:]
    steps, levels, lats, lon_count = state.shape
    half = lon_count // 2
    rows = send.shape[2]

    def copies(n):
        span = pl.ds(begin + n * levels, levels)
        return (
            pltpu.make_async_copy(state_hbm.at[span], state.at[n], arrived.at[n, 0]),
            pltpu.make_async_copy(forcing_hbm.at[span], forcing.at[n], arrived.at[n, 1]),
        )

    def leaving(n):
        span = pl.ds(n * levels, levels)
        return pltpu.make_async_copy(send.at[:, span], send_hbm.at[:, span], left.at[n])

    fetch = pltpu.make_async_copy(waves_hbm, waves, ready)
    fetch.start()

    @pl.loop(0, steps)
    def _(n):
        for copy in copies(n):
            copy.start()

    fetch.wait()
    for parity in range(2):
        me = lax.axis_index(OWNERS) if apart else 0
        found, _ = wave_rows(owners, chunks, k, holder_ref, waves, parity, me)
        table[parity] = found.astype(jnp.bfloat16)

    def take(n):
        for copy in copies(n):
            copy.wait()

    def fold(n, now):
        for level in range(levels):
            s = state[n, level].astype(jnp.float32)
            f = forcing[n, level].astype(jnp.float32)
            explicit = s * (0.7 + 0.3 / (1.0 + s * s)) + 0.5 * f
            low, high = explicit[:, :half], explicit[:, half:]
            span = slice(level * lats, (level + 1) * lats)
            folded[now, 0, span, :] = (low + high).astype(jnp.bfloat16)
            folded[now, 1, span, :] = (low - high).astype(jnp.bfloat16)

    def transform(n, now):
        for parity in range(2):
            found = dot(table[parity], folded[now, parity], NT).astype(jnp.bfloat16)
            found = found.reshape(owners, rows // 2, levels * lats)
            mine = slice(parity * (rows // 2), (parity + 1) * (rows // 2))
            for level in range(levels):
                send[:, n * levels + level, mine, :] = found[
                    :, :, level * lats : (level + 1) * lats
                ]
        leaving(n).start()

    take(0)
    fold(0, 0)

    @pl.loop(0, (steps - 1) // 2)
    def _(j):
        take(2 * j + 1)
        take(2 * j + 2)
        transform(2 * j, 0)
        fold(2 * j + 1, 1)
        transform(2 * j + 1, 1)
        fold(2 * j + 2, 0)

    if steps % 2 == 0:
        take(steps - 1)
        fold(steps - 1, 1)
        transform(steps - 2, 0)
    transform(steps - 1, (steps - 1) % 2)

    @pl.loop(0, steps)
    def _(n):
        leaving(n).wait()


def run_analysis(owners, chunks, k, piece, state, forcing, holder, table, before):
    begin, end, apart = piece
    _, lats, lon_count = state.shape
    levels = end - begin
    slots = holder.shape[1]
    rows = 2 * slots // owners // chunks
    count = 2 if levels % 2 == 0 else 1
    steps = levels // count
    kept = pltpu.VMEM((steps, count, lats, lon_count), jnp.bfloat16)
    anywhere = pl.BlockSpec(memory_space=pl.ANY)
    return pl.pallas_call(
        functools.partial(analysis_kernel, owners, chunks, k, begin, apart),
        in_specs=[pl.BlockSpec(memory_space=pltpu.VMEM)] + [anywhere] * (3 + len(before)),
        out_specs=anywhere,
        out_shape=jax.ShapeDtypeStruct((owners, levels, rows, lats), jnp.bfloat16),
        scratch_shapes=[
            pltpu.VMEM(table.shape, jnp.bfloat16),
            pltpu.VMEM((2, slots // chunks, lon_count // 2), jnp.bfloat16),
            kept,
            kept,
            pltpu.VMEM((2, 2, count * lats, lon_count // 2), jnp.bfloat16),
            pltpu.VMEM((owners, levels, rows, lats), jnp.bfloat16),
            pltpu.SemaphoreType.DMA,
            pltpu.SemaphoreType.DMA((steps, 2)),
            pltpu.SemaphoreType.DMA((steps,)),
        ],
        compiler_params=pltpu.CompilerParams(vmem_limit_bytes=VMEM_BYTES),
        cost_estimate=pl.CostEstimate(
            flops=ANALYSIS_HINT * 2 * levels * lats * lon_count * slots // chunks,
            bytes_accessed=6 * levels * lats * lon_count,
            transcendentals=0,
        ),
        name="longitude_analysis",
    )(holder, table, state, forcing, *before)


def synthesis_rows_kernel(owners, chunks, holder_ref, waves_ref, out_ref):
    for parity in range(2):
        for k in range(chunks):
            rows, zero = wave_rows(owners, chunks, k, holder_ref, waves_ref, parity)
            if parity == 0:
                count = zero.shape[0] // owners
                weight = (2.0 - zero).reshape(owners, count, 1)
                weight = jnp.concatenate([weight, weight], axis=1).reshape(-1, 1)
            else:
                weight = 2.0
            out_ref[parity, k] = (rows * weight).astype(jnp.bfloat16)


def synthesis_rows(owners, chunks, holder, table):
    shape = (2, chunks, holder.shape[1] // chunks, table.shape[3])
    return pl.pallas_call(
        functools.partial(synthesis_rows_kernel, owners, chunks),
        out_shape=jax.ShapeDtypeStruct(shape, jnp.bfloat16),
        compiler_params=pltpu.CompilerParams(vmem_limit_bytes=VMEM_BYTES),
        cost_estimate=pl.CostEstimate(
            flops=8 * 200 * holder.shape[1] * table.shape[2] * table.shape[3],
            bytes_accessed=4 * holder.shape[1] * table.shape[3],
            transcendentals=0,
        ),
        name="synthesis_rows",
    )(holder, table)


def pair_slots(first, waves, middle):
    late = (waves[first] >= middle).astype(jnp.int32)
    return first + late, first + 1 - late


def owner_blocks(owners, bands, levels, refs, pieces):
    groups = owners // bands
    blocks = 0
    for ref, (begin, end, apart) in zip(refs, pieces):
        rows = ref.shape[2] + TILE
        for r in range(ref.shape[0]):
            place = (blocks + r) % owners
            owner = lax.bitwise_xor(lax.axis_index(OWNERS), place) if apart else r
            start = (lax.rem(owner, groups) * levels + begin) * rows
            if apart:
                start = pl.multiple_of(start, TILE)
            yield ref.at[r], lax.div(owner, groups), pl.ds(start, (end - begin) * rows)
        blocks += ref.shape[0]


def column_kernel(owners, bands, k, pieces_in, pieces_out, waves_ref, *refs):
    received, refs = refs[: len(pieces_in)], refs[len(pieces_in) :]
    low_basis, high_basis, low_solver, high_solver = refs[:4]
    sends, (spread, back) = refs[-2 - len(pieces_out) : -2], refs[-2:]
    levels = pieces_in[-1][1]
    rows, lats = received[0].shape[-2:]
    per_chunk = rows // 4
    depth = owners // bands * levels
    total = low_basis.shape[1]
    middle = total // 2
    i = pl.program_id(0)

    @pl.when(i == 0)
    def _():
        for ref, band, span in owner_blocks(owners, bands, levels, received, pieces_in):
            part = ref[...].astype(jnp.float32)
            part = jnp.concatenate([part, part[:, :TILE]], axis=1)
            spread[band, span, :] = part.reshape(-1, lats)

    slots = pair_slots(2 * (k * per_chunk + i), waves_ref, middle)
    waves = [waves_ref[slot] for slot in slots]
    bases = [lax.rem(wave, 2) * (2 * per_chunk) + i for wave in waves]
    basis = [low_basis[0], high_basis[0]]
    solvers = [low_solver[0], high_solver[0]]
    lows = [0, middle]
    taken, coeffs, solved, grid = [], [], [], []
    for w in range(2):
        parts = [
            jnp.concatenate(
                [
                    spread[a, pl.ds(bases[w] + c * per_chunk, depth, stride=rows + TILE), :]
                    for a in range(bands)
                ],
                axis=1,
            )
            for c in range(2)
        ]
        taken.append(jnp.concatenate(parts, axis=0).astype(jnp.bfloat16))
    for w in range(2):
        found = dot(taken[w], basis[w])
        coeffs.append(
            jnp.concatenate([found[:depth], found[depth:]], axis=1).astype(jnp.bfloat16)
        )
    for w in range(2):
        found = dot(solvers[w], coeffs[w])
        count = total - lows[w]
        degree = lows[w] + lax.broadcasted_iota(jnp.int32, (depth, count), 1)
        parts = [
            jnp.where(degree >= waves[w], found[:, c * count : (c + 1) * count], 0.0)
            for c in range(2)
        ]
        solved.append(jnp.concatenate(parts, axis=0).astype(jnp.bfloat16))
    for w in range(2):
        grid.append(dot(solved[w], basis[w], NT))
    for w in range(2):
        for c in range(2):
            for a in range(bands):
                back[a, pl.ds(bases[w] + c * per_chunk, depth, stride=rows + TILE), :] = grid[w][
                    c * depth : (c + 1) * depth, a * lats : (a + 1) * lats
                ]

    @pl.when(i == pl.num_programs(0) - 1)
    def _():
        for ref, band, span in owner_blocks(owners, bands, levels, sends, pieces_out):
            part = back[band, span, :].reshape(ref.shape[0], rows + TILE, lats)
            ref[...] = part[:, :rows].astype(jnp.bfloat16)


def run_columns(k, owners, bands, pieces_in, pieces_out, waves, received, before, basis, solver):
    rows, lats = received[0].shape[-2:]
    levels = pieces_in[-1][1]
    depth = owners // bands * levels
    total = basis.shape[1]
    middle = total // 2
    steps = rows // 4
    first = lambda i: 2 * (k * steps + i)
    low = lambda i, waves_ref: (pair_slots(first(i), waves_ref, middle)[0], 0, 0)
    high = lambda i, waves_ref: (pair_slots(first(i), waves_ref, middle)[1], 0, 0)
    upper = lambda i, waves_ref: (pair_slots(first(i), waves_ref, middle)[1], 0, 1)
    whole = lambda shape: pl.BlockSpec(shape, lambda i, waves_ref: (0, 0, 0, 0))
    sizes = [(owners, end - begin, rows, lats) for begin, end, _ in pieces_out]
    scratch = pltpu.VMEM((bands, (depth + 1) * (rows + TILE), lats), jnp.float32)
    return pl.pallas_call(
        functools.partial(column_kernel, owners, bands, k, pieces_in, pieces_out),
        grid_spec=pltpu.PrefetchScalarGridSpec(
            num_scalar_prefetch=1,
            grid=(steps,),
            in_specs=[whole(part.shape) for part in received]
            + [
                pl.BlockSpec((1, total, total), low),
                pl.BlockSpec((1, total, total - middle), upper),
                pl.BlockSpec((1, depth, depth), low),
                pl.BlockSpec((1, depth, depth), high),
            ]
            + [pl.BlockSpec(memory_space=pl.ANY)] * len(before),
            out_specs=[whole(size) for size in sizes],
            scratch_shapes=[scratch, scratch],
        ),
        out_shape=[jax.ShapeDtypeStruct(size, jnp.bfloat16) for size in sizes],
        compiler_params=pltpu.CompilerParams(vmem_limit_bytes=VMEM_BYTES),
        cost_estimate=pl.CostEstimate(
            flops=HINT * 6 * steps * 2 * depth * total * total,
            bytes_accessed=4 * bands * depth * rows * lats + 3 * steps * total * total,
            transcendentals=0,
        ),
        name="legendre_solve",
    )(waves, *received, basis, basis, solver, solver, *before)


def synthesis_kernel(owners, begin, pieces, *refs):
    parts, synth_ref, (out_hbm, kept, out, arrived, left) = (
        refs[: len(pieces)],
        refs[len(pieces)],
        refs[-5:],
    )
    steps, chunks, _, levels, rows, lats = kept.shape
    half = synth_ref.shape[-1]
    me = lax.axis_index(OWNERS)

    def copies(n, entire):
        for k, (part, (start, apart)) in enumerate(zip(parts, pieces)):
            span = pl.ds(begin - start + n * levels, levels)
            if apart and not entire:
                for r in range(owners):
                    place = kept.at[n, k, lax.bitwise_xor(me, r)]
                    yield pltpu.make_async_copy(part.at[r, span], place, arrived.at[n, k])
            else:
                yield pltpu.make_async_copy(part.at[:, span], kept.at[n, k], arrived.at[n, k])

    def leaving(n):
        mine = pl.ds(n * levels, levels)
        span = pl.ds(begin + n * levels, levels)
        return pltpu.make_async_copy(out.at[mine], out_hbm.at[span], left.at[n])

    @pl.loop(0, steps)
    def _(n):
        for copy in copies(n, False):
            copy.start()

    @pl.loop(0, steps)
    def _(i):
        for copy in copies(i, True):
            copy.wait()
        sums = []
        for parity in range(2):
            terms = []
            for k in range(chunks):
                found = kept[i, k, :, :, parity * (rows // 2) : (parity + 1) * (rows // 2), :]
                found = jnp.concatenate(
                    [found[:, n].reshape(owners * rows // 2, lats) for n in range(levels)], axis=1
                )
                terms.append(dot(found, synth_ref[parity, k], TN))
            sums.append(sum(terms[1:], terms[0]))
        for n in range(levels):
            even, odd = [found[n * lats : (n + 1) * lats] for found in sums]
            out[i * levels + n, :, :half] = (even + odd).astype(jnp.bfloat16)
            out[i * levels + n, :, half:] = (even - odd).astype(jnp.bfloat16)
        leaving(i).start()

    @pl.loop(0, steps)
    def _(n):
        leaving(n).wait()


def run_synthesis(begin, end, levels, pieces, parts, synth, before):
    owners, _, rows, lats = parts[0].shape
    lon_count = 2 * synth.shape[-1]
    chunks = len(pieces)
    count = next(count for count in (4, 2, 1) if (end - begin) % count == 0)
    steps = (end - begin) // count
    given = [] if before is None else [before]
    anywhere = pl.BlockSpec(memory_space=pl.ANY)
    return pl.pallas_call(
        functools.partial(synthesis_kernel, owners, begin, pieces),
        in_specs=[anywhere] * len(parts)
        + [pl.BlockSpec(memory_space=pltpu.VMEM)]
        + [anywhere] * len(given),
        out_specs=anywhere,
        out_shape=jax.ShapeDtypeStruct((levels, lats, lon_count), jnp.bfloat16),
        scratch_shapes=[
            pltpu.VMEM((steps, chunks, owners, count, rows, lats), jnp.bfloat16),
            pltpu.VMEM((end - begin, lats, lon_count), jnp.bfloat16),
            pltpu.SemaphoreType.DMA((steps, chunks)),
            pltpu.SemaphoreType.DMA((steps,)),
        ],
        compiler_params=pltpu.CompilerParams(vmem_limit_bytes=VMEM_BYTES),
        cost_estimate=pl.CostEstimate(
            flops=(end - begin) * lats * lon_count * lon_count,
            bytes_accessed=4 * (end - begin) * lats * lon_count,
            transcendentals=0,
        ),
        input_output_aliases={len(parts) + 1: 0} if given else {},
        name="longitude_synthesis",
    )(*parts, synth, *given)


def exchange(part):
    owners, levels, rows, lats = part.shape
    flat = part.reshape(owners, levels * rows, lats)
    return lax.all_to_all(flat, OWNERS, 0, 0, tiled=True).reshape(part.shape)


def give(part, bit):
    owners = part.shape[0]
    halves = part.reshape((owners // 2 // bit, 2, bit) + part.shape[1:])
    given = lax.ppermute(halves[:, 1], OWNERS, [(o, o ^ bit) for o in range(owners)])
    return halves[:, 0], given


def swap(part, bits):
    for bit in bits:
        part = jnp.stack(give(part, bit), axis=1).reshape(part.shape)
    return part


def chunked_shards(lat_bands, level_groups, chunks):
    owners = lat_bands * level_groups
    far, near = owners // 2, [2**n for n in range(int(math.log2(owners)) - 1)]

    def shards(
        thermal_state_grid,
        thermal_forcing,
        spherical_basis_table,
        implicit_solver_matrix,
        fourier_order_holder,
    ):
        levels = thermal_state_grid.shape[0]
        slots = spherical_basis_table.shape[0]
        table = jnp.asarray(longitude_waves(thermal_state_grid.shape[2]))
        holder = fourier_order_holder.reshape(1, -1)
        owner = lax.axis_index(OWNERS)
        waves = lax.dynamic_slice_in_dim(fourier_order_holder, owner * slots, slots)

        def analyse(k, piece, before):
            return run_analysis(
                owners, chunks, k, piece, thermal_state_grid, thermal_forcing, holder, table, before
            )

        def columns(k, pieces_in, pieces_out, received, before):
            return run_columns(
                k, owners, lat_bands, pieces_in, pieces_out, waves, received, before,
                spherical_basis_table, implicit_solver_matrix,
            )

        def share(count):
            return levels * count // 34 // 2 * 2

        def across(part):
            return [half[0] for half in give(part, far)]

        whole = [(0, levels, False)]
        head_cut, last_cut = levels - share(HEAD), levels - share(LAST)
        late_cut = levels - share(LATE)
        early_cut = late_cut - share(EARLY)
        head = analyse(0, (head_cut, levels, True), [])
        main = analyse(0, (0, head_cut, False), [head])
        head = swap(head, [far])
        first = exchange(main)
        main = analyse(1, (0, early_cut, False), [])
        rest = analyse(1, (early_cut, levels, True), [main])
        early, late = rest[:, : late_cut - early_cut], rest[:, late_cut - early_cut :]
        both = swap(jnp.concatenate([head, early], axis=1), near)
        head, early = both[:, : levels - head_cut], across(both[:, levels - head_cut :])
        second = exchange(main)
        pieces = [(0, head_cut, False), (head_cut, levels, True)]
        (solved,) = columns(0, pieces, whole, [first, head], early[1:])
        solved, late = lax.optimization_barrier((solved, late))
        late = across(swap(late, near))
        first = exchange(solved)
        pieces = [(0, early_cut, False)]
        pieces += [(early_cut, late_cut, True)] * 2 + [(late_cut, levels, True)] * 2
        split = [(0, last_cut, False), (last_cut, levels, True)]
        solved, aside = columns(1, pieces, split, [second, *early, *late], [])
        solved, aside = lax.optimization_barrier((solved, aside))
        aside = jnp.concatenate(across(swap(aside, near)))
        second = exchange(solved)
        synth = synthesis_rows(owners, chunks, holder, table)
        result = run_synthesis(
            last_cut, levels, levels, [(0, False), (last_cut, True)], [first, aside], synth, None
        )
        return run_synthesis(
            0, last_cut, levels, [(0, False), (0, False)], [first, second], synth, result
        )

    return shards


def solution(mesh):
    shape = mesh.shape
    bands, groups = shape["lat"], shape["lev"] * shape["sub"]

    def shards(state, forcing, basis, solver, holder):
        levels, lats, lon_count = state.shape
        pairs = basis.shape[0] // 2
        tiled = pairs % (CHUNKS * TILE) == 0 and levels * groups % TILE == 0
        tiled = tiled and bands > 1 and bands * groups == 2 ** int(math.log2(bands * groups))
        if tiled and levels % 2 == 0 and lats % 128 == 0 and lon_count == 2 * holder.shape[0]:
            body = chunked_shards(bands, groups, CHUNKS)
        else:
            body = general_shards(bands, groups)
        return body(state, forcing, basis, solver, holder)

    return jax.shard_map(
        shards,
        mesh=mesh,
        in_specs=(
            P(("members", "lev", "sub"), "lat", None),
            P(("members", "lev", "sub"), "lat", None),
            P(OWNERS, None, None),
            P(OWNERS, None, None),
            P(),
        ),
        out_specs=P(("members", "lev", "sub"), "lat", None),
        check_vma=False,
    )
```
